256 devices in a mesh: diag: 16 (over x_hi, z), slab: 16 (over x_lo, y, core).
Axes of the slice: x: 4 (x_hi: 2, x_lo: 2; x = x_hi * 2 + x_lo), y: 4, z: 8, core: 2. Of those that a mesh axis runs over, the one named last changes fastest.
Arguments:
- left: float32 [16, 768, 768], P('diag', 'slab'), may hold values from -0.355756237 to 0.355756237
- right: float32 [16, 768, 768], P('diag', 'slab'), may hold values from -0.355756237 to 0.355756237
- window_a: float32 [16, 768, 768], P('diag', 'slab'), may hold values from -6 to 6
- window_b: float32 [16, 768, 768], P('diag', 'slab'), may hold values from -6 to 6
- row_slab_a: float32 [16, 2048, 768], P('diag', 'slab'), may hold values from -6 to 6
- row_slab_b: float32 [16, 2048, 768], P('diag', 'slab'), may hold values from -6 to 6
- column_slab_a: float32 [16, 2048, 768], P('diag', 'slab'), may hold values from -6 to 6
- column_slab_b: float32 [16, 2048, 768], P('diag', 'slab'), may hold values from -6 to 6
- row_live: int32 [16], P('diag'), may hold values from 1024 to 2048, as said below
- column_live: int32 [16], P('diag'), may hold values from 1024 to 2048, as said below
Outputs:
- updated_window_a: float32 [16, 768, 768], P('diag', 'slab')
- updated_window_b: float32 [16, 768, 768], P('diag', 'slab')
- updated_row_slab_a: float32 [16, 2048, 768], P('diag', 'slab')
- updated_row_slab_b: float32 [16, 2048, 768], P('diag', 'slab')
- updated_column_slab_a: float32 [16, 2048, 768], P('diag', 'slab')
- updated_column_slab_b: float32 [16, 2048, 768], P('diag', 'slab')
The draws below stay inside these ranges and needn't reach their ends.
Inputs may be any that keep to these rules, and one draw needn't show every extreme that they name: `row_live`: in every draw one window has all 2048 positions live and another exactly half of them. `column_live`: in every draw one window has all 2048 positions live and another exactly half of them.
All inputs are finite; a program needn't handle non-finite values.
Results may differ from the reference program's by a relative error of at most 0.0002.
Values sent between devices are 32-bit elements; how exact they have to be, the bound alone decides.
No kernel may reach another device: no remote copies, remote signals or barrier semaphores. Data moves between devices by JAX's collectives and lax.ppermute only.
A program may use at most 64 MiB of HBM per device.

```python
import math
import jax
import jax.numpy as jnp
from jax import lax

W = 768
OVL = 256
OWNERS = 16
SLAB_LEN = 2048


def factor_draw(key):
    full_shape = (OWNERS, W, W)
    entries = jnp.clip(jax.random.normal(key, full_shape, jnp.float32), -6.0, 6.0)
    row_index = lax.broadcasted_iota(jnp.int32, full_shape, 1)
    column_index = lax.broadcasted_iota(jnp.int32, full_shape, 2)
    inside = (row_index < OVL) & (column_index >= W - OVL)
    corner_gain = jnp.where(inside, math.sqrt(0.9 * W / OVL), 1.0)
    return entries * corner_gain / math.sqrt(W)


def draw_left(key, part):
    return factor_draw(jax.random.fold_in(key, 11))


def draw_right(key, part):
    return factor_draw(jax.random.fold_in(key, 23))


def live_draw(key):
    counts = jax.random.randint(key, (OWNERS,), SLAB_LEN // 2, SLAB_LEN + 1, jnp.int32)
    shuffled = jax.random.permutation(jax.random.fold_in(key, 7), OWNERS)
    counts = counts.at[shuffled[0]].set(SLAB_LEN)
    return counts.at[shuffled[1]].set(SLAB_LEN // 2)


def draw_row_live(key, part):
    return live_draw(jax.random.fold_in(key, 31))


def draw_column_live(key, part):
    return live_draw(jax.random.fold_in(key, 37))


def steps_of(rng, extent, pieces, least, top_value):
    gain = 1.0
    for position, blocks in pieces:
        heights = jax.random.uniform(jax.random.fold_in(jax.random.fold_in(rng, 6), position), (blocks,), jnp.float32, least / len(pieces), top_value / len(pieces))
        gain = gain * jnp.repeat(jnp.exp(heights), extent[position] // blocks).reshape((-1,) + (1,) * (len(extent) - 1 - position))
    return gain


def normal_values(own_key, shape, scale, most, pieces=(), dtype=jnp.bfloat16):
    values = jax.random.normal(own_key, shape, jnp.float32) * scale
    if len(pieces) > 0:
        values = steps_of(own_key, shape, pieces, -0.22, 0.18) * values
    return jnp.clip(values, min=-most, max=most).astype(dtype)


def setup_inputs(seed: int = 0) -> dict:
    arg_keys = jax.random.split(jax.random.key(seed), 11)
    left = draw_left(jax.random.fold_in(arg_keys[10], 71), 0)
    right = draw_right(jax.random.fold_in(arg_keys[10], 71), 0)
    window_a = normal_values(arg_keys[2], (OWNERS, W, W), 1.0, 6.0, ((0, 16), (1, 16)), jnp.float32)
    window_b = normal_values(arg_keys[3], (OWNERS, W, W), 1.0, 6.0, ((0, 16), (1, 16)), jnp.float32)
    row_slab_a = normal_values(arg_keys[4], (OWNERS, SLAB_LEN, W), 1.0, 6.0, ((0, 16), (1, 16)), jnp.float32)
    row_slab_b = normal_values(arg_keys[5], (OWNERS, SLAB_LEN, W), 1.0, 6.0, ((0, 16), (1, 16)), jnp.float32)
    column_slab_a = normal_values(arg_keys[6], (OWNERS, SLAB_LEN, W), 1.0, 6.0, ((0, 16), (1, 16)), jnp.float32)
    column_slab_b = normal_values(arg_keys[7], (OWNERS, SLAB_LEN, W), 1.0, 6.0, ((0, 16), (1, 16)), jnp.float32)
    row_live = draw_row_live(jax.random.fold_in(arg_keys[10], 71), 0)
    column_live = draw_column_live(jax.random.fold_in(arg_keys[10], 71), 0)
    return {"left": left, "right": right, "window_a": window_a, "window_b": window_b, "row_slab_a": row_slab_a, "row_slab_b": row_slab_b, "column_slab_a": column_slab_a, "column_slab_b": column_slab_b, "row_live": row_live, "column_live": column_live}


HIGHEST = lax.Precision.HIGHEST


def product(first_matrix, second_matrix):
    return jnp.dot(first_matrix, second_matrix, precision=HIGHEST, preferred_element_type=jnp.float32)


def over_product(first_matrix, second_matrix):
    return lax.dot_general(first_matrix, second_matrix, (((0,), (0,)), ((), ())), precision=HIGHEST, preferred_element_type=jnp.float32)


def reference(left, right, window_a, window_b, row_slab_a, row_slab_b, column_slab_a, column_slab_b, row_live, column_live):
    positions = lax.broadcasted_iota(jnp.int32, (SLAB_LEN, 1), 0)
    carry_a = jnp.zeros((OVL, OVL), jnp.float32)
    carry_b = jnp.zeros((OVL, OVL), jnp.float32)
    windows_a = []
    windows_b = []
    rows_out_a = []
    rows_out_b = []
    columns_out_a = []
    columns_out_b = []
    for owner_index in range(OWNERS):
        left_owner = left[owner_index]
        right_owner = right[owner_index]
        top_left = left_owner[:OVL]
        top_right = right_owner[:OVL]
        updated_a = product(over_product(left_owner, window_a[owner_index]), right_owner) + product(over_product(top_left, carry_a), top_right)
        updated_b = product(over_product(left_owner, window_b[owner_index]), right_owner) + product(over_product(top_left, carry_b), top_right)
        carry_a = updated_a[W - OVL:, W - OVL:]
        carry_b = updated_b[W - OVL:, W - OVL:]
        windows_a.append(updated_a)
        windows_b.append(updated_b)
        row_keep = positions < row_live[owner_index]
        column_keep = positions < column_live[owner_index]
        rows_out_a.append(jnp.where(row_keep, product(row_slab_a[owner_index], left_owner), row_slab_a[owner_index]))
        rows_out_b.append(jnp.where(row_keep, product(row_slab_b[owner_index], left_owner), row_slab_b[owner_index]))
        columns_out_a.append(jnp.where(column_keep, product(column_slab_a[owner_index], right_owner), column_slab_a[owner_index]))
        columns_out_b.append(jnp.where(column_keep, product(column_slab_b[owner_index], right_owner), column_slab_b[owner_index]))
    return (jnp.stack(windows_a), jnp.stack(windows_b), jnp.stack(rows_out_a), jnp.stack(rows_out_b), jnp.stack(columns_out_a), jnp.stack(columns_out_b))
```

```python
import jax
import jax.numpy as jnp
from jax import lax
from jax.sharding import PartitionSpec as P

OVL = 256
W = 768
ROWS = 96
CHIPS = 8
SLICE = OVL // CHIPS

HIGH = lax.Precision.HIGH
NN = (((1,), (0,)), ((), ()))
TN = (((0,), (0,)), ((), ()))


def mul(a, b, dims=NN):
    return lax.dot_general(a, b, dims, precision=HIGH, preferred_element_type=jnp.float32)


def slab_route(move):
    return [
        ((x * 4 + y) * 2 + c, (move(x, y)[0] * 4 + move(x, y)[1]) * 2 + c)
        for x in range(2)
        for y in range(4)
        for c in range(2)
    ]


CROSS = slab_route(lambda x, y: (1 - x, y))
UP = slab_route(lambda x, y: (x, (y + 1) % 4))
DOWN = slab_route(lambda x, y: (x, (y + 3) % 4))
OTHER_CORE = [(i, i ^ 1) for i in range(16)]
SAME_CORE = [[i for i in range(16) if i % 2 == c] for c in range(2)]


def z_route(d):
    return [(h * 8 + z, h * 8 + (z + d) % 8) for h in range(2) for z in range(8)]


def swap_cores(block):
    return lax.ppermute(block, "slab", OTHER_CORE)


def gather_chips(own):
    cross = lax.ppermute(own, "slab", CROSS)
    below = lax.ppermute(own, "slab", UP)
    above = lax.ppermute(own, "slab", DOWN)
    cross_above = lax.ppermute(above, "slab", CROSS)
    cross_below = lax.ppermute(cross, "slab", UP)
    far = lax.ppermute(above, "slab", DOWN)
    third = own.shape[0] // 3
    cross_far = jnp.concatenate(
        [
            lax.ppermute(far[:third], "slab", CROSS),
            lax.ppermute(cross_below[third : 2 * third], "slab", UP),
            lax.ppermute(cross_above[2 * third :], "slab", DOWN),
        ]
    )
    return [own, above, far, below, cross, cross_above, cross_far, cross_below]


def ring(own):
    blocks = [own] + [None] * 7
    forward = backward = own
    for t in range(1, 5):
        forward = lax.ppermute(forward, "diag", z_route(-1))
        blocks[t] = forward
        if t < 4:
            backward = lax.ppermute(backward, "diag", z_route(1))
            blocks[8 - t] = backward
    return blocks


def shards(left, right, window_a, window_b, row_a, row_b, column_a, column_b, row_live, column_live):
    slab_index = lax.axis_index("slab")
    owner = lax.axis_index("diag")
    first_core = slab_index % 2 == 0
    chip = slab_index // 2
    x, y = chip // 4, chip % 4
    half, z = owner // 8, owner % 8

    mine = jnp.where(first_core, jnp.stack([left[0], window_a[0]]), jnp.stack([right[0], window_b[0]]))
    others = jnp.where(first_core, jnp.stack([right[0], window_b[0]]), jnp.stack([left[0], window_a[0]]))
    got = swap_cores(others)
    block = jnp.concatenate(
        [jnp.where(first_core, mine, got), jnp.where(first_core, got, mine)], axis=1
    )

    piece = block[0][:, W - OVL :]
    pieces = [piece]
    for d in range(1, CHIPS):
        route = [
            (c * 2 + core, ((c + d) % CHIPS) * 2 + core) for c in range(3) for core in range(2)
        ]
        pieces.append(lax.ppermute(piece, "slab", route))
    pieces = jnp.stack(pieces)
    corner = jnp.concatenate(
        [
            lax.dynamic_index_in_dim(pieces, (chip - r) % CHIPS, 0, keepdims=False)
            for r in range(3)
        ]
    )[:OVL]
    around = ring(corner)

    eye = jnp.eye(OVL, dtype=jnp.float32)
    chain = [around[1]]
    before = [eye, around[7]]
    for t in range(2, 8):
        chain.append(mul(chain[-1], around[t]))
        before.append(mul(around[8 - t], before[-1]))
    prefix = lax.dynamic_index_in_dim(jnp.stack(before), z, 0)
    chain = jnp.concatenate([jnp.stack(chain), prefix])
    chain_other = swap_cores(chain)
    chain_left = jnp.where(first_core, chain, chain_other)
    chain_right = jnp.where(first_core, chain_other, chain)

    blocks = gather_chips(block.reshape(2 * ROWS, W))
    full = jnp.zeros((2, CHIPS, ROWS, W), jnp.float32)
    for dx in range(2):
        for dy in range(4):
            place = (x ^ dx) * 4 + (y + dy) % 4
            full = lax.dynamic_update_slice(
                full, blocks[dx * 4 + dy].reshape(2, 1, ROWS, W), (0, place, 0, 0)
            )
    factor = full[0].reshape(W, W)
    window = full[1].reshape(W, W)
    factor_other = swap_cores(factor)
    left_full = jnp.where(first_core, factor, factor_other)
    right_full = jnp.where(first_core, factor_other, factor)

    base_corner = mul(mul(left_full[:, W - OVL :], window, TN), right_full[:, W - OVL :])
    left_columns = lax.dynamic_slice_in_dim(chain_left[:7], chip * SLICE, SLICE, 2)
    reach = mul(
        left_columns.transpose(1, 0, 2).reshape(OVL, 7 * SLICE), base_corner, TN
    ).reshape(7, SLICE, OVL)
    reach = lax.dot_general(
        reach,
        chain_right[:7],
        (((2,), (1,)), ((0,), (0,))),
        precision=HIGH,
        preferred_element_type=jnp.float32,
    )
    nearest = lax.dynamic_slice_in_dim(base_corner, chip * SLICE, SLICE, 0)
    padded = jnp.concatenate([jnp.zeros((8, SLICE, OVL), jnp.float32), nearest[None], reach])
    near = lax.dynamic_slice_in_dim(padded, 7 - z, 8, 0)
    leaving = jnp.broadcast_to(
        lax.dynamic_slice_in_dim(padded, 15 - z, 1, 0), (8, SLICE, OVL)
    )
    outgoing = jnp.concatenate(
        [jnp.where(half == 0, near, 0.0), jnp.where(half == 0, leaving, near)]
    )
    incoming = lax.all_to_all(outgoing, "diag", split_axis=0, concat_axis=0, tiled=True)
    from_low = jnp.sum(incoming[:8], 0)
    from_high = jnp.sum(incoming[8:], 0)
    share = jnp.stack(
        [jnp.where(half == 0, from_low, from_high), jnp.where(half == 0, 0.0, from_low)]
    )
    shares = lax.all_to_all(
        jnp.broadcast_to(share[None], (CHIPS, 2, SLICE, OVL)),
        "slab",
        split_axis=0,
        concat_axis=0,
        tiled=True,
        axis_index_groups=SAME_CORE,
    )
    carry = shares[:, 0].reshape(OVL, OVL)
    entering = shares[:, 1].reshape(OVL, OVL)
    scale = jnp.asarray([2.0 ** (-7 * i) for i in range(8)], jnp.float32)[z]
    unscale = jnp.asarray([2.0 ** (7 * i) for i in range(8)], jnp.float32)[z]
    through = mul(mul(chain_left[7] * scale, entering, TN), chain_right[7] * scale)
    carry = carry + through * unscale * unscale

    own_columns = lax.dynamic_slice_in_dim(left_full, chip * ROWS, ROWS, 1)
    base = mul(mul(own_columns, window, TN), right_full)
    updated = base + mul(mul(own_columns[:OVL], carry, TN), right_full[:OVL])
    kept = jnp.where(first_core, updated[: ROWS // 2], updated[ROWS // 2 :])
    sent = jnp.where(first_core, updated[ROWS // 2 :], updated[: ROWS // 2])
    received = swap_cores(sent)
    updated_a = jnp.where(first_core, kept, received)
    updated_b = jnp.where(first_core, received, kept)

    length = row_a.shape[1]
    positions = slab_index * length + lax.broadcasted_iota(jnp.int32, (length, 1), 0)
    row_keep = positions < row_live[0]
    column_keep = positions < column_live[0]

    def slab(block, factor, keep):
        return jnp.where(keep, mul(block[0], factor), block[0])[None]

    return (
        updated_a[None],
        updated_b[None],
        slab(row_a, left_full, row_keep),
        slab(row_b, left_full, row_keep),
        slab(column_a, right_full, column_keep),
        slab(column_b, right_full, column_keep),
    )


def solution(mesh):
    rows = P("diag", "slab", None)
    return jax.shard_map(
        shards,
        mesh=mesh,
        in_specs=(rows,) * 8 + (P("diag"),) * 2,
        out_specs=(rows,) * 6,
        check_vma=False,
    )
```

```python
import jax
import jax.numpy as jnp
from jax import lax
from jax.sharding import PartitionSpec as P

OVL = 256
W = 768
EDGE = W - OVL
ROWS = 96
CHIPS = 8
SLICE = OVL // CHIPS
GROUP = 4

HIGH = lax.Precision.HIGH
NN = (((1,), (0,)), ((), ()))
TN = (((0,), (0,)), ((), ()))
NT = (((1,), (1,)), ((), ()))


def mul(a, b, dims=NN):
    return lax.dot_general(a, b, dims, precision=HIGH, preferred_element_type=jnp.float32)


def slab_route(move):
    return [
        ((x * 4 + y) * 2 + c, (move(x, y)[0] * 4 + move(x, y)[1]) * 2 + c)
        for x in range(2)
        for y in range(4)
        for c in range(2)
    ]


CROSS = slab_route(lambda x, y: (1 - x, y))
UP = slab_route(lambda x, y: (x, (y + 1) % 4))
DOWN = slab_route(lambda x, y: (x, (y + 3) % 4))
OTHER_CORE = [(i, i ^ 1) for i in range(16)]
SAME_CORE = [[i for i in range(16) if i % 2 == c] for c in range(2)]


def swap_cores(block):
    return lax.ppermute(block, "slab", OTHER_CORE)


def from_member(block, d):
    route = [(g * 4 + (m + d) % 4, g * 4 + m) for g in range(4) for m in range(4)]
    return lax.ppermute(block, "diag", route)


def from_group(block, d):
    return lax.ppermute(block, "diag", [(i, i + 4 * d) for i in range(16 - 4 * d)])


def to_cores(for_first, for_second):
    pieces = jnp.stack([for_first, for_second])
    pieces = jnp.broadcast_to(pieces[None], (CHIPS,) + pieces.shape)
    pieces = pieces.reshape((2 * CHIPS,) + for_first.shape)
    return lax.all_to_all(pieces, "slab", split_axis=0, concat_axis=0, tiled=True)


def shards(left, right, window_a, window_b, row_a, row_b, column_a, column_b, row_live, column_live):
    slab_index = lax.axis_index("slab")
    owner = lax.axis_index("diag")
    first_core = slab_index % 2 == 0
    chip = slab_index // 2
    x, y = chip // 4, chip % 4
    group, member = owner // GROUP, owner % GROUP

    mine = jnp.where(first_core, jnp.stack([left[0], window_a[0]]), jnp.stack([right[0], window_b[0]]))
    others = jnp.where(first_core, jnp.stack([right[0], window_b[0]]), jnp.stack([left[0], window_a[0]]))
    got = swap_cores(others)
    own = jnp.concatenate(
        [jnp.where(first_core, mine, got), jnp.where(first_core, got, mine)], axis=1
    ).reshape(2 * ROWS, W)
    corner = to_cores(left[0, :, EDGE:], right[0, :, EDGE:])

    cross = lax.ppermute(own, "slab", CROSS)
    below = lax.ppermute(own, "slab", UP)
    above = lax.ppermute(own, "slab", DOWN)
    corner, cross, below, above = lax.optimization_barrier((corner, cross, below, above))
    corner = corner[:6].reshape(6 * left.shape[1], OVL)[:OVL].T
    around = [corner] + [from_member(corner, d) for d in range(1, GROUP)]
    cross_above = lax.ppermute(above, "slab", CROSS)
    cross_below = lax.ppermute(cross, "slab", UP)
    far = lax.ppermute(above, "slab", DOWN)
    third = own.shape[0] // 3
    cross_far = jnp.concatenate(
        [
            lax.ppermute(far[:third], "slab", CROSS),
            lax.ppermute(cross_below[third : 2 * third], "slab", UP),
            lax.ppermute(cross_above[2 * third :], "slab", DOWN),
        ]
    )
    full = jnp.zeros((2, CHIPS, ROWS, W), jnp.float32)
    blocks = [own, above, far, below, cross, cross_above, cross_far, cross_below]
    for i, block in enumerate(blocks):
        place = (x ^ (i // 4)) * 4 + (y + i % 4) % 4
        full = lax.dynamic_update_slice(full, block.reshape(2, 1, ROWS, W), (0, place, 0, 0))
    factor = full[0].reshape(W, W)
    window = full[1].reshape(W, W)

    eye = jnp.eye(OVL, dtype=jnp.float32)
    chain, before = [eye, around[1]], [eye, around[3]]
    for t in range(2, GROUP):
        chain.append(mul(around[t], chain[-1]))
        before.append(mul(before[-1], around[GROUP - t]))
    chain = jnp.stack(chain)
    slices = swap_cores(lax.dynamic_slice_in_dim(chain, chip * SLICE, SLICE, 1))
    prefix = lax.dynamic_index_in_dim(jnp.stack(before), member, 0, keepdims=False)
    rest = lax.dynamic_index_in_dim(chain, GROUP - 1 - member, 0, keepdims=False)
    whole = mul(rest, mul(corner, prefix))
    second = mul(prefix, from_group(whole, 1))
    third_back = mul(second, from_group(whole, 2))
    spans = jnp.stack([third_back, second, prefix])
    spans_other = swap_cores(spans)

    edge = factor[:, EDGE:]
    edge_other = swap_cores(edge)
    edge_left = jnp.where(first_core, edge, edge_other)
    edge_right = jnp.where(first_core, edge_other, edge)
    base_corner = mul(mul(edge_left, window, TN), edge_right)
    base_corner = jnp.where(first_core, base_corner.T, base_corner)
    reach = mul(slices.reshape(GROUP * SLICE, OVL), base_corner).reshape(GROUP, SLICE, OVL)
    reach = lax.dot_general(
        reach,
        chain,
        (((2,), (2,)), ((0,), (0,))),
        precision=HIGH,
        preferred_element_type=jnp.float32,
    )
    padded = jnp.concatenate([jnp.zeros((GROUP, SLICE, OVL), jnp.float32), reach])
    near = lax.dynamic_slice_in_dim(padded, GROUP - 1 - member, GROUP, 0)
    leaving = lax.dynamic_slice_in_dim(padded, 2 * GROUP - 1 - member, 1, 0)
    outgoing = jnp.concatenate(
        [
            jnp.where(group == g, near, jnp.where(group < g, leaving, 0.0))
            for g in range(4)
        ]
    )
    incoming = lax.all_to_all(outgoing, "diag", split_axis=0, concat_axis=0, tiled=True)
    sums = jnp.sum(incoming.reshape(4, GROUP, SLICE, OVL), 1)
    sums = jnp.concatenate([jnp.zeros((3, SLICE, OVL), jnp.float32), sums])
    share = lax.dynamic_slice_in_dim(sums, group, 4, 0)
    shares = lax.all_to_all(
        jnp.broadcast_to(share[None], (CHIPS, 4, SLICE, OVL)),
        "slab",
        split_axis=0,
        concat_axis=0,
        tiled=True,
        axis_index_groups=SAME_CORE,
    )
    ends = shares.transpose(1, 0, 2, 3).reshape(4, OVL, OVL)
    step = lax.dot_general(
        ends[:3],
        spans * 2.0**-16,
        (((2,), (2,)), ((0,), (0,))),
        precision=HIGH,
        preferred_element_type=jnp.float32,
    )
    through = mul(spans_other.transpose(1, 0, 2).reshape(OVL, 3 * OVL), step.reshape(3 * OVL, OVL))
    carry = ends[3] + through * 2.0**16
    carry = jnp.where(first_core, carry.T, carry)

    factor_other = swap_cores(factor)
    left_full = jnp.where(first_core, factor, factor_other)
    right_full = jnp.where(first_core, factor_other, factor)
    own_columns = lax.dynamic_slice_in_dim(left_full, chip * ROWS, ROWS, 1)
    base = mul(mul(own_columns, window, TN), right_full)
    updated = base + mul(mul(own_columns[:OVL], carry, TN), right_full[:OVL])
    kept = jnp.where(first_core, updated[: ROWS // 2], updated[ROWS // 2 :])
    sent = jnp.where(first_core, updated[ROWS // 2 :], updated[: ROWS // 2])
    received = swap_cores(sent)
    updated_a = jnp.where(first_core, kept, received)
    updated_b = jnp.where(first_core, received, kept)

    length = row_a.shape[1]
    positions = slab_index * length + lax.broadcasted_iota(jnp.int32, (length, 1), 0)
    row_keep = positions < row_live[0]
    column_keep = positions < column_live[0]

    def slab(block, factor, keep):
        return jnp.where(keep, mul(block[0], factor), block[0])[None]

    return (
        updated_a[None],
        updated_b[None],
        slab(row_a, left_full, row_keep),
        slab(row_b, left_full, row_keep),
        slab(column_a, right_full, column_keep),
        slab(column_b, right_full, column_keep),
    )


def solution(mesh):
    rows = P("diag", "slab", None)
    return jax.shard_map(
        shards,
        mesh=mesh,
        in_specs=(rows,) * 8 + (P("diag"),) * 2,
        out_specs=(rows,) * 6,
        check_vma=False,
    )
```

```python
import jax
import jax.numpy as jnp
from jax import lax
from jax.experimental import pallas as pl
from jax.experimental.pallas import tpu as pltpu
from jax.sharding import PartitionSpec as P

OVL = 256
W = 768
EDGE = W - OVL
ROWS = 96
CHIPS = 8
SLICE = OVL // CHIPS
GROUP = 4

HIGH = lax.Precision.HIGH
NN = (((1,), (0,)), ((), ()))
TN = (((0,), (0,)), ((), ()))
NT = (((1,), (1,)), ((), ()))


def mul(a, b, dims=NN):
    return lax.dot_general(a, b, dims, precision=HIGH, preferred_element_type=jnp.float32)


def slab_route(move):
    return [
        ((x * 4 + y) * 2 + c, (move(x, y)[0] * 4 + move(x, y)[1]) * 2 + c)
        for x in range(2)
        for y in range(4)
        for c in range(2)
    ]


CROSS = slab_route(lambda x, y: (1 - x, y))
UP = slab_route(lambda x, y: (x, (y + 1) % 4))
DOWN = slab_route(lambda x, y: (x, (y + 3) % 4))
OTHER_CORE = [(i, i ^ 1) for i in range(16)]
SAME_CORE = [[i for i in range(16) if i % 2 == c] for c in range(2)]


def swap_cores(block):
    return lax.ppermute(block, "slab", OTHER_CORE)


def from_member(block, d):
    route = [(g * 4 + (m + d) % 4, g * 4 + m) for g in range(4) for m in range(4)]
    return lax.ppermute(block, "diag", route)


def from_group(block, d):
    return lax.ppermute(block, "diag", [(i, i + 4 * d) for i in range(4, 16 - 4 * d)])


def first_round(own):
    return [lax.ppermute(own, "slab", route) for route in (CROSS, UP, DOWN)]


def later_rounds(own, first):
    cross, below, above = first
    far = lax.ppermute(above, "slab", DOWN)
    cross_above = lax.ppermute(above, "slab", CROSS)
    cross_below = lax.ppermute(cross, "slab", UP)
    cross_far = lax.ppermute(far, "slab", CROSS)
    return [own, above, far, below, cross, cross_above, cross_far, cross_below]


def split(a):
    high = a.astype(jnp.bfloat16)
    return high, (a - high.astype(jnp.float32)).astype(jnp.bfloat16)


def three(a, b, dims=NN):
    def dot(p, q):
        return lax.dot_general(p, q, dims, preferred_element_type=jnp.float32)

    return dot(a[0], b[0]) + (dot(a[0], b[1]) + dot(a[1], b[0]))


def slab_kernel(at_ref, own_ref, other_ref, ra_ref, rb_ref, ca_ref, cb_ref, *outs):
    length = ra_ref.shape[0]

    def update(factor_ref, sources, targets, live):
        stacked = split(jnp.concatenate([source[...] for source in sources]))
        keep = lax.broadcasted_iota(jnp.int32, (length, OVL), 0) < live
        for t in range(W // OVL):
            columns = pl.ds(t * OVL, OVL)
            new = three(stacked, split(factor_ref[:, columns]))
            for i in range(2):
                targets[i][:, columns] = jnp.where(
                    keep, new[i * length : (i + 1) * length], sources[i][:, columns]
                )

    for core in range(2):

        @pl.when(at_ref[0] == core)
        def _(core=core):
            refs = (own_ref, other_ref) if core == 0 else (other_ref, own_ref)
            update(refs[0], (ra_ref, rb_ref), outs[:2], at_ref[1])
            update(refs[1], (ca_ref, cb_ref), outs[2:], at_ref[2])


def slab_products(at, factor, factor_other, slabs):
    whole = pl.BlockSpec(memory_space=pltpu.VMEM)
    return pl.pallas_call(
        slab_kernel,
        out_shape=[jax.ShapeDtypeStruct(s.shape, jnp.float32) for s in slabs],
        in_specs=[pl.BlockSpec(memory_space=pltpu.SMEM)] + [whole] * 6,
        out_specs=[whole] * 4,
        compiler_params=pltpu.CompilerParams(vmem_limit_bytes=40 * 2**20),
        cost_estimate=pl.CostEstimate(flops=4 * 2 * 3 * 128 * W * W, bytes_accessed=8 * 2**20, transcendentals=0),
    )(at, factor, factor_other, *slabs)


def source_kernel(at_ref, own_ref, other_ref, window_ref, slices_ref, chain_ref, out_ref, base, reach):
    for core in range(2):

        @pl.when(at_ref[0] == core)
        def _(core=core):
            left_ref, right_ref = (own_ref, other_ref) if core == 0 else (other_ref, own_ref)
            half = split(three(split(window_ref[...]), split(right_ref[...])))
            left = split(left_ref[...])
            base[...] = three(half, left, TN) if core == 0 else three(left, half, TN)

    source = split(base[...])
    reach[:GROUP] = jnp.zeros((GROUP, SLICE, OVL), jnp.float32)
    for t in range(GROUP):
        near = split(three(split(slices_ref[t]), source))
        reach[GROUP + t] = three(near, split(chain_ref[t]), NT)
    group, member = at_ref[3], at_ref[4]
    for target in range(16):
        g, m = target // GROUP, target % GROUP
        place = jnp.where(
            group == g, GROUP + m - 1 - member, jnp.where(group < g, 2 * GROUP - 1 - member, 0)
        )
        out_ref[target] = reach[place]


def source_terms(at, factor, factor_other, window, slices, chain):
    whole = pl.BlockSpec(memory_space=pltpu.VMEM)
    edge = pl.BlockSpec((W, OVL), lambda i: (0, EDGE // OVL))

    def block(shape):
        return pl.BlockSpec(shape, lambda i: (0,) * len(shape))

    return pl.pallas_call(
        source_kernel,
        grid=(1,),
        out_shape=jax.ShapeDtypeStruct((16, SLICE, OVL), jnp.float32),
        in_specs=[
            pl.BlockSpec(memory_space=pltpu.SMEM),
            edge,
            edge,
            block((W, W)),
            block((GROUP, SLICE, OVL)),
            block((GROUP, OVL, OVL)),
        ],
        out_specs=block((16, SLICE, OVL)),
        scratch_shapes=[
            pltpu.VMEM((OVL, OVL), jnp.float32),
            pltpu.VMEM((2 * GROUP, SLICE, OVL), jnp.float32),
        ],
        compiler_params=pltpu.CompilerParams(vmem_limit_bytes=40 * 2**20),
        cost_estimate=pl.CostEstimate(flops=2 * 3 * OVL * W * (W + OVL), bytes_accessed=7 * 2**20, transcendentals=0),
    )(at, factor, factor_other, window, slices, chain)


def shards(left, right, window_a, window_b, row_a, row_b, column_a, column_b, row_live, column_live):
    slab_index = lax.axis_index("slab")
    owner = lax.axis_index("diag")
    first_core = slab_index % 2 == 0
    chip = slab_index // 2
    x, y = chip // 4, chip % 4
    group, member = owner // GROUP, owner % GROUP

    def of_chip(for_first, for_second):
        got = swap_cores(jnp.where(first_core, for_second, for_first))
        return jnp.where(
            first_core,
            jnp.concatenate([for_first, got]),
            jnp.concatenate([got, for_second]),
        )

    def placed(blocks):
        full = jnp.zeros((CHIPS, ROWS, W), jnp.float32)
        for i, block in enumerate(blocks):
            place = (x ^ (i // 4)) * 4 + (y + i % 4) % 4
            full = lax.dynamic_update_slice(full, block[None], (place, 0, 0))
        return full.reshape(W, W)

    own_factor = of_chip(left[0], right[0])
    own_window = of_chip(window_a[0], window_b[0])
    first = first_round(own_factor)
    own_window, *first = lax.optimization_barrier((own_window, *first))
    first_window = first_round(own_window)
    factor = placed(later_rounds(own_factor, first))
    window = placed(later_rounds(own_window, first_window))
    factor_other = swap_cores(factor)
    corner = factor[:OVL, EDGE:].T
    around = [corner] + [from_member(corner, d) for d in range(1, GROUP)]

    eye = jnp.eye(OVL, dtype=jnp.float32)
    chain, before = [eye, around[1]], [eye, around[3]]
    for t in range(2, GROUP):
        chain.append(mul(around[t], chain[-1]))
        before.append(mul(before[-1], around[GROUP - t]))
    chain = jnp.stack(chain)
    slices = swap_cores(lax.dynamic_slice_in_dim(chain, chip * SLICE, SLICE, 1))
    prefix = lax.dynamic_index_in_dim(jnp.stack(before), member, 0, keepdims=False)
    rest = lax.dynamic_index_in_dim(chain, GROUP - 1 - member, 0, keepdims=False)
    whole = mul(rest, mul(corner, prefix))
    second = mul(prefix, from_group(whole, 1))
    third_back = mul(second, from_group(whole, 2))
    spans = jnp.stack([third_back, second, prefix])
    spans_other = swap_cores(spans)

    length = row_a.shape[1]
    begin = slab_index * length
    at = jnp.stack(
        [slab_index % 2, row_live[0] - begin, column_live[0] - begin, group, member]
    ).astype(jnp.int32)
    outgoing = source_terms(at, factor, factor_other, window, slices, chain)
    incoming = lax.all_to_all(outgoing, "diag", split_axis=0, concat_axis=0, tiled=True)
    sums = jnp.sum(incoming.reshape(4, GROUP, SLICE, OVL), 1)
    sums = jnp.concatenate([jnp.zeros((3, SLICE, OVL), jnp.float32), sums])
    share = lax.dynamic_slice_in_dim(sums, group, 4, 0)
    shares = lax.all_to_all(
        jnp.broadcast_to(share[None], (CHIPS, 4, SLICE, OVL)),
        "slab",
        split_axis=0,
        concat_axis=0,
        tiled=True,
        axis_index_groups=SAME_CORE,
    )
    ends = shares.transpose(1, 0, 2, 3).reshape(4, OVL, OVL)
    step = lax.dot_general(
        ends[:3],
        spans * 2.0**-16,
        (((2,), (2,)), ((0,), (0,))),
        precision=HIGH,
        preferred_element_type=jnp.float32,
    )
    through = mul(spans_other.transpose(1, 0, 2).reshape(OVL, 3 * OVL), step.reshape(3 * OVL, OVL))
    carry = ends[3] + through * 2.0**16
    carry = jnp.where(first_core, carry.T, carry)

    left_full = jnp.where(first_core, factor, factor_other)
    right_full = jnp.where(first_core, factor_other, factor)
    own_columns = lax.dynamic_slice_in_dim(left_full, chip * ROWS, ROWS, 1)
    base = mul(mul(own_columns, window, TN), right_full)
    updated = base + mul(mul(own_columns[:OVL], carry, TN), right_full[:OVL])
    kept = jnp.where(first_core, updated[: ROWS // 2], updated[ROWS // 2 :])
    sent = jnp.where(first_core, updated[ROWS // 2 :], updated[: ROWS // 2])
    received = swap_cores(sent)
    updated_a = jnp.where(first_core, kept, received)
    updated_b = jnp.where(first_core, received, kept)

    slabs = slab_products(
        at, factor, factor_other, (row_a[0], row_b[0], column_a[0], column_b[0])
    )
    return (updated_a[None], updated_b[None], *(slab[None] for slab in slabs))


def solution(mesh):
    rows = P("diag", "slab", None)
    return jax.shard_map(
        shards,
        mesh=mesh,
        in_specs=(rows,) * 8 + (P("diag"),) * 2,
        out_specs=(rows,) * 6,
        check_vma=False,
    )
```

```python
import jax
import jax.numpy as jnp
from jax import lax
from jax.experimental import pallas as pl
from jax.experimental.pallas import tpu as pltpu
from jax.sharding import PartitionSpec as P

OVL = 256
W = 768
EDGE = W - OVL
ROWS = 96
CHIPS = 8
SLICE = OVL // CHIPS
GROUP = 4

NN = (((1,), (0,)), ((), ()))
TN = (((0,), (0,)), ((), ()))


def slab_route(move):
    return [
        ((x * 4 + y) * 2 + c, (move(x, y)[0] * 4 + move(x, y)[1]) * 2 + c)
        for x in range(2)
        for y in range(4)
        for c in range(2)
    ]


CROSS = slab_route(lambda x, y: (1 - x, y))
UP = slab_route(lambda x, y: (x, (y + 1) % 4))
DOWN = slab_route(lambda x, y: (x, (y + 3) % 4))
OTHER_CORE = [(i, i ^ 1) for i in range(16)]
SAME_CORE = [[i for i in range(16) if i % 2 == c] for c in range(2)]


def swap_cores(block):
    return lax.ppermute(block, "slab", OTHER_CORE)


def from_member(block, d):
    route = [(g * 4 + (m + d) % 4, g * 4 + m) for g in range(4) for m in range(4)]
    return lax.ppermute(block, "diag", route)


def from_group(block, d):
    return lax.ppermute(block, "diag", [(i, i + 4 * d) for i in range(4, 16 - 4 * d)])


def first_round(own):
    return [lax.ppermute(own, "slab", route) for route in (CROSS, UP, DOWN)]


def later_rounds(own, first):
    cross, below, above = first
    far = lax.ppermute(above, "slab", DOWN)
    cross_above = lax.ppermute(above, "slab", CROSS)
    cross_below = lax.ppermute(cross, "slab", UP)
    cross_far = lax.ppermute(far, "slab", CROSS)
    return [own, above, far, below, cross, cross_above, cross_far, cross_below]


def split(a):
    high = a.astype(jnp.bfloat16)
    return high, (a - high.astype(jnp.float32)).astype(jnp.bfloat16)


def three(a, b, dims=NN):
    def dot(p, q):
        return lax.dot_general(p, q, dims, preferred_element_type=jnp.float32)

    return dot(a[0], b[0]) + (dot(a[0], b[1]) + dot(a[1], b[0]))


CORE, ROW_LIVE, COLUMN_LIVE, MY_GROUP, MEMBER, CHIP, PLACE = range(7)
SCALARS = pl.BlockSpec(memory_space=pltpu.SMEM)
WHOLE = pl.BlockSpec(memory_space=pltpu.VMEM)


def local_kernel(body, shapes, flops, scratch=(), in_specs=None):
    def call(at, *arrays):
        specs = [WHOLE] * len(arrays) if in_specs is None else in_specs
        moved = sum(a.size for a in arrays) * 4
        return pl.pallas_call(
            body,
            grid=(1,),
            out_shape=[jax.ShapeDtypeStruct(shape, jnp.float32) for shape in shapes],
            in_specs=[SCALARS] + specs,
            out_specs=[WHOLE] * len(shapes),
            scratch_shapes=[pltpu.VMEM(shape, jnp.float32) for shape in scratch],
            compiler_params=pltpu.CompilerParams(vmem_limit_bytes=40 * 2**20),
            cost_estimate=pl.CostEstimate(flops=6 * flops, bytes_accessed=moved, transcendentals=0),
        )(at, *arrays)

    return call


def product_of(a, b, dims=NN):
    return three(split(a), split(b), dims)


def chip_rows(at_ref):
    return pl.ds(pl.multiple_of(at_ref[CHIP] * SLICE, SLICE), SLICE)


def by_core(at_ref, own_ref, other_ref, run):
    for core in range(2):

        @pl.when(at_ref[CORE] == core)
        def _(core=core):
            run(*((own_ref, other_ref) if core == 0 else (other_ref, own_ref)), core)


def slab_body(at_ref, own_ref, other_ref, ra_ref, rb_ref, ca_ref, cb_ref, *outs):
    length = ra_ref.shape[0]

    def update(factor_ref, sources, targets, live):
        stacked = split(jnp.concatenate([source[...] for source in sources]))
        keep = lax.broadcasted_iota(jnp.int32, (length, OVL), 0) < live
        for t in range(W // OVL):
            columns = pl.ds(t * OVL, OVL)
            new = three(stacked, split(factor_ref[:, columns]))
            for i in range(2):
                targets[i][:, columns] = jnp.where(
                    keep, new[i * length : (i + 1) * length], sources[i][:, columns]
                )

    def run(left_ref, right_ref, core):
        update(left_ref, (ra_ref, rb_ref), outs[:2], at_ref[ROW_LIVE])
        update(right_ref, (ca_ref, cb_ref), outs[2:], at_ref[COLUMN_LIVE])

    by_core(at_ref, own_ref, other_ref, run)


def corner_body(at_ref, own_ref, other_ref, *refs):
    blocks, (corner_ref, window_ref) = refs[:CHIPS], refs[CHIPS:]
    for i in range(CHIPS):
        start = pl.multiple_of(at_ref[PLACE + i] * ROWS, ROWS)
        window_ref[pl.ds(start, ROWS), :] = blocks[i][...]

    def run(left_ref, right_ref, core):
        half = split(product_of(window_ref[...], right_ref[...]))
        left = split(left_ref[...])
        corner_ref[...] = three(half, left, TN) if core == 0 else three(left, half, TN)

    by_core(at_ref, own_ref, other_ref, run)


def chain_body(at_ref, one_ref, two_ref, three_ref, chain_ref, slices_ref, turned):
    second = product_of(one_ref[...], two_ref[...])
    chain_ref[0] = second
    chain_ref[1] = product_of(second, three_ref[...])
    for t in range(GROUP - 1):
        turned[...] = (one_ref[...] if t == 0 else chain_ref[t - 1]).T
        slices_ref[t] = turned[chip_rows(at_ref), :]


def terms_body(at_ref, corner_ref, slices_ref, one_ref, chain_ref, out_ref, reach):
    corner = split(corner_ref[...])
    reach[:GROUP] = jnp.zeros((GROUP, SLICE, OVL), jnp.float32)
    reach[GROUP] = corner_ref[chip_rows(at_ref), :]
    for t in range(GROUP - 1):
        near = three(split(slices_ref[t]), corner)
        reach[GROUP + 1 + t] = product_of(near, one_ref[...] if t == 0 else chain_ref[t - 1])
    group, member = at_ref[MY_GROUP], at_ref[MEMBER]
    for target in range(16):
        g, m = target // GROUP, target % GROUP
        place = jnp.where(
            group == g, GROUP + m - 1 - member, jnp.where(group < g, 2 * GROUP - 1 - member, 0)
        )
        out_ref[target] = reach[place]


def prefix_body(at_ref, zero_ref, one_ref, two_ref, three_ref, chain_ref, prefix_ref, whole_ref):
    member = at_ref[MEMBER]
    third = three_ref[...]
    second = product_of(two_ref[...], third)

    @pl.when(member == 0)
    def _():
        row = lax.broadcasted_iota(jnp.int32, (OVL, OVL), 0)
        column = lax.broadcasted_iota(jnp.int32, (OVL, OVL), 1)
        prefix_ref[...] = jnp.where(row == column, 1.0, 0.0)

    @pl.when(member == 1)
    def _():
        prefix_ref[...] = third

    @pl.when(member == 2)
    def _():
        prefix_ref[...] = second

    @pl.when(member == 3)
    def _():
        prefix_ref[...] = product_of(one_ref[...], second)

    part = product_of(prefix_ref[chip_rows(at_ref), :], zero_ref[...])
    whole_ref[...] = part
    for t in range(1, GROUP):

        @pl.when(member == GROUP - 1 - t)
        def _(t=t):
            whole_ref[...] = product_of(part, one_ref[...] if t == 1 else chain_ref[t - 2])


def base_body(at_ref, own_ref, other_ref, window_ref, columns_ref, base_ref):
    def run(left_ref, right_ref, core):
        base_ref[...] = product_of(
            product_of(columns_ref[...], window_ref[...], TN), right_ref[...]
        )

    by_core(at_ref, own_ref, other_ref, run)


def final_body(
    at_ref, own_ref, other_ref, ends_ref, spans_ref, prefix_ref, prefix_other_ref, columns_ref, base_ref, out_ref
):
    core = at_ref[CORE]

    def end(i):
        return ends_ref[:, i].reshape(OVL, OVL)

    def span(of, i):
        return spans_ref[:, pl.ds(of, 1), i].reshape(OVL, OVL)

    def through(carry, span_own, span_other):
        return product_of(span_other, product_of(carry, span_own * 2.0**-32), TN) * 2.0**32

    carry = end(0)
    for i in range(2):
        carry = end(i + 1) + through(carry, span(core, i), span(1 - core, i))
    carry = end(3) + through(carry, prefix_ref[...], prefix_other_ref[...])

    def run(left_ref, right_ref, core):
        turned = (((0,), (1,)), ((), ())) if core == 0 else TN
        part = product_of(columns_ref[...], carry, turned)
        out_ref[...] = base_ref[...] + product_of(part, right_ref[...])

    by_core(at_ref, own_ref, other_ref, run)


EDGE_COLUMNS = pl.BlockSpec((W, OVL), lambda i: (0, EDGE // OVL))
TOP_ROWS = pl.BlockSpec((OVL, W), lambda i: (0, 0))


def shards(left, right, window_a, window_b, row_a, row_b, column_a, column_b, row_live, column_live):
    slab_index = lax.axis_index("slab")
    owner = lax.axis_index("diag")
    first_core = slab_index % 2 == 0
    chip = slab_index // 2
    x, y = chip // 4, chip % 4
    group, member = owner // GROUP, owner % GROUP

    def of_chip(for_first, for_second):
        got = swap_cores(jnp.where(first_core, for_second, for_first))
        return jnp.where(
            first_core,
            jnp.concatenate([for_first, got]),
            jnp.concatenate([got, for_second]),
        )

    def placed(blocks):
        full = jnp.zeros((CHIPS, ROWS, W), jnp.float32)
        for i, block in enumerate(blocks):
            place = (x ^ (i // 4)) * 4 + (y + i % 4) % 4
            full = lax.dynamic_update_slice(full, block[None], (place, 0, 0))
        return full.reshape(W, W)

    places = [(x ^ (i // 4)) * 4 + (y + i % 4) % 4 for i in range(CHIPS)]
    length = row_a.shape[1]
    begin = slab_index * length
    at = [slab_index % 2, row_live[0] - begin, column_live[0] - begin, group, member, chip]
    at = jnp.stack(at + places).astype(jnp.int32)

    own_factor = of_chip(left[0], right[0])
    own_window = of_chip(window_a[0], window_b[0])
    blocks = first_round(own_factor)
    blocks = later_rounds(own_factor, blocks)
    own_window, *blocks[:6] = lax.optimization_barrier((own_window, *blocks[:6]))
    window_blocks = later_rounds(own_window, first_round(own_window))
    factor = placed(blocks)
    factor_other = swap_cores(factor)
    corner = factor[:OVL, EDGE:]
    around = [corner] + [from_member(corner, d) for d in range(1, GROUP)]

    base_corner, window = local_kernel(
        corner_body,
        [(OVL, OVL), (W, W)],
        OVL * W * (W + OVL),
        in_specs=[EDGE_COLUMNS] * 2 + [WHOLE] * CHIPS,
    )(at, factor, factor_other, *window_blocks)
    chain, slices = local_kernel(
        chain_body, [(2, OVL, OVL), (3, SLICE, OVL)], 2 * OVL**3, [(OVL, OVL)]
    )(at, *around[1:])
    slices = swap_cores(slices)
    (outgoing,) = local_kernel(
        terms_body, [(16, SLICE, OVL)], 6 * SLICE * OVL * OVL, [(2 * GROUP, SLICE, OVL)]
    )(at, base_corner, slices, around[1], chain)
    incoming = lax.all_to_all(outgoing, "diag", split_axis=0, concat_axis=0, tiled=True)

    prefix, whole = local_kernel(prefix_body, [(OVL, OVL), (SLICE, OVL)], 3 * OVL**3)(
        at, *around, chain
    )
    prefix_other = swap_cores(prefix)
    spans = jnp.stack([from_group(whole, 2), from_group(whole, 1)])
    spans = lax.all_to_all(
        jnp.broadcast_to(spans[None], (2 * CHIPS, 2, SLICE, OVL)),
        "slab",
        split_axis=0,
        concat_axis=0,
        tiled=True,
    ).reshape(CHIPS, 2, 2, SLICE, OVL)

    slabs = local_kernel(slab_body, [row_a.shape[1:]] * 4, 4 * length * W * W)(
        at, factor, factor_other, row_a[0], row_b[0], column_a[0], column_b[0]
    )
    own_columns = jnp.where(
        first_core,
        lax.dynamic_slice_in_dim(factor, chip * ROWS, ROWS, 1),
        lax.dynamic_slice_in_dim(factor_other, chip * ROWS, ROWS, 1),
    )
    (base,) = local_kernel(base_body, [(ROWS, W)], 2 * ROWS * W * W)(
        at, factor, factor_other, window, own_columns
    )
    incoming, base, *slabs = lax.optimization_barrier((incoming, base, *slabs))

    sums = jnp.sum(incoming.reshape(4, GROUP, SLICE, OVL), 1)
    sums = jnp.concatenate([jnp.zeros((3, SLICE, OVL), jnp.float32), sums])
    share = lax.dynamic_slice_in_dim(sums, group, 4, 0)
    ends = lax.all_to_all(
        jnp.broadcast_to(share[None], (CHIPS, 4, SLICE, OVL)),
        "slab",
        split_axis=0,
        concat_axis=0,
        tiled=True,
        axis_index_groups=SAME_CORE,
    )
    (updated,) = local_kernel(
        final_body,
        [(ROWS, W)],
        6 * OVL**3 + ROWS * OVL * (OVL + W),
        in_specs=[TOP_ROWS] * 2 + [WHOLE] * 6,
    )(at, factor, factor_other, ends, spans, prefix, prefix_other, own_columns[:OVL], base)
    kept = jnp.where(first_core, updated[: ROWS // 2], updated[ROWS // 2 :])
    sent = jnp.where(first_core, updated[ROWS // 2 :], updated[: ROWS // 2])
    received = swap_cores(sent)
    updated_a = jnp.where(first_core, kept, received)
    updated_b = jnp.where(first_core, received, kept)
    return (updated_a[None], updated_b[None], *(slab[None] for slab in slabs))


def solution(mesh):
    rows = P("diag", "slab", None)
    return jax.shard_map(
        shards,
        mesh=mesh,
        in_specs=(rows,) * 8 + (P("diag"),) * 2,
        out_specs=(rows,) * 6,
        check_vma=False,
    )
```

```python
import jax
import jax.numpy as jnp
from jax import lax
from jax.experimental import pallas as pl
from jax.experimental.pallas import tpu as pltpu
from jax.sharding import PartitionSpec as P

OVL = 256
W = 768
EDGE = W - OVL
ROWS = 96
CHIPS = 8
SLICE = OVL // CHIPS
GROUP = 4
QUARTER = OVL // 4

NN = (((1,), (0,)), ((), ()))
TN = (((0,), (0,)), ((), ()))


def slab_route(move):
    return [
        ((x * 4 + y) * 2 + c, (move(x, y)[0] * 4 + move(x, y)[1]) * 2 + c)
        for x in range(2)
        for y in range(4)
        for c in range(2)
    ]


CROSS = slab_route(lambda x, y: (1 - x, y))
UP = slab_route(lambda x, y: (x, (y + 1) % 4))
DOWN = slab_route(lambda x, y: (x, (y + 3) % 4))
OTHER_CORE = [(i, i ^ 1) for i in range(16)]
SAME_CORE = [[i for i in range(16) if i % 2 == c] for c in range(2)]


def swap_cores(block):
    return lax.ppermute(block, "slab", OTHER_CORE)


def from_member(block, d):
    route = [(g * 4 + (m + d) % 4, g * 4 + m) for g in range(4) for m in range(4)]
    return lax.ppermute(block, "diag", route)


def from_group(block, d):
    return lax.ppermute(block, "diag", [(i, i + 4 * d) for i in range(4, 16 - 4 * d)])


def first_round(own):
    return [lax.ppermute(own, "slab", route) for route in (CROSS, UP, DOWN)]


def second_round(cross, below, above):
    return [
        lax.ppermute(block, "slab", route)
        for block, route in ((above, DOWN), (above, CROSS), (cross, UP))
    ]


def last_round(far):
    return lax.ppermute(far, "slab", CROSS)


def by_position(own, first, second, last):
    cross, below, above = first
    far, cross_above, cross_below = second
    return [own, above, far, below, cross, cross_above, last, cross_below]


def split(a):
    high = a.astype(jnp.bfloat16)
    return high, (a - high.astype(jnp.float32)).astype(jnp.bfloat16)


def three(a, b, dims=NN):
    def dot(p, q):
        return lax.dot_general(p, q, dims, preferred_element_type=jnp.float32)

    return dot(a[0], b[0]) + (dot(a[0], b[1]) + dot(a[1], b[0]))


CORE, ROW_LIVE, COLUMN_LIVE, MY_GROUP, MEMBER, CHIP, MY_Y, PLACE = range(8)
SCALARS = pl.BlockSpec(memory_space=pltpu.SMEM)


def block_of(shape):
    return pl.BlockSpec(shape, lambda i: (0,) * len(shape))


def local_kernel(body, shapes, flops, scratch=(), in_specs=()):
    def call(at, *arrays):
        specs = list(in_specs) + [block_of(a.shape) for a in arrays[len(in_specs) :]]
        moved = sum(a.size for a in arrays) * 4
        return pl.pallas_call(
            body,
            grid=(1,),
            out_shape=[jax.ShapeDtypeStruct(shape, jnp.float32) for shape in shapes],
            in_specs=[SCALARS] + specs,
            out_specs=[block_of(shape) for shape in shapes],
            scratch_shapes=[pltpu.VMEM(shape, jnp.float32) for shape in scratch],
            compiler_params=pltpu.CompilerParams(vmem_limit_bytes=48 * 2**20),
            cost_estimate=pl.CostEstimate(flops=6 * flops, bytes_accessed=moved, transcendentals=0),
        )(at, *arrays)

    return call


def product_of(a, b, dims=NN):
    return three(split(a), split(b), dims)


def chip_rows(at_ref):
    return pl.ds(pl.multiple_of(at_ref[CHIP] * SLICE, SLICE), SLICE)


def by_core(at_ref, own_ref, other_ref, run):
    for core in range(2):

        @pl.when(at_ref[CORE] == core)
        def _(core=core):
            run(*((own_ref, other_ref) if core == 0 else (other_ref, own_ref)), core)


def slab_body(at_ref, own_ref, other_ref, ra_ref, rb_ref, ca_ref, cb_ref, *outs):
    length = ra_ref.shape[0]

    def update(factor_ref, sources, targets, live):
        stacked = split(jnp.concatenate([source[...] for source in sources]))
        keep = lax.broadcasted_iota(jnp.int32, (length, OVL), 0) < live
        for t in range(W // OVL):
            columns = pl.ds(t * OVL, OVL)
            new = three(stacked, split(factor_ref[:, columns]))
            for i in range(2):
                targets[i][:, columns] = jnp.where(
                    keep, new[i * length : (i + 1) * length], sources[i][:, columns]
                )

    def run(left_ref, right_ref, core):
        update(left_ref, (ra_ref, rb_ref), outs[:2], at_ref[ROW_LIVE])
        update(right_ref, (ca_ref, cb_ref), outs[2:], at_ref[COLUMN_LIVE])

    by_core(at_ref, own_ref, other_ref, run)


def corner_body(at_ref, own_ref, other_ref, *refs):
    blocks, (corner_ref, window_ref) = refs[:CHIPS], refs[CHIPS:]
    for i in range(CHIPS):
        start = pl.multiple_of(at_ref[PLACE + i] * ROWS, ROWS)
        window_ref[pl.ds(start, ROWS), :] = blocks[i][...]

    def run(left_ref, right_ref, core):
        half = split(product_of(window_ref[...], right_ref[...]))
        left = split(left_ref[...])
        corner_ref[...] = three(half, left, TN) if core == 0 else three(left, half, TN)

    by_core(at_ref, own_ref, other_ref, run)


def chain_body(at_ref, one_ref, two_ref, three_ref, chain_ref, slices_ref, turned):
    second = product_of(one_ref[...], two_ref[...])
    chain_ref[0] = second
    chain_ref[1] = product_of(second, three_ref[...])
    for t in range(GROUP - 1):
        turned[...] = (one_ref[...] if t == 0 else chain_ref[t - 1]).T
        slices_ref[t] = turned[chip_rows(at_ref), :]


def terms_body(at_ref, corner_ref, slices_ref, one_ref, chain_ref, out_ref, reach):
    corner = split(corner_ref[...])
    reach[:GROUP] = jnp.zeros((GROUP, SLICE, OVL), jnp.float32)
    reach[GROUP] = corner_ref[chip_rows(at_ref), :]
    for t in range(GROUP - 1):
        near = three(split(slices_ref[t]), corner)
        reach[GROUP + 1 + t] = product_of(near, one_ref[...] if t == 0 else chain_ref[t - 1])
    group, member = at_ref[MY_GROUP], at_ref[MEMBER]
    for target in range(16):
        g, m = target // GROUP, target % GROUP
        place = jnp.where(
            group == g, GROUP + m - 1 - member, jnp.where(group < g, 2 * GROUP - 1 - member, 0)
        )
        out_ref[target] = reach[place]


def prefix_body(at_ref, zero_ref, one_ref, two_ref, three_ref, chain_ref, prefix_ref, whole_ref):
    member = at_ref[MEMBER]
    third = three_ref[...]
    second = product_of(two_ref[...], third)

    @pl.when(member == 0)
    def _():
        row = lax.broadcasted_iota(jnp.int32, (OVL, OVL), 0)
        column = lax.broadcasted_iota(jnp.int32, (OVL, OVL), 1)
        prefix_ref[...] = jnp.where(row == column, 1.0, 0.0)

    @pl.when(member == 1)
    def _():
        prefix_ref[...] = third

    @pl.when(member == 2)
    def _():
        prefix_ref[...] = second

    @pl.when(member == 3)
    def _():
        prefix_ref[...] = product_of(one_ref[...], second)

    rows = pl.ds(pl.multiple_of(at_ref[MY_Y] * QUARTER, QUARTER), QUARTER)
    part = product_of(prefix_ref[rows, :], zero_ref[...])
    whole_ref[...] = part
    for t in range(1, GROUP):

        @pl.when(member == GROUP - 1 - t)
        def _(t=t):
            whole_ref[...] = product_of(part, one_ref[...] if t == 1 else chain_ref[t - 2])


def sum_body(at_ref, in_ref, out_ref):
    for i in range(4):
        group = at_ref[MY_GROUP] - 3 + i
        first = jnp.maximum(group, 0) * GROUP
        total = in_ref[first]
        for m in range(1, GROUP):
            total = total + in_ref[first + m]
        total = jnp.where(group >= 0, total, 0.0)
        for chip in range(CHIPS):
            out_ref[chip, i] = total


def base_body(at_ref, own_ref, other_ref, window_ref, columns_ref, base_ref):
    def run(left_ref, right_ref, core):
        base_ref[...] = product_of(
            product_of(columns_ref[...], window_ref[...], TN), right_ref[...]
        )

    by_core(at_ref, own_ref, other_ref, run)


def final_body(
    at_ref, own_ref, other_ref, ends_ref, prefix_ref, prefix_other_ref, columns_ref, base_ref,
    span_0_ref, span_1_ref, span_2_ref, span_3_ref, out_ref, spans,
):
    for dy, ref in enumerate((span_0_ref, span_1_ref, span_2_ref, span_3_ref)):
        start = pl.multiple_of((at_ref[MY_Y] + dy) % 4 * QUARTER, QUARTER)
        for i in range(4):
            spans[i, pl.ds(start, QUARTER), :] = ref[i]

    def end(i):
        return ends_ref[:, i].reshape(OVL, OVL)

    def through(carry, span_own, span_other):
        return product_of(span_other, product_of(carry, span_own * 2.0**-32), TN) * 2.0**32

    carry = end(0)
    for i in range(2):
        carry = end(i + 1) + through(carry, spans[i], spans[2 + i])
    carry = end(3) + through(carry, prefix_ref[...], prefix_other_ref[...])

    def run(left_ref, right_ref, core):
        turned = (((0,), (1,)), ((), ())) if core == 0 else TN
        part = product_of(columns_ref[...], carry, turned)
        out_ref[...] = base_ref[...] + product_of(part, right_ref[...])

    by_core(at_ref, own_ref, other_ref, run)


EDGE_COLUMNS = pl.BlockSpec((W, OVL), lambda i: (0, EDGE // OVL))
TOP_ROWS = pl.BlockSpec((OVL, W), lambda i: (0, 0))


def shards(left, right, window_a, window_b, row_a, row_b, column_a, column_b, row_live, column_live):
    slab_index = lax.axis_index("slab")
    owner = lax.axis_index("diag")
    first_core = slab_index % 2 == 0
    chip = slab_index // 2
    x, y = chip // 4, chip % 4
    group, member = owner // GROUP, owner % GROUP

    def of_chip(for_first, for_second):
        got = swap_cores(jnp.where(first_core, for_second, for_first))
        return jnp.where(
            first_core,
            jnp.concatenate([for_first, got]),
            jnp.concatenate([got, for_second]),
        )

    def placed(blocks):
        full = jnp.zeros((CHIPS, ROWS, W), jnp.float32)
        for i, block in enumerate(blocks):
            place = (x ^ (i // 4)) * 4 + (y + i % 4) % 4
            full = lax.dynamic_update_slice(full, block[None], (place, 0, 0))
        return full.reshape(W, W)

    places = [(x ^ (i // 4)) * 4 + (y + i % 4) % 4 for i in range(CHIPS)]
    length = row_a.shape[1]
    begin = slab_index * length
    at = [slab_index % 2, row_live[0] - begin, column_live[0] - begin, group, member, chip, y]
    at = jnp.stack(at + places).astype(jnp.int32)

    together = lax.optimization_barrier
    own_factor = of_chip(left[0], right[0])
    own_window = of_chip(window_a[0], window_b[0])
    factor_1 = first_round(own_factor)
    own_window, *factor_1 = together((own_window, *factor_1))
    factor_2 = second_round(*factor_1)
    own_window, *factor_2 = together((own_window, *factor_2))
    factor_3 = last_round(factor_2[0])
    window_1 = first_round(own_window)
    factor_3, *window_1 = together((factor_3, *window_1))
    factor = placed(by_position(own_factor, factor_1, factor_2, factor_3))
    corner = factor[:OVL, EDGE:]
    corner, *window_1 = together((corner, *window_1))
    one, two = from_member(corner, 1), from_member(corner, 2)
    window_2 = second_round(*window_1)
    factor_other = swap_cores(factor)
    corner, one, two, factor_other, *window_2 = together((corner, one, two, factor_other, *window_2))
    three_on = from_member(corner, 3)
    window_3 = last_round(window_2[0])
    slabs = local_kernel(slab_body, [row_a.shape[1:]] * 4, 4 * length * W * W)(
        at, factor, factor_other, row_a[0], row_b[0], column_a[0], column_b[0]
    )
    three_on, window_3, *slabs = together((three_on, window_3, *slabs))
    window_blocks = by_position(own_window, window_1, window_2, window_3)

    chain, slices = local_kernel(
        chain_body, [(2, OVL, OVL), (3, SLICE, OVL)], 2 * OVL**3, [(OVL, OVL)]
    )(at, one, two, three_on)
    slices = swap_cores(slices)
    base_corner, window = local_kernel(
        corner_body, [(OVL, OVL), (W, W)], OVL * W * (W + OVL), in_specs=[EDGE_COLUMNS] * 2
    )(at, factor, factor_other, *window_blocks)
    (outgoing,) = local_kernel(
        terms_body, [(16, SLICE, OVL)], 6 * SLICE * OVL * OVL, [(2 * GROUP, SLICE, OVL)]
    )(at, base_corner, slices, one, chain)
    outgoing, window, chain = together((outgoing, window, chain))
    incoming = lax.all_to_all(outgoing, "diag", split_axis=0, concat_axis=0, tiled=True)

    prefix, whole = local_kernel(prefix_body, [(OVL, OVL), (QUARTER, OVL)], 3 * OVL**3)(
        at, corner, one, two, three_on, chain
    )
    spans = jnp.stack([from_group(whole, 2), from_group(whole, 1)])
    spans = jnp.concatenate([spans, swap_cores(spans)])
    spans = [spans] + [
        lax.ppermute(spans, "slab", slab_route(lambda x, y: (x, (y - d) % 4))) for d in range(1, 4)
    ]
    own_columns = jnp.where(
        first_core,
        lax.dynamic_slice_in_dim(factor, chip * ROWS, ROWS, 1),
        lax.dynamic_slice_in_dim(factor_other, chip * ROWS, ROWS, 1),
    )
    (base,) = local_kernel(base_body, [(ROWS, W)], 2 * ROWS * W * W)(
        at, factor, factor_other, window, own_columns
    )
    prefix_other = swap_cores(prefix)
    incoming, base, prefix_other, *spans = together((incoming, base, prefix_other, *spans))

    (shares,) = local_kernel(sum_body, [(CHIPS, 4, SLICE, OVL)], 0)(at, incoming)
    ends = lax.all_to_all(
        shares, "slab", split_axis=0, concat_axis=0, tiled=True, axis_index_groups=SAME_CORE
    )
    (updated,) = local_kernel(
        final_body,
        [(ROWS, W)],
        6 * OVL**3 + ROWS * OVL * (OVL + W),
        [(4, OVL, OVL)],
        in_specs=[TOP_ROWS] * 2,
    )(at, factor, factor_other, ends, prefix, prefix_other, own_columns[:OVL], base, *spans)
    kept = jnp.where(first_core, updated[: ROWS // 2], updated[ROWS // 2 :])
    sent = jnp.where(first_core, updated[ROWS // 2 :], updated[: ROWS // 2])
    received = swap_cores(sent)
    updated_a = jnp.where(first_core, kept, received)
    updated_b = jnp.where(first_core, received, kept)
    return (updated_a[None], updated_b[None], *(slab[None] for slab in slabs))


def solution(mesh):
    rows = P("diag", "slab", None)
    return jax.shard_map(
        shards,
        mesh=mesh,
        in_specs=(rows,) * 8 + (P("diag"),) * 2,
        out_specs=(rows,) * 6,
        check_vma=False,
    )
```

```python
import jax
import jax.numpy as jnp
from jax import lax
from jax.experimental import pallas as pl
from jax.experimental.pallas import tpu as pltpu
from jax.sharding import PartitionSpec as P

OVL = 256
W = 768
EDGE = W - OVL
ROWS = 96
CHIPS = 8
SLICE = OVL // CHIPS
GROUP = 4
QUARTER = OVL // 4

NN = (((1,), (0,)), ((), ()))
TN = (((0,), (0,)), ((), ()))


def slab_route(move):
    return [
        ((x * 4 + y) * 2 + c, (move(x, y)[0] * 4 + move(x, y)[1]) * 2 + c)
        for x in range(2)
        for y in range(4)
        for c in range(2)
    ]


CROSS = slab_route(lambda x, y: (1 - x, y))
UP = slab_route(lambda x, y: (x, (y + 1) % 4))
DOWN = slab_route(lambda x, y: (x, (y + 3) % 4))
OTHER_CORE = [(i, i ^ 1) for i in range(16)]
SAME_CORE = [[i for i in range(16) if i % 2 == c] for c in range(2)]


def swap_cores(block):
    return lax.ppermute(block, "slab", OTHER_CORE)


def from_member(block, d):
    route = [(g * 4 + (m + d) % 4, g * 4 + m) for g in range(4) for m in range(4)]
    return lax.ppermute(block, "diag", route)


def from_group(block, d):
    return lax.ppermute(block, "diag", [(i, i + 4 * d) for i in range(4, 16 - 4 * d)])


def first_round(own):
    return [lax.ppermute(own, "slab", route) for route in (CROSS, UP, DOWN)]


def second_round(cross, below, above):
    return [
        lax.ppermute(block, "slab", route)
        for block, route in ((above, DOWN), (above, CROSS), (cross, UP))
    ]


def by_position(own, first, second, last):
    cross, below, above = first
    far, cross_above, cross_below = second
    return [own, above, far, below, cross, cross_above, last, cross_below]


def split(a):
    high = a.astype(jnp.bfloat16)
    return high, (a - high.astype(jnp.float32)).astype(jnp.bfloat16)


def three(a, b, dims=NN):
    def dot(p, q):
        return lax.dot_general(p, q, dims, preferred_element_type=jnp.float32)

    return dot(a[0], b[0]) + (dot(a[0], b[1]) + dot(a[1], b[0]))


CORE, ROW_LIVE, COLUMN_LIVE, MY_GROUP, MEMBER, CHIP, MY_Y, PLACE = range(8)
SCALARS = pl.BlockSpec(memory_space=pltpu.SMEM)


def block_of(shape):
    return pl.BlockSpec(shape, lambda i: (0,) * len(shape))


def local_kernel(body, shapes, flops, scratch=(), in_specs=()):
    def call(at, *arrays):
        specs = list(in_specs) + [block_of(a.shape) for a in arrays[len(in_specs) :]]
        moved = sum(a.size for a in arrays) * 4
        return pl.pallas_call(
            body,
            grid=(1,),
            out_shape=[jax.ShapeDtypeStruct(shape, jnp.float32) for shape in shapes],
            in_specs=[SCALARS] + specs,
            out_specs=[block_of(shape) for shape in shapes],
            scratch_shapes=[pltpu.VMEM(shape, jnp.float32) for shape in scratch],
            compiler_params=pltpu.CompilerParams(vmem_limit_bytes=56 * 2**20),
            cost_estimate=pl.CostEstimate(flops=6 * flops, bytes_accessed=moved, transcendentals=0),
        )(at, *arrays)

    return call


def product_of(a, b, dims=NN):
    return three(split(a), split(b), dims)


def chip_rows(at_ref):
    return pl.ds(pl.multiple_of(at_ref[CHIP] * SLICE, SLICE), SLICE)


def by_core(at_ref, own_ref, other_ref, run):
    for core in range(2):

        @pl.when(at_ref[CORE] == core)
        def _(core=core):
            run(*((own_ref, other_ref) if core == 0 else (other_ref, own_ref)), core)


def slab_body(at_ref, own_ref, other_ref, ra_ref, rb_ref, ca_ref, cb_ref, *outs):
    length = ra_ref.shape[0]

    def update(factor_ref, sources, targets, live):
        stacked = split(jnp.concatenate([source[...] for source in sources]))
        keep = lax.broadcasted_iota(jnp.int32, (length, OVL), 0) < live
        for t in range(W // OVL):
            columns = pl.ds(t * OVL, OVL)
            new = three(stacked, split(factor_ref[:, columns]))
            for i in range(2):
                targets[i][:, columns] = jnp.where(
                    keep, new[i * length : (i + 1) * length], sources[i][:, columns]
                )

    def run(left_ref, right_ref, core):
        update(left_ref, (ra_ref, rb_ref), outs[:2], at_ref[ROW_LIVE])
        update(right_ref, (ca_ref, cb_ref), outs[2:], at_ref[COLUMN_LIVE])

    by_core(at_ref, own_ref, other_ref, run)


def corner_body(at_ref, own_ref, other_ref, *refs):
    blocks, (corner_ref, window_ref) = refs[:CHIPS], refs[CHIPS:]
    for i in range(CHIPS):
        start = pl.multiple_of(at_ref[PLACE + i] * ROWS, ROWS)
        window_ref[pl.ds(start, ROWS), :] = blocks[i][0]

    def run(left_ref, right_ref, core):
        half = split(product_of(window_ref[...], right_ref[...]))
        left = split(left_ref[...])
        corner_ref[...] = three(half, left, TN) if core == 0 else three(left, half, TN)

    by_core(at_ref, own_ref, other_ref, run)


def chain_body(at_ref, *refs):
    blocks, (corners_ref, chain_ref, slices_ref, rows, turned) = refs[:CHIPS], refs[CHIPS:]
    for i in range(CHIPS):
        place = at_ref[PLACE + i]

        @pl.when(place < 3)
        def _(i=i, place=place):
            rows[pl.ds(pl.multiple_of(place * ROWS, ROWS), ROWS), :] = blocks[i][0]

    corners_ref[...] = rows[:OVL]
    one = corners_ref[:, :OVL]
    second = product_of(one, corners_ref[:, OVL : 2 * OVL])
    chain_ref[0] = second
    chain_ref[1] = product_of(second, corners_ref[:, 2 * OVL :])
    for t in range(GROUP - 1):
        turned[...] = (one if t == 0 else chain_ref[t - 1]).T
        slices_ref[t] = turned[chip_rows(at_ref), :]


def terms_body(at_ref, one_ref, corner_ref, slices_ref, chain_ref, out_ref, reach):
    corner = split(corner_ref[...])
    reach[:GROUP] = jnp.zeros((GROUP, SLICE, OVL), jnp.float32)
    reach[GROUP] = corner_ref[chip_rows(at_ref), :]
    for t in range(GROUP - 1):
        near = three(split(slices_ref[t]), corner)
        reach[GROUP + 1 + t] = product_of(near, one_ref[...] if t == 0 else chain_ref[t - 1])
    group, member = at_ref[MY_GROUP], at_ref[MEMBER]
    for target in range(16):
        g, m = target // GROUP, target % GROUP
        place = jnp.where(
            group == g, GROUP + m - 1 - member, jnp.where(group < g, 2 * GROUP - 1 - member, 0)
        )
        out_ref[target] = reach[place]


def prefix_body(at_ref, zero_ref, corners_ref, chain_ref, prefix_ref, whole_ref):
    member = at_ref[MEMBER]
    one = corners_ref[:, :OVL]
    third = corners_ref[:, 2 * OVL :]
    second = product_of(corners_ref[:, OVL : 2 * OVL], third)

    @pl.when(member == 0)
    def _():
        row = lax.broadcasted_iota(jnp.int32, (OVL, OVL), 0)
        column = lax.broadcasted_iota(jnp.int32, (OVL, OVL), 1)
        prefix_ref[...] = jnp.where(row == column, 1.0, 0.0)

    @pl.when(member == 1)
    def _():
        prefix_ref[...] = third

    @pl.when(member == 2)
    def _():
        prefix_ref[...] = second

    @pl.when(member == 3)
    def _():
        prefix_ref[...] = product_of(one, second)

    rows = pl.ds(pl.multiple_of(at_ref[MY_Y] * QUARTER, QUARTER), QUARTER)
    part = product_of(prefix_ref[rows, :], zero_ref[...])
    whole_ref[...] = part
    for t in range(1, GROUP):

        @pl.when(member == GROUP - 1 - t)
        def _(t=t):
            whole_ref[...] = product_of(part, one if t == 1 else chain_ref[t - 2])


def sum_body(at_ref, in_ref, out_ref):
    for i in range(4):
        group = at_ref[MY_GROUP] - 3 + i
        first = jnp.maximum(group, 0) * GROUP
        total = in_ref[first]
        for m in range(1, GROUP):
            total = total + in_ref[first + m]
        total = jnp.where(group >= 0, total, 0.0)
        for chip in range(CHIPS):
            out_ref[chip, i] = total


def base_body(at_ref, own_ref, other_ref, window_ref, columns_ref, base_ref):
    def run(left_ref, right_ref, core):
        base_ref[...] = product_of(
            product_of(columns_ref[...], window_ref[...], TN), right_ref[...]
        )

    by_core(at_ref, own_ref, other_ref, run)


def final_body(
    at_ref, own_ref, other_ref, ends_ref, prefix_ref, prefix_other_ref, columns_ref, base_ref,
    span_0_ref, span_1_ref, span_2_ref, span_3_ref, out_ref, spans,
):
    for dy, ref in enumerate((span_0_ref, span_1_ref, span_2_ref, span_3_ref)):
        start = pl.multiple_of((at_ref[MY_Y] + dy) % 4 * QUARTER, QUARTER)
        for i in range(4):
            spans[i, pl.ds(start, QUARTER), :] = ref[i]

    def end(i):
        return ends_ref[:, i].reshape(OVL, OVL)

    def through(carry, span_own, span_other):
        return product_of(span_other, product_of(carry, span_own * 2.0**-32), TN) * 2.0**32

    carry = end(0)
    for i in range(2):
        carry = end(i + 1) + through(carry, spans[i], spans[2 + i])
    carry = end(3) + through(carry, prefix_ref[...], prefix_other_ref[...])

    def run(left_ref, right_ref, core):
        turned = (((0,), (1,)), ((), ())) if core == 0 else TN
        part = product_of(columns_ref[...], carry, turned)
        out_ref[...] = base_ref[...] + product_of(part, right_ref[...])

    by_core(at_ref, own_ref, other_ref, run)


EDGE_COLUMNS = pl.BlockSpec((W, OVL), lambda i: (0, EDGE // OVL))
TOP_ROWS = pl.BlockSpec((OVL, W), lambda i: (0, 0))
CORNER = pl.BlockSpec((OVL, OVL), lambda i: (0, EDGE // OVL))
FIRST_SQUARE = pl.BlockSpec((OVL, OVL), lambda i: (0, 0))
FIRST_PART = pl.BlockSpec((1, ROWS, W), lambda i: (0, 0, 0))
SECOND_PART = pl.BlockSpec((1, ROWS, W), lambda i: (1, 0, 0))


def shards(left, right, window_a, window_b, row_a, row_b, column_a, column_b, row_live, column_live):
    slab_index = lax.axis_index("slab")
    owner = lax.axis_index("diag")
    first_core = slab_index % 2 == 0
    chip = slab_index // 2
    x, y = chip // 4, chip % 4
    group, member = owner // GROUP, owner % GROUP

    def of_chip(for_first, for_second):
        got = swap_cores(jnp.where(first_core, for_second, for_first))
        return jnp.where(
            first_core,
            jnp.concatenate([for_first, got]),
            jnp.concatenate([got, for_second]),
        )

    def placed(blocks):
        full = jnp.zeros((CHIPS, ROWS, W), jnp.float32)
        for i, block in enumerate(blocks):
            place = (x ^ (i // 4)) * 4 + (y + i % 4) % 4
            full = lax.dynamic_update_slice(full, block[None], (place, 0, 0))
        return full.reshape(W, W)

    places = [(x ^ (i // 4)) * 4 + (y + i % 4) % 4 for i in range(CHIPS)]
    length = row_a.shape[1]
    begin = slab_index * length
    at = [slab_index % 2, row_live[0] - begin, column_live[0] - begin, group, member, chip, y]
    at = jnp.stack(at + places).astype(jnp.int32)

    together = lax.optimization_barrier
    own_factor = of_chip(left[0], right[0])
    own_window = of_chip(window_a[0], window_b[0])
    factor_1 = first_round(own_factor)
    own_corners = [from_member(own_factor[:, EDGE:], d) for d in range(1, GROUP)]
    own_window, factor_1, own_corners = together((own_window, factor_1, own_corners))
    factor_2 = second_round(*factor_1)
    own_pair = jnp.stack([own_window, jnp.concatenate(own_corners, axis=1)])
    pair_1 = first_round(own_pair)
    factor_2, pair_1 = together((factor_2, pair_1))
    factor_3 = lax.ppermute(factor_2[2], "slab", UP)
    pair_2 = second_round(*pair_1)
    factor_3, pair_2 = together((factor_3, pair_2))
    last_window = lax.ppermute(pair_2[0][:1], "slab", CROSS)
    last_corners = lax.ppermute(pair_2[1][1:], "slab", DOWN)
    factor = placed(by_position(own_factor, factor_1, factor_2, factor_3))
    factor_other = swap_cores(factor)
    own_columns = jnp.where(
        first_core,
        lax.dynamic_slice_in_dim(factor, chip * ROWS, ROWS, 1),
        lax.dynamic_slice_in_dim(factor_other, chip * ROWS, ROWS, 1),
    )
    last_window, last_corners, factor, factor_other, own_columns = together(
        (last_window, last_corners, factor, factor_other, own_columns)
    )

    corners, chain, slices = local_kernel(
        chain_body,
        [(OVL, 3 * OVL), (2, OVL, OVL), (3, SLICE, OVL)],
        2 * OVL**3,
        [(3 * ROWS, 3 * OVL), (OVL, OVL)],
        in_specs=[FIRST_PART if i == 6 else SECOND_PART for i in range(CHIPS)],
    )(at, *by_position(own_pair, pair_1, pair_2, last_corners))
    slices = swap_cores(slices)
    prefix, whole = local_kernel(
        prefix_body, [(OVL, OVL), (QUARTER, OVL)], 3 * OVL**3, in_specs=[CORNER]
    )(at, factor, corners, chain)
    factor_other, whole = together((factor_other, whole))
    spans = [from_group(whole, 2), from_group(whole, 1)]
    base_corner, window = local_kernel(
        corner_body,
        [(OVL, OVL), (W, W)],
        OVL * W * (W + OVL),
        in_specs=[EDGE_COLUMNS] * 2 + [FIRST_PART] * CHIPS,
    )(at, factor, factor_other, *by_position(own_pair, pair_1, pair_2, last_window))
    (outgoing,) = local_kernel(
        terms_body,
        [(16, SLICE, OVL)],
        6 * SLICE * OVL * OVL,
        [(2 * GROUP, SLICE, OVL)],
        in_specs=[FIRST_SQUARE],
    )(at, corners, base_corner, slices, chain)
    outgoing, window, spans = together((outgoing, window, spans))
    incoming = lax.all_to_all(outgoing, "diag", split_axis=0, concat_axis=0, tiled=True)

    spans = jnp.stack(spans)
    spans = jnp.concatenate([spans, swap_cores(spans)])
    spans = [spans] + [
        lax.ppermute(spans, "slab", slab_route(lambda x, y: (x, (y - d) % 4))) for d in range(1, 4)
    ]
    (base,) = local_kernel(base_body, [(ROWS, W)], 2 * ROWS * W * W)(
        at, factor, factor_other, window, own_columns
    )
    prefix_other = swap_cores(prefix)
    incoming, base, prefix_other, *spans = together((incoming, base, prefix_other, *spans))

    (shares,) = local_kernel(sum_body, [(CHIPS, 4, SLICE, OVL)], 0)(at, incoming)
    shares, factor, factor_other = together((shares, factor, factor_other))
    ends = lax.all_to_all(
        shares, "slab", split_axis=0, concat_axis=0, tiled=True, axis_index_groups=SAME_CORE
    )
    slabs = local_kernel(slab_body, [row_a.shape[1:]] * 4, 4 * length * W * W)(
        at, factor, factor_other, row_a[0], row_b[0], column_a[0], column_b[0]
    )
    ends, slabs = together((ends, slabs))
    (updated,) = local_kernel(
        final_body,
        [(ROWS, W)],
        6 * OVL**3 + ROWS * OVL * (OVL + W),
        [(4, OVL, OVL)],
        in_specs=[TOP_ROWS] * 2,
    )(at, factor, factor_other, ends, prefix, prefix_other, own_columns[:OVL], base, *spans)
    kept = jnp.where(first_core, updated[: ROWS // 2], updated[ROWS // 2 :])
    sent = jnp.where(first_core, updated[ROWS // 2 :], updated[: ROWS // 2])
    received = swap_cores(sent)
    updated_a = jnp.where(first_core, kept, received)
    updated_b = jnp.where(first_core, received, kept)
    return (updated_a[None], updated_b[None], *(slab[None] for slab in slabs))


def solution(mesh):
    rows = P("diag", "slab", None)
    return jax.shard_map(
        shards,
        mesh=mesh,
        in_specs=(rows,) * 8 + (P("diag"),) * 2,
        out_specs=(rows,) * 6,
        check_vma=False,
    )
```

```python
import jax
import jax.numpy as jnp
from jax import lax
from jax.experimental import pallas as pl
from jax.experimental.pallas import tpu as pltpu
from jax.sharding import PartitionSpec as P

OVL = 256
W = 768
EDGE = W - OVL
ROWS = 96
CHIPS = 8
SLICE = OVL // CHIPS
GROUP = 8

NN = (((1,), (0,)), ((), ()))
TN = (((0,), (0,)), ((), ()))


def slab_route(move):
    return [
        ((x * 4 + y) * 2 + c, (move(x, y)[0] * 4 + move(x, y)[1]) * 2 + c)
        for x in range(2)
        for y in range(4)
        for c in range(2)
    ]


CROSS = slab_route(lambda x, y: (1 - x, y))
UP = slab_route(lambda x, y: (x, (y + 1) % 4))
DOWN = slab_route(lambda x, y: (x, (y + 3) % 4))
OTHER_CORE = [(i, i ^ 1) for i in range(16)]
SAME_CORE = [[i for i in range(16) if i % 2 == c] for c in range(2)]


def swap_cores(block):
    return lax.ppermute(block, "slab", OTHER_CORE)


def from_member(block, d):
    route = [(g * GROUP + (m + d) % GROUP, g * GROUP + m) for g in range(2) for m in range(GROUP)]
    return lax.ppermute(block, "diag", route)


def across(block, route):
    return lax.ppermute(block, "slab", route)


def pieces_body(left_ref, right_ref, out_ref):
    for chip in range(CHIPS):
        out_ref[2 * chip] = left_ref[0]
        out_ref[2 * chip + 1] = right_ref[0]


def corner_to_all(left, right):
    rows = left.shape[1]
    edge = pl.BlockSpec((1, rows, OVL), lambda i: (0, 0, EDGE // OVL))
    pieces = pl.pallas_call(
        pieces_body,
        grid=(1,),
        out_shape=jax.ShapeDtypeStruct((2 * CHIPS, rows, OVL), jnp.float32),
        in_specs=[edge, edge],
        out_specs=pl.BlockSpec((2 * CHIPS, rows, OVL), lambda i: (0, 0, 0)),
    )(left, right)
    pieces = lax.all_to_all(pieces, "slab", split_axis=0, concat_axis=0, tiled=True)
    count = -(-OVL // rows)
    return pieces[:count].reshape(count * rows, OVL)[:OVL]


def split(a):
    high = a.astype(jnp.bfloat16)
    return high, (a - high.astype(jnp.float32)).astype(jnp.bfloat16)


def three(a, b, dims=NN):
    def dot(p, q):
        return lax.dot_general(p, q, dims, preferred_element_type=jnp.float32)

    return dot(a[0], b[0]) + (dot(a[0], b[1]) + dot(a[1], b[0]))


CORE, ROW_LIVE, COLUMN_LIVE, MY_GROUP, MEMBER, CHIP, PLACE = range(7)
SCALARS = pl.BlockSpec(memory_space=pltpu.SMEM)


def block_of(shape):
    return pl.BlockSpec(shape, lambda i: (0,) * len(shape))


def local_kernel(body, shapes, flops, scratch=(), in_specs=()):
    def call(at, *arrays):
        specs = list(in_specs) + [block_of(a.shape) for a in arrays[len(in_specs) :]]
        moved = sum(a.size for a in arrays) * 4
        return pl.pallas_call(
            body,
            grid=(1,),
            out_shape=[jax.ShapeDtypeStruct(shape, jnp.float32) for shape in shapes],
            in_specs=[SCALARS] + specs,
            out_specs=[block_of(shape) for shape in shapes],
            scratch_shapes=[pltpu.VMEM(shape, jnp.float32) for shape in scratch],
            compiler_params=pltpu.CompilerParams(vmem_limit_bytes=56 * 2**20),
            cost_estimate=pl.CostEstimate(flops=6 * flops, bytes_accessed=moved, transcendentals=0),
        )(at, *arrays)

    return call


def product_of(a, b, dims=NN):
    return three(split(a), split(b), dims)


def chip_rows(at_ref):
    return pl.ds(pl.multiple_of(at_ref[CHIP] * SLICE, SLICE), SLICE)


def by_core(at_ref, own_ref, other_ref, run):
    for core in range(2):

        @pl.when(at_ref[CORE] == core)
        def _(core=core):
            run(*((own_ref, other_ref) if core == 0 else (other_ref, own_ref)), core)


def slab_body(at_ref, own_ref, other_ref, ra_ref, rb_ref, ca_ref, cb_ref, *outs):
    length = ra_ref.shape[0]

    def update(factor_ref, sources, targets, live):
        stacked = split(jnp.concatenate([source[...] for source in sources]))
        keep = lax.broadcasted_iota(jnp.int32, (length, OVL), 0) < live
        for t in range(W // OVL):
            columns = pl.ds(t * OVL, OVL)
            new = three(stacked, split(factor_ref[:, columns]))
            for i in range(2):
                targets[i][:, columns] = jnp.where(
                    keep, new[i * length : (i + 1) * length], sources[i][:, columns]
                )

    def run(left_ref, right_ref, core):
        update(left_ref, (ra_ref, rb_ref), outs[:2], at_ref[ROW_LIVE])
        update(right_ref, (ca_ref, cb_ref), outs[2:], at_ref[COLUMN_LIVE])

    by_core(at_ref, own_ref, other_ref, run)


def corner_body(at_ref, own_ref, other_ref, *refs):
    blocks, (corner_ref, window_ref) = refs[:CHIPS], refs[CHIPS:]
    for i in range(CHIPS):
        start = pl.multiple_of(at_ref[PLACE + i] * ROWS, ROWS)
        window_ref[pl.ds(start, ROWS), :] = blocks[i][...]

    def run(left_ref, right_ref, core):
        half = split(product_of(window_ref[...], right_ref[...]))
        left = split(left_ref[...])
        corner_ref[...] = three(half, left, TN) if core == 0 else three(left, half, TN)

    by_core(at_ref, own_ref, other_ref, run)


def slice_into(at_ref, product, out_ref, turned):
    turned[...] = product.T
    out_ref[...] = turned[chip_rows(at_ref), :]


def early_chain_body(at_ref, one, two, three_on, five, six, seven, chain_ref, tail_ref, slices_ref, turned):
    chain_ref[0] = product_of(one[...], two[...])
    chain_ref[1] = product_of(chain_ref[0], three_on[...])
    tail_ref[0] = product_of(five[...], six[...])
    tail_ref[1] = product_of(tail_ref[0], seven[...])
    for t in range(3):
        slice_into(at_ref, one[...] if t == 0 else chain_ref[t - 1], slices_ref.at[t], turned)


def late_chain_body(at_ref, early_ref, tail_ref, early_slices_ref, four, five, chain_ref, slices_ref, turned):
    fourth = product_of(early_ref[1], four[...])
    chain_ref[0] = fourth
    parts = split(fourth)
    chain_ref[1] = three(parts, split(five[...]))
    chain_ref[2] = three(parts, split(tail_ref[0]))
    chain_ref[3] = three(parts, split(tail_ref[1]))
    slices_ref[:3] = early_slices_ref[...]
    for t in range(4):
        slice_into(at_ref, chain_ref[t], slices_ref.at[3 + t], turned)


def terms_body(at_ref, corner_ref, slices_ref, one_ref, early_ref, late_ref, out_ref, reach):
    corner = split(corner_ref[...])
    reach[:GROUP] = jnp.zeros((GROUP, SLICE, OVL), jnp.float32)
    reach[GROUP] = corner_ref[chip_rows(at_ref), :]
    near = product_of(slices_ref[...].reshape((GROUP - 1) * SLICE, OVL), corner_ref[...])
    for t in range(GROUP - 1):
        chain = one_ref[...] if t == 0 else early_ref[t - 1] if t < 3 else late_ref[t - 3]
        reach[GROUP + 1 + t] = product_of(near[t * SLICE : (t + 1) * SLICE], chain)
    group, member = at_ref[MY_GROUP], at_ref[MEMBER]
    for target in range(16):
        g, m = target // GROUP, target % GROUP
        place = jnp.where(
            group == g, GROUP + m - 1 - member, jnp.where(group < g, 2 * GROUP - 1 - member, 0)
        )
        out_ref[target] = reach[place]


def prefix_body(at_ref, one, two, three_on, four, seven, tail_ref, six, out_ref):
    member = at_ref[MEMBER]
    row = lax.broadcasted_iota(jnp.int32, (OVL, OVL), 0)
    column = lax.broadcasted_iota(jnp.int32, (OVL, OVL), 1)
    out_ref[...] = jnp.where(row == column, 1.0, 0.0)

    @pl.when(member == 1)
    def _():
        out_ref[...] = seven[...]

    @pl.when(member == 2)
    def _():
        out_ref[...] = product_of(six[...], seven[...])

    @pl.when(member >= 3)
    def _():
        out_ref[...] = tail_ref[1]

    for least, ref in ((4, four), (5, three_on), (6, two), (7, one)):

        @pl.when(member >= least)
        def _(ref=ref):
            out_ref[...] = product_of(ref[...], out_ref[...])


def sum_body(at_ref, in_ref, out_ref):
    group = at_ref[MY_GROUP]
    low = in_ref[0]
    high = in_ref[GROUP]
    for m in range(1, GROUP):
        low = low + in_ref[m]
        high = high + in_ref[GROUP + m]
    entering = jnp.where(group == 0, 0.0, low)
    within = jnp.where(group == 0, low, high)
    for chip in range(CHIPS):
        out_ref[chip, 0] = entering
        out_ref[chip, 1] = within


def base_body(at_ref, own_ref, other_ref, window_ref, columns_ref, base_ref):
    def run(left_ref, right_ref, core):
        base_ref[...] = product_of(
            product_of(columns_ref[...], window_ref[...], TN), right_ref[...]
        )

    by_core(at_ref, own_ref, other_ref, run)


def final_body(
    at_ref, own_ref, other_ref, ends_ref, prefix_ref, prefix_other_ref, columns_ref, base_ref, out_ref
):
    entering = ends_ref[:, 0].reshape(OVL, OVL)
    within = ends_ref[:, 1].reshape(OVL, OVL)
    step = product_of(entering, prefix_ref[...] * 2.0**-48)
    carry = within + product_of(prefix_other_ref[...], step, TN) * 2.0**48

    def run(left_ref, right_ref, core):
        turned = (((0,), (1,)), ((), ())) if core == 0 else TN
        part = product_of(columns_ref[...], carry, turned)
        out_ref[...] = base_ref[...] + product_of(part, right_ref[...])

    by_core(at_ref, own_ref, other_ref, run)


EDGE_COLUMNS = pl.BlockSpec((W, OVL), lambda i: (0, EDGE // OVL))
TOP_ROWS = pl.BlockSpec((OVL, W), lambda i: (0, 0))


def shards(left, right, window_a, window_b, row_a, row_b, column_a, column_b, row_live, column_live):
    slab_index = lax.axis_index("slab")
    owner = lax.axis_index("diag")
    first_core = slab_index % 2 == 0
    chip = slab_index // 2
    x, y = chip // 4, chip % 4
    group, member = owner // GROUP, owner % GROUP

    def of_chip(for_first, for_second):
        got = swap_cores(jnp.where(first_core, for_second, for_first))
        return jnp.where(
            first_core,
            jnp.concatenate([for_first, got]),
            jnp.concatenate([got, for_second]),
        )

    def placed(blocks):
        full = jnp.zeros((CHIPS, ROWS, W), jnp.float32)
        for i, block in enumerate(blocks):
            place = (x ^ (i // 4)) * 4 + (y + i % 4) % 4
            full = lax.dynamic_update_slice(full, block[None], (place, 0, 0))
        return full.reshape(W, W)

    places = [(x ^ (i // 4)) * 4 + (y + i % 4) % 4 for i in range(CHIPS)]
    length = row_a.shape[1]
    begin = slab_index * length
    at = [slab_index % 2, row_live[0] - begin, column_live[0] - begin, group, member, chip]
    at = jnp.stack(at + places).astype(jnp.int32)

    together = lax.optimization_barrier
    own_factor = of_chip(left[0], right[0])
    own_window = of_chip(window_a[0], window_b[0])
    corner = corner_to_all(left, right)
    cross, below, above = (across(own_factor, route) for route in (CROSS, UP, DOWN))
    corner, own_window, cross, below, above = together((corner, own_window, cross, below, above))
    far, cross_above = across(above, DOWN), across(above, CROSS)
    cross_below = across(cross, UP)
    up_1, down_1 = from_member(corner, 1), from_member(corner, -1)
    own_window, far, cross_above, cross_below, up_1, down_1 = together(
        (own_window, far, cross_above, cross_below, up_1, down_1)
    )
    cross_far = across(cross_below, UP)
    up_2, down_2 = from_member(up_1, 1), from_member(down_1, -1)
    w_below, w_above = across(own_window, UP), across(own_window, DOWN)
    cross_far, up_2, down_2, w_below, w_above = together(
        (cross_far, up_2, down_2, w_below, w_above)
    )
    up_3, down_3 = from_member(up_2, 1), from_member(down_2, -1)
    w_far, w_cross = across(w_above, DOWN), across(own_window, CROSS)
    factor = placed([own_factor, above, far, below, cross, cross_above, cross_far, cross_below])
    factor_other = swap_cores(factor)
    up_3, down_3, w_far, w_cross, factor, factor_other = together(
        (up_3, down_3, w_far, w_cross, factor, factor_other)
    )
    up_4 = from_member(up_3, 1)
    w_cross_above, w_cross_below = across(w_cross, DOWN), across(w_cross, UP)
    w_cross_far = across(w_far, CROSS)
    square = (OVL, OVL)
    early, tail, early_slices = local_kernel(
        early_chain_body, [(2, *square), (2, *square), (3, SLICE, OVL)], 4 * OVL**3, [square]
    )(at, up_1, up_2, up_3, down_3, down_2, down_1)
    own_columns = jnp.where(
        first_core,
        lax.dynamic_slice_in_dim(factor, chip * ROWS, ROWS, 1),
        lax.dynamic_slice_in_dim(factor_other, chip * ROWS, ROWS, 1),
    )
    up_4, w_cross_above, w_cross_below, w_cross_far, early, tail, early_slices, own_columns = together(
        (up_4, w_cross_above, w_cross_below, w_cross_far, early, tail, early_slices, own_columns)
    )
    late, slices = local_kernel(
        late_chain_body, [(4, *square), (7, SLICE, OVL)], 4 * OVL**3, [square]
    )(at, early, tail, early_slices, up_4, down_3)
    factor_other, slices = together((factor_other, slices))
    slices = swap_cores(slices)
    base_corner, window = local_kernel(
        corner_body, [square, (W, W)], OVL * W * (W + OVL), in_specs=[EDGE_COLUMNS] * 2
    )(
        at, factor, factor_other,
        own_window, w_above, w_far, w_below, w_cross, w_cross_above, w_cross_far, w_cross_below,
    )
    (outgoing,) = local_kernel(
        terms_body, [(16, SLICE, OVL)], 14 * SLICE * OVL * OVL, [(2 * GROUP, SLICE, OVL)]
    )(at, base_corner, slices, up_1, early, late)
    outgoing, window, tail = together((outgoing, window, tail))
    incoming = lax.all_to_all(outgoing, "diag", split_axis=0, concat_axis=0, tiled=True)

    (prefix,) = local_kernel(prefix_body, [square], 4 * OVL**3)(
        at, up_1, up_2, up_3, up_4, down_1, tail, down_2
    )
    prefix_other = swap_cores(prefix)
    (base,) = local_kernel(base_body, [(ROWS, W)], 2 * ROWS * W * W)(
        at, factor, factor_other, window, own_columns
    )
    slabs = local_kernel(slab_body, [row_a.shape[1:]] * 4, 4 * length * W * W)(
        at, factor, factor_other, row_a[0], row_b[0], column_a[0], column_b[0]
    )
    incoming, base, prefix_other, slabs = together((incoming, base, prefix_other, slabs))
    (shares,) = local_kernel(sum_body, [(CHIPS, 2, SLICE, OVL)], 0)(at, incoming)
    ends = lax.all_to_all(
        shares, "slab", split_axis=0, concat_axis=0, tiled=True, axis_index_groups=SAME_CORE
    )
    (updated,) = local_kernel(
        final_body,
        [(ROWS, W)],
        2 * OVL**3 + ROWS * OVL * (OVL + W),
        in_specs=[TOP_ROWS] * 2,
    )(at, factor, factor_other, ends, prefix, prefix_other, own_columns[:OVL], base)
    kept = jnp.where(first_core, updated[: ROWS // 2], updated[ROWS // 2 :])
    sent = jnp.where(first_core, updated[ROWS // 2 :], updated[: ROWS // 2])
    received = swap_cores(sent)
    updated_a = jnp.where(first_core, kept, received)
    updated_b = jnp.where(first_core, received, kept)
    return (updated_a[None], updated_b[None], *(slab[None] for slab in slabs))


def solution(mesh):
    rows = P("diag", "slab", None)
    return jax.shard_map(
        shards,
        mesh=mesh,
        in_specs=(rows,) * 8 + (P("diag"),) * 2,
        out_specs=(rows,) * 6,
        check_vma=False,
    )
```

```python
import functools

import jax
import jax.numpy as jnp
from jax import lax
from jax.experimental import pallas as pl
from jax.experimental.pallas import tpu as pltpu
from jax.sharding import PartitionSpec as P

OVL = 256
W = 768
EDGE = W - OVL
ROWS = 96
CHIPS = 8
SLICE = OVL // CHIPS
GROUP = 8

NN = (((1,), (0,)), ((), ()))
TN = (((0,), (0,)), ((), ()))


def slab_route(move):
    return [
        ((x * 4 + y) * 2 + c, (move(x, y)[0] * 4 + move(x, y)[1]) * 2 + c)
        for x in range(2)
        for y in range(4)
        for c in range(2)
    ]


CROSS = slab_route(lambda x, y: (1 - x, y))
UP = slab_route(lambda x, y: (x, (y + 1) % 4))
DOWN = slab_route(lambda x, y: (x, (y + 3) % 4))
OTHER_CORE = [(i, i ^ 1) for i in range(16)]
SAME_CORE = [[i for i in range(16) if i % 2 == c] for c in range(2)]


def swap_cores(block):
    return lax.ppermute(block, "slab", OTHER_CORE)


def from_member(block, d):
    route = [(g * GROUP + (m + d) % GROUP, g * GROUP + m) for g in range(2) for m in range(GROUP)]
    return lax.ppermute(block, "diag", route)


def across(block, route):
    return lax.ppermute(block, "slab", route)


def pieces_body(left_ref, right_ref, out_ref):
    for chip in range(CHIPS):
        out_ref[2 * chip] = left_ref[0]
        out_ref[2 * chip + 1] = right_ref[0]


def corner_to_all(left, right):
    rows = left.shape[1]
    edge = pl.BlockSpec((1, rows, OVL), lambda i: (0, 0, EDGE // OVL))
    pieces = pl.pallas_call(
        pieces_body,
        grid=(1,),
        out_shape=jax.ShapeDtypeStruct((2 * CHIPS, rows, OVL), jnp.float32),
        in_specs=[edge, edge],
        out_specs=pl.BlockSpec((2 * CHIPS, rows, OVL), lambda i: (0, 0, 0)),
    )(left, right)
    pieces = lax.all_to_all(pieces, "slab", split_axis=0, concat_axis=0, tiled=True)
    count = -(-OVL // rows)
    return pieces[:count].reshape(count * rows, OVL)[:OVL]


def split(a):
    high = a.astype(jnp.bfloat16)
    return high, (a - high.astype(jnp.float32)).astype(jnp.bfloat16)


def three(a, b, dims=NN):
    def dot(p, q):
        return lax.dot_general(p, q, dims, preferred_element_type=jnp.float32)

    return dot(a[0], b[0]) + (dot(a[0], b[1]) + dot(a[1], b[0]))


CORE, ROW_LIVE, COLUMN_LIVE, MY_GROUP, MEMBER, CHIP, PLACE = range(7)
SCALARS = pl.BlockSpec(memory_space=pltpu.SMEM)


def block_of(shape):
    return pl.BlockSpec(shape, lambda i: (0,) * len(shape))


def local_kernel(body, shapes, flops, scratch=(), in_specs=(), mib=16):
    def call(at, *arrays):
        specs = list(in_specs) + [block_of(a.shape) for a in arrays[len(in_specs) :]]
        moved = sum(a.size for a in arrays) * 4
        return pl.pallas_call(
            body,
            grid=(1,),
            out_shape=[jax.ShapeDtypeStruct(shape, jnp.float32) for shape in shapes],
            in_specs=[SCALARS] + specs,
            out_specs=[block_of(shape) for shape in shapes],
            scratch_shapes=[pltpu.VMEM(shape, jnp.float32) for shape in scratch],
            compiler_params=pltpu.CompilerParams(vmem_limit_bytes=mib * 2**20),
            cost_estimate=pl.CostEstimate(flops=6 * flops, bytes_accessed=moved, transcendentals=0),
        )(at, *arrays)

    return call


def product_of(a, b, dims=NN):
    return three(split(a), split(b), dims)


def chip_rows(at_ref):
    return pl.ds(pl.multiple_of(at_ref[CHIP] * SLICE, SLICE), SLICE)


def by_core(at_ref, own_ref, other_ref, run):
    for core in range(2):

        @pl.when(at_ref[CORE] == core)
        def _(core=core):
            run(*((own_ref, other_ref) if core == 0 else (other_ref, own_ref)), core)


def slab_body(at_ref, own_ref, other_ref, ra_ref, rb_ref, ca_ref, cb_ref, *outs):
    length = ra_ref.shape[0]

    def update(factor_ref, sources, targets, live):
        stacked = split(jnp.concatenate([source[...] for source in sources]))
        keep = lax.broadcasted_iota(jnp.int32, (length, OVL), 0) < live
        for t in range(W // OVL):
            columns = pl.ds(t * OVL, OVL)
            new = three(stacked, split(factor_ref[:, columns]))
            for i in range(2):
                targets[i][:, columns] = jnp.where(
                    keep, new[i * length : (i + 1) * length], sources[i][:, columns]
                )

    def run(left_ref, right_ref, core):
        update(left_ref, (ra_ref, rb_ref), outs[:2], at_ref[ROW_LIVE])
        update(right_ref, (ca_ref, cb_ref), outs[2:], at_ref[COLUMN_LIVE])

    by_core(at_ref, own_ref, other_ref, run)


def corner_body(positions, at_ref, own_ref, other_ref, *refs):
    blocks, (*before, out_ref, window, factor) = refs[: len(positions)], refs[len(positions) :]

    def run(left_ref, right_ref, core):
        for j, i in enumerate(positions):
            rows = pl.ds(j * ROWS, ROWS)
            start = pl.multiple_of(at_ref[PLACE + i] * ROWS, ROWS)
            window[rows, :] = blocks[j][...]
            factor[rows, :] = left_ref[pl.ds(start, ROWS), :]
        half = split(product_of(window[...], right_ref[...]))
        left = split(factor[...])
        part = three(half, left, TN) if core == 0 else three(left, half, TN)
        out_ref[...] = part + before[0][...] if before else part

    by_core(at_ref, own_ref, other_ref, run)


def corner_part(positions, at, factor, factor_other, blocks, *before):
    rows = len(positions) * ROWS
    return local_kernel(
        functools.partial(corner_body, positions),
        [(OVL, OVL)],
        rows * OVL * (W + OVL),
        [(rows, W), (rows, OVL)],
        in_specs=[EDGE_COLUMNS] * 2,
        mib=20,
    )(at, factor, factor_other, *(blocks[i] for i in positions), *before)[0]


def slice_into(at_ref, product, out_ref, turned):
    turned[...] = product.T
    out_ref[...] = turned[chip_rows(at_ref), :]


def early_chain_body(
    at_ref, one, two, three_on, five, six, seven, chain_ref, tail_ref, slices_ref, tail_slices_ref, turned
):
    chain_ref[0] = product_of(one[...], two[...])
    chain_ref[1] = product_of(chain_ref[0], three_on[...])
    tail_ref[0] = product_of(five[...], six[...])
    tail_ref[1] = product_of(tail_ref[0], seven[...])
    for t in range(3):
        slice_into(at_ref, one[...] if t == 0 else chain_ref[t - 1], slices_ref.at[t], turned)
        slice_into(at_ref, five[...] if t == 0 else tail_ref[t - 1], tail_slices_ref.at[t], turned)


def late_chain_body(at_ref, early_ref, early_slices_ref, tail_slices_ref, four, chain_ref, slices_ref, turned):
    chain_ref[...] = product_of(early_ref[1], four[...])
    slices_ref[:3] = early_slices_ref[...]
    slice_into(at_ref, chain_ref[...], slices_ref.at[3], turned)
    tails = product_of(tail_slices_ref[...].reshape(3 * SLICE, OVL), turned[...])
    slices_ref[4:] = tails.reshape(3, SLICE, OVL)


def terms_body(at_ref, corner_ref, slices_ref, one_ref, early_ref, four_ref, five_ref, tail_ref, out_ref, reach):
    reach[:GROUP] = jnp.zeros((GROUP, SLICE, OVL), jnp.float32)
    reach[GROUP] = corner_ref[chip_rows(at_ref), :]
    near = product_of(slices_ref[...].reshape((GROUP - 1) * SLICE, OVL), corner_ref[...])
    for t in range(3):
        chain = one_ref[...] if t == 0 else early_ref[t - 1]
        reach[GROUP + 1 + t] = product_of(near[t * SLICE : (t + 1) * SLICE], chain)
    far = product_of(near[3 * SLICE :], four_ref[...])
    reach[GROUP + 4] = far[:SLICE]
    for t in range(3):
        tail = five_ref[...] if t == 0 else tail_ref[t - 1]
        reach[GROUP + 5 + t] = product_of(far[(t + 1) * SLICE : (t + 2) * SLICE], tail)
    group, member = at_ref[MY_GROUP], at_ref[MEMBER]
    for target in range(16):
        g, m = target // GROUP, target % GROUP
        place = jnp.where(
            group == g, GROUP + m - 1 - member, jnp.where(group < g, 2 * GROUP - 1 - member, 0)
        )
        out_ref[target] = reach[place]


def prefix_body(at_ref, one, two, three_on, four, seven, tail_ref, six, out_ref):
    member = at_ref[MEMBER]
    row = lax.broadcasted_iota(jnp.int32, (OVL, OVL), 0)
    column = lax.broadcasted_iota(jnp.int32, (OVL, OVL), 1)
    out_ref[...] = jnp.where(row == column, 1.0, 0.0)

    @pl.when(member == 1)
    def _():
        out_ref[...] = seven[...]

    @pl.when(member == 2)
    def _():
        out_ref[...] = product_of(six[...], seven[...])

    @pl.when(member >= 3)
    def _():
        out_ref[...] = tail_ref[1]

    for least, ref in ((4, four), (5, three_on), (6, two), (7, one)):

        @pl.when(member >= least)
        def _(ref=ref):
            out_ref[...] = product_of(ref[...], out_ref[...])


def sum_body(at_ref, in_ref, out_ref):
    group = at_ref[MY_GROUP]
    low = in_ref[0]
    high = in_ref[GROUP]
    for m in range(1, GROUP):
        low = low + in_ref[m]
        high = high + in_ref[GROUP + m]
    entering = jnp.where(group == 0, 0.0, low)
    within = jnp.where(group == 0, low, high)
    for chip in range(CHIPS):
        out_ref[chip, 0] = entering
        out_ref[chip, 1] = within


def base_body(at_ref, own_ref, other_ref, columns_ref, *refs):
    blocks, (base_ref, window) = refs[:CHIPS], refs[CHIPS:]
    for i in range(CHIPS):
        start = pl.multiple_of(at_ref[PLACE + i] * ROWS, ROWS)
        window[pl.ds(start, ROWS), :] = blocks[i][...]
    half = product_of(columns_ref[...], window[...], TN)

    def run(left_ref, right_ref, core):
        base_ref[...] = product_of(half, right_ref[...])

    by_core(at_ref, own_ref, other_ref, run)


def final_body(
    at_ref, own_ref, other_ref, ends_ref, prefix_ref, prefix_other_ref, columns_ref, base_ref,
    kept_ref, sent_ref,
):
    entering = ends_ref[:, 0].reshape(OVL, OVL)
    within = ends_ref[:, 1].reshape(OVL, OVL)
    step = product_of(entering, prefix_ref[...] * 2.0**-48)
    carry = within + product_of(prefix_other_ref[...], step, TN) * 2.0**48

    def run(left_ref, right_ref, core):
        turned = (((0,), (1,)), ((), ())) if core == 0 else TN
        part = product_of(columns_ref[...], carry, turned)
        updated = base_ref[...] + product_of(part, right_ref[...])
        rows = ROWS // 2
        kept_ref[...] = updated[core * rows : (core + 1) * rows]
        sent_ref[...] = updated[(1 - core) * rows : (2 - core) * rows]

    by_core(at_ref, own_ref, other_ref, run)


EDGE_COLUMNS = pl.BlockSpec((W, OVL), lambda i: (0, EDGE // OVL))
TOP_ROWS = pl.BlockSpec((OVL, W), lambda i: (0, 0))


def shards(left, right, window_a, window_b, row_a, row_b, column_a, column_b, row_live, column_live):
    slab_index = lax.axis_index("slab")
    owner = lax.axis_index("diag")
    first_core = slab_index % 2 == 0
    chip = slab_index // 2
    x, y = chip // 4, chip % 4
    group, member = owner // GROUP, owner % GROUP

    def of_chip(for_first, for_second):
        got = swap_cores(jnp.where(first_core, for_second, for_first))
        return jnp.where(
            first_core,
            jnp.concatenate([for_first, got]),
            jnp.concatenate([got, for_second]),
        )

    def placed(blocks):
        full = jnp.zeros((CHIPS, ROWS, W), jnp.float32)
        for i, block in enumerate(blocks):
            place = (x ^ (i // 4)) * 4 + (y + i % 4) % 4
            full = lax.dynamic_update_slice(full, block[None], (place, 0, 0))
        return full.reshape(W, W)

    places = [(x ^ (i // 4)) * 4 + (y + i % 4) % 4 for i in range(CHIPS)]
    length = row_a.shape[1]
    begin = slab_index * length
    at = [slab_index % 2, row_live[0] - begin, column_live[0] - begin, group, member, chip]
    at = jnp.stack(at + places).astype(jnp.int32)

    together = lax.optimization_barrier
    own_factor = of_chip(left[0], right[0])
    own_window = of_chip(window_a[0], window_b[0])
    corner = corner_to_all(left, right)
    cross, below, above = (across(own_factor, route) for route in (CROSS, UP, DOWN))
    corner, own_window, cross, below, above = together((corner, own_window, cross, below, above))
    far, cross_above = across(above, DOWN), across(above, CROSS)
    cross_below = across(cross, UP)
    up_1, down_1 = from_member(corner, 1), from_member(corner, -1)
    own_window, far, cross_above, cross_below, up_1, down_1 = together(
        (own_window, far, cross_above, cross_below, up_1, down_1)
    )
    cross_far = across(far, CROSS)
    up_2, down_2 = from_member(up_1, 1), from_member(down_1, -1)
    w_below, w_above = across(own_window, UP), across(own_window, DOWN)
    cross_far, up_2, down_2, w_below, w_above = together(
        (cross_far, up_2, down_2, w_below, w_above)
    )
    up_3, down_3 = from_member(up_2, 1), from_member(down_2, -1)
    w_far, w_cross = across(w_above, DOWN), across(own_window, CROSS)
    factor = placed([own_factor, above, far, below, cross, cross_above, cross_far, cross_below])
    factor_other = swap_cores(factor)
    up_3, down_3, w_far, w_cross, factor, factor_other = together(
        (up_3, down_3, w_far, w_cross, factor, factor_other)
    )
    up_4 = from_member(up_3, 1)
    w_cross_above, w_cross_below = across(w_cross, DOWN), across(w_cross, UP)
    w_cross_far = across(w_far, CROSS)
    square = (OVL, OVL)
    early, tail, early_slices, tail_slices = local_kernel(
        early_chain_body,
        [(2, *square), (2, *square), (3, SLICE, OVL), (3, SLICE, OVL)],
        4 * OVL**3,
        [square],
    )(at, up_1, up_2, up_3, down_3, down_2, down_1)
    blocks = [own_window, w_above, w_far, w_below, w_cross]
    part = corner_part((0, 1, 2, 3, 4), at, factor, factor_other, blocks)
    up_4, w_cross_above, w_cross_far, w_cross_below, early, tail, early_slices, tail_slices, part = together(
        (up_4, w_cross_above, w_cross_far, w_cross_below, early, tail, early_slices, tail_slices, part)
    )
    blocks += [w_cross_above, w_cross_far, w_cross_below]
    fourth, slices = local_kernel(
        late_chain_body, [square, (7, SLICE, OVL)], 2 * OVL**3, [square]
    )(at, early, early_slices, tail_slices, up_4)
    part, slices = together((part, slices))
    slices = swap_cores(slices)
    base_corner = corner_part((5, 6, 7), at, factor, factor_other, blocks, part)
    (outgoing,) = local_kernel(
        terms_body, [(16, SLICE, OVL)], 14 * SLICE * OVL * OVL, [(2 * GROUP, SLICE, OVL)]
    )(at, base_corner, slices, up_1, early, fourth, down_3, tail)
    outgoing, factor, factor_other, tail = together((outgoing, factor, factor_other, tail))
    incoming = lax.all_to_all(outgoing, "diag", split_axis=0, concat_axis=0, tiled=True)

    (prefix,) = local_kernel(prefix_body, [square], 4 * OVL**3)(
        at, up_1, up_2, up_3, up_4, down_1, tail, down_2
    )
    prefix_other = swap_cores(prefix)
    own_columns = jnp.where(
        first_core,
        lax.dynamic_slice_in_dim(factor, chip * ROWS, ROWS, 1),
        lax.dynamic_slice_in_dim(factor_other, chip * ROWS, ROWS, 1),
    )
    (base,) = local_kernel(base_body, [(ROWS, W)], 2 * ROWS * W * W, [(W, W)], mib=32)(
        at, factor, factor_other, own_columns, *blocks
    )
    slabs = local_kernel(slab_body, [row_a.shape[1:]] * 4, 4 * length * W * W, mib=32)(
        at, factor, factor_other, row_a[0], row_b[0], column_a[0], column_b[0]
    )
    top_columns = own_columns[:OVL]
    incoming, base, prefix_other, top_columns, slabs = together(
        (incoming, base, prefix_other, top_columns, slabs)
    )
    (shares,) = local_kernel(sum_body, [(CHIPS, 2, SLICE, OVL)], 0)(at, incoming)
    ends = lax.all_to_all(
        shares, "slab", split_axis=0, concat_axis=0, tiled=True, axis_index_groups=SAME_CORE
    )
    kept, sent = local_kernel(
        final_body,
        [(ROWS // 2, W)] * 2,
        2 * OVL**3 + ROWS * OVL * (OVL + W),
        in_specs=[TOP_ROWS] * 2,
    )(at, factor, factor_other, ends, prefix, prefix_other, top_columns, base)
    received = swap_cores(sent)
    updated_a = jnp.where(first_core, kept, received)
    updated_b = jnp.where(first_core, received, kept)
    return (updated_a[None], updated_b[None], *(slab[None] for slab in slabs))


def solution(mesh):
    rows = P("diag", "slab", None)
    return jax.shard_map(
        shards,
        mesh=mesh,
        in_specs=(rows,) * 8 + (P("diag"),) * 2,
        out_specs=(rows,) * 6,
        check_vma=False,
    )
```

```python
import functools

import jax
import jax.numpy as jnp
from jax import lax
from jax.experimental import pallas as pl
from jax.experimental.pallas import tpu as pltpu
from jax.sharding import PartitionSpec as P

OVL = 256
W = 768
EDGE = W - OVL
ROWS = 96
CHIPS = 8
SLICE = OVL // CHIPS
GROUP = 8

NN = (((1,), (0,)), ((), ()))
TN = (((0,), (0,)), ((), ()))


def slab_route(move):
    return [
        ((x * 4 + y) * 2 + c, (move(x, y)[0] * 4 + move(x, y)[1]) * 2 + c)
        for x in range(2)
        for y in range(4)
        for c in range(2)
    ]


CROSS = slab_route(lambda x, y: (1 - x, y))
UP = slab_route(lambda x, y: (x, (y + 1) % 4))
DOWN = slab_route(lambda x, y: (x, (y + 3) % 4))
OTHER_CORE = [(i, i ^ 1) for i in range(16)]
SAME_CORE = [[i for i in range(16) if i % 2 == c] for c in range(2)]


def swap_cores(block):
    return lax.ppermute(block, "slab", OTHER_CORE)


def from_member(block, d):
    route = [(g * GROUP + (m + d) % GROUP, g * GROUP + m) for g in range(2) for m in range(GROUP)]
    return lax.ppermute(block, "diag", route)


def across(block, route):
    return lax.ppermute(block, "slab", route)


def pieces_body(left_ref, right_ref, out_ref):
    for chip in range(CHIPS):
        out_ref[2 * chip] = left_ref[0]
        out_ref[2 * chip + 1] = right_ref[0]


def corner_to_all(left, right):
    rows = left.shape[1]
    edge = pl.BlockSpec((1, rows, OVL), lambda i: (0, 0, EDGE // OVL))
    pieces = pl.pallas_call(
        pieces_body,
        grid=(1,),
        out_shape=jax.ShapeDtypeStruct((2 * CHIPS, rows, OVL), jnp.float32),
        in_specs=[edge, edge],
        out_specs=pl.BlockSpec((2 * CHIPS, rows, OVL), lambda i: (0, 0, 0)),
    )(left, right)
    pieces = lax.all_to_all(pieces, "slab", split_axis=0, concat_axis=0, tiled=True)
    count = -(-OVL // rows)
    return pieces[:count].reshape(count * rows, OVL)[:OVL]


def split(a):
    high = a.astype(jnp.bfloat16)
    return high, (a - high.astype(jnp.float32)).astype(jnp.bfloat16)


def three(a, b, dims=NN):
    def dot(p, q):
        return lax.dot_general(p, q, dims, preferred_element_type=jnp.float32)

    return dot(a[0], b[0]) + (dot(a[0], b[1]) + dot(a[1], b[0]))


CORE, ROW_LIVE, COLUMN_LIVE, MY_GROUP, MEMBER, CHIP, PLACE = range(7)
SCALARS = pl.BlockSpec(memory_space=pltpu.SMEM)


def block_of(shape):
    return pl.BlockSpec(shape, lambda i: (0,) * len(shape))


def local_kernel(body, shapes, flops, scratch=(), in_specs=(), mib=16):
    def call(at, *arrays):
        specs = list(in_specs) + [block_of(a.shape) for a in arrays[len(in_specs) :]]
        moved = sum(a.size for a in arrays) * 4
        return pl.pallas_call(
            body,
            grid=(1,),
            out_shape=[jax.ShapeDtypeStruct(shape, jnp.float32) for shape in shapes],
            in_specs=[SCALARS] + specs,
            out_specs=[block_of(shape) for shape in shapes],
            scratch_shapes=[pltpu.VMEM(shape, jnp.float32) for shape in scratch],
            compiler_params=pltpu.CompilerParams(vmem_limit_bytes=mib * 2**20),
            cost_estimate=pl.CostEstimate(flops=6 * flops, bytes_accessed=moved, transcendentals=0),
        )(at, *arrays)

    return call


def product_of(a, b, dims=NN):
    return three(split(a), split(b), dims)


def chip_rows(at_ref):
    return pl.ds(pl.multiple_of(at_ref[CHIP] * SLICE, SLICE), SLICE)


def by_core(at_ref, own_ref, other_ref, run):
    for core in range(2):

        @pl.when(at_ref[CORE] == core)
        def _(core=core):
            run(*((own_ref, other_ref) if core == 0 else (other_ref, own_ref)), core)


def slab_body(at_ref, own_ref, other_ref, ra_ref, rb_ref, ca_ref, cb_ref, *outs):
    length = ra_ref.shape[0]

    def update(factor_ref, sources, targets, live):
        stacked = split(jnp.concatenate([source[...] for source in sources]))
        keep = lax.broadcasted_iota(jnp.int32, (length, OVL), 0) < live
        for t in range(W // OVL):
            columns = pl.ds(t * OVL, OVL)
            new = three(stacked, split(factor_ref[:, columns]))
            for i in range(2):
                targets[i][:, columns] = jnp.where(
                    keep, new[i * length : (i + 1) * length], sources[i][:, columns]
                )

    def run(left_ref, right_ref, core):
        update(left_ref, (ra_ref, rb_ref), outs[:2], at_ref[ROW_LIVE])
        update(right_ref, (ca_ref, cb_ref), outs[2:], at_ref[COLUMN_LIVE])

    by_core(at_ref, own_ref, other_ref, run)


def corner_body(positions, at_ref, own_ref, other_ref, *refs):
    blocks, (*before, out_ref, window, factor) = refs[: len(positions)], refs[len(positions) :]

    def run(left_ref, right_ref, core):
        for j, i in enumerate(positions):
            rows = pl.ds(j * ROWS, ROWS)
            start = pl.multiple_of(at_ref[PLACE + i] * ROWS, ROWS)
            window[rows, :] = blocks[j][...]
            factor[rows, :] = left_ref[pl.ds(start, ROWS), :]
        half = split(product_of(window[...], right_ref[...]))
        left = split(factor[...])
        part = three(half, left, TN) if core == 0 else three(left, half, TN)
        out_ref[...] = part + before[0][...] if before else part

    by_core(at_ref, own_ref, other_ref, run)


def corner_part(positions, at, factor, factor_other, blocks, *before):
    rows = len(positions) * ROWS
    return local_kernel(
        functools.partial(corner_body, positions),
        [(OVL, OVL)],
        rows * OVL * (W + OVL),
        [(rows, W), (rows, OVL)],
        in_specs=[EDGE_COLUMNS] * 2,
        mib=16 if before else 52,
    )(at, factor, factor_other, *(blocks[i] for i in positions), *before)[0]


def slice_into(at_ref, product, out_ref, turned):
    turned[...] = product.T
    out_ref[...] = turned[chip_rows(at_ref), :]


def early_chain_body(
    at_ref, one, two, three_on, five, six, seven, chain_ref, tail_ref, slices_ref, tail_slices_ref, turned
):
    chain_ref[0] = product_of(one[...], two[...])
    chain_ref[1] = product_of(chain_ref[0], three_on[...])
    tail_ref[0] = product_of(five[...], six[...])
    tail_ref[1] = product_of(tail_ref[0], seven[...])
    for t in range(3):
        slice_into(at_ref, one[...] if t == 0 else chain_ref[t - 1], slices_ref.at[t], turned)
        slice_into(at_ref, five[...] if t == 0 else tail_ref[t - 1], tail_slices_ref.at[t], turned)


def late_chain_body(at_ref, early_ref, early_slices_ref, tail_slices_ref, four, chain_ref, slices_ref, turned):
    chain_ref[...] = product_of(early_ref[1], four[...])
    slices_ref[:3] = early_slices_ref[...]
    slice_into(at_ref, chain_ref[...], slices_ref.at[3], turned)
    tails = product_of(tail_slices_ref[...].reshape(3 * SLICE, OVL), turned[...])
    slices_ref[4:] = tails.reshape(3, SLICE, OVL)


def terms_body(at_ref, corner_ref, slices_ref, one_ref, early_ref, four_ref, five_ref, tail_ref, out_ref, reach):
    reach[:GROUP] = jnp.zeros((GROUP, SLICE, OVL), jnp.float32)
    reach[GROUP] = corner_ref[chip_rows(at_ref), :]
    near = product_of(slices_ref[...].reshape((GROUP - 1) * SLICE, OVL), corner_ref[...])
    for t in range(3):
        chain = one_ref[...] if t == 0 else early_ref[t - 1]
        reach[GROUP + 1 + t] = product_of(near[t * SLICE : (t + 1) * SLICE], chain)
    far = product_of(near[3 * SLICE :], four_ref[...])
    reach[GROUP + 4] = far[:SLICE]
    for t in range(3):
        tail = five_ref[...] if t == 0 else tail_ref[t - 1]
        reach[GROUP + 5 + t] = product_of(far[(t + 1) * SLICE : (t + 2) * SLICE], tail)
    group, member = at_ref[MY_GROUP], at_ref[MEMBER]
    for target in range(16):
        g, m = target // GROUP, target % GROUP
        place = jnp.where(
            group == g, GROUP + m - 1 - member, jnp.where(group < g, 2 * GROUP - 1 - member, 0)
        )
        out_ref[target] = reach[place]


def prefix_body(at_ref, one, two, three_on, four, seven, tail_ref, six, out_ref):
    member = at_ref[MEMBER]
    row = lax.broadcasted_iota(jnp.int32, (OVL, OVL), 0)
    column = lax.broadcasted_iota(jnp.int32, (OVL, OVL), 1)
    out_ref[...] = jnp.where(row == column, 1.0, 0.0)

    @pl.when(member == 1)
    def _():
        out_ref[...] = seven[...]

    @pl.when(member == 2)
    def _():
        out_ref[...] = product_of(six[...], seven[...])

    @pl.when(member >= 3)
    def _():
        out_ref[...] = tail_ref[1]

    for least, ref in ((4, four), (5, three_on), (6, two), (7, one)):

        @pl.when(member >= least)
        def _(ref=ref):
            out_ref[...] = product_of(ref[...], out_ref[...])


def sum_body(at_ref, in_ref, out_ref):
    group = at_ref[MY_GROUP]
    low = in_ref[0]
    high = in_ref[GROUP]
    for m in range(1, GROUP):
        low = low + in_ref[m]
        high = high + in_ref[GROUP + m]
    entering = jnp.where(group == 0, 0.0, low)
    within = jnp.where(group == 0, low, high)
    for chip in range(CHIPS):
        out_ref[chip, 0] = entering
        out_ref[chip, 1] = within


def base_body(at_ref, own_ref, other_ref, columns_ref, *refs):
    blocks, (base_ref, window) = refs[:CHIPS], refs[CHIPS:]
    for i in range(CHIPS):
        start = pl.multiple_of(at_ref[PLACE + i] * ROWS, ROWS)
        window[pl.ds(start, ROWS), :] = blocks[i][...]
    half = product_of(columns_ref[...], window[...], TN)

    def run(left_ref, right_ref, core):
        base_ref[...] = product_of(half, right_ref[...])

    by_core(at_ref, own_ref, other_ref, run)


def final_body(
    at_ref, own_ref, other_ref, ends_ref, prefix_ref, prefix_other_ref, columns_ref, base_ref,
    kept_ref, sent_ref,
):
    entering = ends_ref[:, 0].reshape(OVL, OVL)
    within = ends_ref[:, 1].reshape(OVL, OVL)
    step = product_of(entering, prefix_ref[...] * 2.0**-48)
    carry = within + product_of(prefix_other_ref[...], step, TN) * 2.0**48

    def run(left_ref, right_ref, core):
        turned = (((0,), (1,)), ((), ())) if core == 0 else TN
        part = product_of(columns_ref[...], carry, turned)
        updated = base_ref[...] + product_of(part, right_ref[...])
        rows = ROWS // 2
        kept_ref[...] = updated[core * rows : (core + 1) * rows]
        sent_ref[...] = updated[(1 - core) * rows : (2 - core) * rows]

    by_core(at_ref, own_ref, other_ref, run)


EDGE_COLUMNS = pl.BlockSpec((W, OVL), lambda i: (0, EDGE // OVL))
TOP_ROWS = pl.BlockSpec((OVL, W), lambda i: (0, 0))


def shards(left, right, window_a, window_b, row_a, row_b, column_a, column_b, row_live, column_live):
    slab_index = lax.axis_index("slab")
    owner = lax.axis_index("diag")
    first_core = slab_index % 2 == 0
    chip = slab_index // 2
    x, y = chip // 4, chip % 4
    group, member = owner // GROUP, owner % GROUP

    def of_chip(for_first, for_second):
        got = swap_cores(jnp.where(first_core, for_second, for_first))
        return jnp.where(
            first_core,
            jnp.concatenate([for_first, got]),
            jnp.concatenate([got, for_second]),
        )

    def placed(blocks):
        full = jnp.zeros((CHIPS, ROWS, W), jnp.float32)
        for i, block in enumerate(blocks):
            place = (x ^ (i // 4)) * 4 + (y + i % 4) % 4
            full = lax.dynamic_update_slice(full, block[None], (place, 0, 0))
        return full.reshape(W, W)

    places = [(x ^ (i // 4)) * 4 + (y + i % 4) % 4 for i in range(CHIPS)]
    length = row_a.shape[1]
    begin = slab_index * length
    at = [slab_index % 2, row_live[0] - begin, column_live[0] - begin, group, member, chip]
    at = jnp.stack(at + places).astype(jnp.int32)

    together = lax.optimization_barrier
    own_factor = of_chip(left[0], right[0])
    own_window = of_chip(window_a[0], window_b[0])
    corner = corner_to_all(left, right)
    cross, below, above = (across(own_factor, route) for route in (CROSS, UP, DOWN))
    own_window, cross, below, above = together((own_window, cross, below, above))
    far, cross_above = across(above, DOWN), across(above, CROSS)
    cross_below = across(cross, UP)
    up_1, down_1 = from_member(corner, 1), from_member(corner, -1)
    own_window, far, cross_above, cross_below, up_1, down_1 = together(
        (own_window, far, cross_above, cross_below, up_1, down_1)
    )
    cross_far = across(far, CROSS)
    up_2, down_2 = from_member(up_1, 1), from_member(down_1, -1)
    w_below, w_above = across(own_window, UP), across(own_window, DOWN)
    cross_far, up_2, down_2, w_below, w_above = together(
        (cross_far, up_2, down_2, w_below, w_above)
    )
    up_3, down_3 = from_member(up_2, 1), from_member(down_2, -1)
    w_far, w_cross = across(w_above, DOWN), across(own_window, CROSS)
    factor = placed([own_factor, above, far, below, cross, cross_above, cross_far, cross_below])
    factor_other = swap_cores(factor)
    up_3, down_3, w_far, w_cross, factor, factor_other = together(
        (up_3, down_3, w_far, w_cross, factor, factor_other)
    )
    up_4 = from_member(up_3, 1)
    w_cross_above, w_cross_below = across(w_cross, DOWN), across(w_cross, UP)
    w_cross_far = across(w_far, CROSS)
    square = (OVL, OVL)
    early, tail, early_slices, tail_slices = local_kernel(
        early_chain_body,
        [(2, *square), (2, *square), (3, SLICE, OVL), (3, SLICE, OVL)],
        4 * OVL**3,
        [square],
        mib=52,
    )(at, up_1, up_2, up_3, down_3, down_2, down_1)
    blocks = [own_window, w_above, w_far, w_below, w_cross]
    part = corner_part((0, 1, 2, 3, 4), at, factor, factor_other, blocks)
    up_4, w_cross_above, w_cross_far, w_cross_below, early, tail, early_slices, tail_slices, part = together(
        (up_4, w_cross_above, w_cross_far, w_cross_below, early, tail, early_slices, tail_slices, part)
    )
    blocks += [w_cross_above, w_cross_far, w_cross_below]
    fourth, slices = local_kernel(
        late_chain_body, [square, (7, SLICE, OVL)], 2 * OVL**3, [square]
    )(at, early, early_slices, tail_slices, up_4)
    part, slices = together((part, slices))
    slices = swap_cores(slices)
    base_corner = corner_part((5, 6, 7), at, factor, factor_other, blocks, part)
    (outgoing,) = local_kernel(
        terms_body, [(16, SLICE, OVL)], 14 * SLICE * OVL * OVL, [(2 * GROUP, SLICE, OVL)]
    )(at, base_corner, slices, up_1, early, fourth, down_3, tail)
    outgoing, factor, factor_other, tail = together((outgoing, factor, factor_other, tail))
    incoming = lax.all_to_all(outgoing, "diag", split_axis=0, concat_axis=0, tiled=True)

    (prefix,) = local_kernel(prefix_body, [square], 4 * OVL**3, mib=52)(
        at, up_1, up_2, up_3, up_4, down_1, tail, down_2
    )
    prefix_other = swap_cores(prefix)
    own_columns = jnp.where(
        first_core,
        lax.dynamic_slice_in_dim(factor, chip * ROWS, ROWS, 1),
        lax.dynamic_slice_in_dim(factor_other, chip * ROWS, ROWS, 1),
    )
    (base,) = local_kernel(base_body, [(ROWS, W)], 2 * ROWS * W * W, [(W, W)], mib=32)(
        at, factor, factor_other, own_columns, *blocks
    )
    slabs = local_kernel(slab_body, [row_a.shape[1:]] * 4, 4 * length * W * W, mib=32)(
        at, factor, factor_other, row_a[0], row_b[0], column_a[0], column_b[0]
    )
    top_columns = own_columns[:OVL]
    incoming, base, prefix_other, top_columns, slabs = together(
        (incoming, base, prefix_other, top_columns, slabs)
    )
    (shares,) = local_kernel(sum_body, [(CHIPS, 2, SLICE, OVL)], 0)(at, incoming)
    ends = lax.all_to_all(
        shares, "slab", split_axis=0, concat_axis=0, tiled=True, axis_index_groups=SAME_CORE
    )
    kept, sent = local_kernel(
        final_body,
        [(ROWS // 2, W)] * 2,
        2 * OVL**3 + ROWS * OVL * (OVL + W),
        in_specs=[TOP_ROWS] * 2,
    )(at, factor, factor_other, ends, prefix, prefix_other, top_columns, base)
    received = swap_cores(sent)
    updated_a = jnp.where(first_core, kept, received)
    updated_b = jnp.where(first_core, received, kept)
    return (updated_a[None], updated_b[None], *(slab[None] for slab in slabs))


def solution(mesh):
    rows = P("diag", "slab", None)
    return jax.shard_map(
        shards,
        mesh=mesh,
        in_specs=(rows,) * 8 + (P("diag"),) * 2,
        out_specs=(rows,) * 6,
        check_vma=False,
    )
```

```python
import functools

import jax
import jax.numpy as jnp
from jax import lax
from jax.experimental import pallas as pl
from jax.experimental.pallas import tpu as pltpu
from jax.sharding import PartitionSpec as P

OVL = 256
W = 768
EDGE = W - OVL
ROWS = 96
CHIPS = 8
SLICE = OVL // CHIPS
GROUP = 8

NN = (((1,), (0,)), ((), ()))
TN = (((0,), (0,)), ((), ()))


def slab_route(move):
    return [
        ((x * 4 + y) * 2 + c, (move(x, y)[0] * 4 + move(x, y)[1]) * 2 + c)
        for x in range(2)
        for y in range(4)
        for c in range(2)
    ]


CROSS = slab_route(lambda x, y: (1 - x, y))
UP = slab_route(lambda x, y: (x, (y + 1) % 4))
DOWN = slab_route(lambda x, y: (x, (y + 3) % 4))
OTHER_CORE = [(i, i ^ 1) for i in range(16)]
SAME_CORE = [[i for i in range(16) if i % 2 == c] for c in range(2)]


def swap_cores(block):
    return lax.ppermute(block, "slab", OTHER_CORE)


def from_member(block, d):
    route = [(g * GROUP + (m + d) % GROUP, g * GROUP + m) for g in range(2) for m in range(GROUP)]
    return lax.ppermute(block, "diag", route)


def across(block, route):
    return lax.ppermute(block, "slab", route)


def pieces_body(left_ref, right_ref, out_ref):
    for chip in range(CHIPS):
        out_ref[2 * chip] = left_ref[0]
        out_ref[2 * chip + 1] = right_ref[0]


def corner_to_all(left, right):
    rows = left.shape[1]
    edge = pl.BlockSpec((1, rows, OVL), lambda i: (0, 0, EDGE // OVL))
    pieces = pl.pallas_call(
        pieces_body,
        grid=(1,),
        out_shape=jax.ShapeDtypeStruct((2 * CHIPS, rows, OVL), jnp.float32),
        in_specs=[edge, edge],
        out_specs=pl.BlockSpec((2 * CHIPS, rows, OVL), lambda i: (0, 0, 0)),
    )(left, right)
    pieces = lax.all_to_all(pieces, "slab", split_axis=0, concat_axis=0, tiled=True)
    count = -(-OVL // rows)
    return pieces[:count].reshape(count * rows, OVL)[:OVL]


def split(a):
    high = a.astype(jnp.bfloat16)
    return high, (a - high.astype(jnp.float32)).astype(jnp.bfloat16)


def three(a, b, dims=NN):
    def dot(p, q):
        return lax.dot_general(p, q, dims, preferred_element_type=jnp.float32)

    return dot(a[0], b[0]) + (dot(a[0], b[1]) + dot(a[1], b[0]))


CORE, ROW_LIVE, COLUMN_LIVE, MY_GROUP, MEMBER, CHIP, PLACE = range(7)
SCALARS = pl.BlockSpec(memory_space=pltpu.SMEM)
WHOLE = pl.BlockSpec(memory_space=pltpu.VMEM)


def block_of(shape):
    return pl.BlockSpec(shape, lambda i: (0,) * len(shape))


def local_kernel(body, shapes, flops, scratch=()):
    def call(at, *arrays):
        moved = sum(a.size for a in arrays) * 4
        return pl.pallas_call(
            body,
            grid=(1,),
            out_shape=[jax.ShapeDtypeStruct(shape, jnp.float32) for shape in shapes],
            in_specs=[SCALARS] + [WHOLE] * len(arrays),
            out_specs=[block_of(shape) for shape in shapes],
            scratch_shapes=[pltpu.VMEM(shape, jnp.float32) for shape in scratch],
            compiler_params=pltpu.CompilerParams(vmem_limit_bytes=16 * 2**20),
            cost_estimate=pl.CostEstimate(flops=6 * flops, bytes_accessed=moved, transcendentals=0),
        )(at, *arrays)

    return call


def product_of(a, b, dims=NN):
    return three(split(a), split(b), dims)


def chip_rows(at_ref):
    return pl.ds(pl.multiple_of(at_ref[CHIP] * SLICE, SLICE), SLICE)


def by_core(at_ref, own_ref, other_ref, run):
    for core in range(2):

        @pl.when(at_ref[CORE] == core)
        def _(core=core):
            run(*((own_ref, other_ref) if core == 0 else (other_ref, own_ref)), core)


def slab_body(at_ref, own_ref, other_ref, ra_ref, rb_ref, ca_ref, cb_ref, *outs):
    length = ra_ref.shape[0]

    def update(factor_ref, sources, targets, live):
        stacked = split(jnp.concatenate([source[...] for source in sources]))
        keep = lax.broadcasted_iota(jnp.int32, (length, OVL), 0) < live
        for t in range(W // OVL):
            columns = pl.ds(t * OVL, OVL)
            new = three(stacked, split(factor_ref[:, columns]))
            for i in range(2):
                targets[i][:, columns] = jnp.where(
                    keep, new[i * length : (i + 1) * length], sources[i][:, columns]
                )

    def run(left_ref, right_ref, core):
        update(left_ref, (ra_ref, rb_ref), outs[:2], at_ref[ROW_LIVE])
        update(right_ref, (ca_ref, cb_ref), outs[2:], at_ref[COLUMN_LIVE])

    by_core(at_ref, own_ref, other_ref, run)


def corner_body(positions, at_ref, own_ref, other_ref, *refs):
    blocks, (*before, out_ref, window, factor) = refs[: len(positions)], refs[len(positions) :]

    def run(left_ref, right_ref, core):
        for j, i in enumerate(positions):
            rows = pl.ds(j * ROWS, ROWS)
            start = pl.multiple_of(at_ref[PLACE + i] * ROWS, ROWS)
            window[rows, :] = blocks[j][...]
            factor[rows, :] = left_ref[pl.ds(start, ROWS), EDGE:]
        half = split(product_of(window[...], right_ref[:, EDGE:]))
        left = split(factor[...])
        part = three(half, left, TN) if core == 0 else three(left, half, TN)
        out_ref[...] = part + before[0][...] if before else part

    by_core(at_ref, own_ref, other_ref, run)


def corner_part(positions, at, factor, factor_other, blocks, *before):
    rows = len(positions) * ROWS
    return local_kernel(
        functools.partial(corner_body, positions),
        [(OVL, OVL)],
        rows * OVL * (W + OVL),
        [(rows, W), (rows, OVL)],
    )(at, factor, factor_other, *(blocks[i] for i in positions), *before)[0]


def slice_into(at_ref, product, out_ref, turned):
    turned[...] = product.T
    out_ref[...] = turned[chip_rows(at_ref), :]


def early_chain_body(
    at_ref, one, two, three_on, five, six, seven, chain_ref, tail_ref, slices_ref, tail_slices_ref, turned
):
    chain_ref[0] = product_of(one[...], two[...])
    chain_ref[1] = product_of(chain_ref[0], three_on[...])
    tail_ref[0] = product_of(five[...], six[...])
    tail_ref[1] = product_of(tail_ref[0], seven[...])
    for t in range(3):
        slice_into(at_ref, one[...] if t == 0 else chain_ref[t - 1], slices_ref.at[t], turned)
        slice_into(at_ref, five[...] if t == 0 else tail_ref[t - 1], tail_slices_ref.at[t], turned)


def late_chain_body(at_ref, early_ref, early_slices_ref, tail_slices_ref, four, chain_ref, slices_ref, turned):
    chain_ref[...] = product_of(early_ref[1], four[...])
    slices_ref[:3] = early_slices_ref[...]
    slice_into(at_ref, chain_ref[...], slices_ref.at[3], turned)
    tails = product_of(tail_slices_ref[...].reshape(3 * SLICE, OVL), turned[...])
    slices_ref[4:] = tails.reshape(3, SLICE, OVL)


def terms_body(at_ref, corner_ref, slices_ref, one_ref, early_ref, four_ref, five_ref, tail_ref, out_ref, reach):
    reach[:GROUP] = jnp.zeros((GROUP, SLICE, OVL), jnp.float32)
    reach[GROUP] = corner_ref[chip_rows(at_ref), :]
    near = product_of(slices_ref[...].reshape((GROUP - 1) * SLICE, OVL), corner_ref[...])
    for t in range(3):
        chain = one_ref[...] if t == 0 else early_ref[t - 1]
        reach[GROUP + 1 + t] = product_of(near[t * SLICE : (t + 1) * SLICE], chain)
    far = product_of(near[3 * SLICE :], four_ref[...])
    reach[GROUP + 4] = far[:SLICE]
    for t in range(3):
        tail = five_ref[...] if t == 0 else tail_ref[t - 1]
        reach[GROUP + 5 + t] = product_of(far[(t + 1) * SLICE : (t + 2) * SLICE], tail)
    group, member = at_ref[MY_GROUP], at_ref[MEMBER]
    for target in range(16):
        g, m = target // GROUP, target % GROUP
        place = jnp.where(
            group == g, GROUP + m - 1 - member, jnp.where(group < g, 2 * GROUP - 1 - member, 0)
        )
        out_ref[target] = reach[place]


def prefix_body(at_ref, one, two, three_on, four, seven, tail_ref, six, out_ref):
    member = at_ref[MEMBER]
    row = lax.broadcasted_iota(jnp.int32, (OVL, OVL), 0)
    column = lax.broadcasted_iota(jnp.int32, (OVL, OVL), 1)
    out_ref[...] = jnp.where(row == column, 1.0, 0.0)

    @pl.when(member == 1)
    def _():
        out_ref[...] = seven[...]

    @pl.when(member == 2)
    def _():
        out_ref[...] = product_of(six[...], seven[...])

    @pl.when(member >= 3)
    def _():
        out_ref[...] = tail_ref[1]

    for least, ref in ((4, four), (5, three_on), (6, two), (7, one)):

        @pl.when(member >= least)
        def _(ref=ref):
            out_ref[...] = product_of(ref[...], out_ref[...])


def sum_body(at_ref, in_ref, out_ref):
    group = at_ref[MY_GROUP]
    low = in_ref[0]
    high = in_ref[GROUP]
    for m in range(1, GROUP):
        low = low + in_ref[m]
        high = high + in_ref[GROUP + m]
    entering = jnp.where(group == 0, 0.0, low)
    within = jnp.where(group == 0, low, high)
    for chip in range(CHIPS):
        out_ref[chip, 0] = entering
        out_ref[chip, 1] = within


def base_body(at_ref, own_ref, other_ref, columns_ref, *refs):
    blocks, (base_ref, window) = refs[:CHIPS], refs[CHIPS:]
    for i in range(CHIPS):
        start = pl.multiple_of(at_ref[PLACE + i] * ROWS, ROWS)
        window[pl.ds(start, ROWS), :] = blocks[i][...]
    half = product_of(columns_ref[...], window[...], TN)

    def run(left_ref, right_ref, core):
        base_ref[...] = product_of(half, right_ref[...])

    by_core(at_ref, own_ref, other_ref, run)


def final_body(
    at_ref, own_ref, other_ref, ends_ref, prefix_ref, prefix_other_ref, columns_ref, base_ref,
    kept_ref, sent_ref,
):
    entering = ends_ref[:, 0].reshape(OVL, OVL)
    within = ends_ref[:, 1].reshape(OVL, OVL)
    step = product_of(entering, prefix_ref[...] * 2.0**-48)
    carry = within + product_of(prefix_other_ref[...], step, TN) * 2.0**48

    def run(left_ref, right_ref, core):
        turned = (((0,), (1,)), ((), ())) if core == 0 else TN
        part = product_of(columns_ref[...], carry, turned)
        updated = base_ref[...] + product_of(part, right_ref[:OVL, :])
        rows = ROWS // 2
        kept_ref[...] = updated[core * rows : (core + 1) * rows]
        sent_ref[...] = updated[(1 - core) * rows : (2 - core) * rows]

    by_core(at_ref, own_ref, other_ref, run)


def shards(left, right, window_a, window_b, row_a, row_b, column_a, column_b, row_live, column_live):
    slab_index = lax.axis_index("slab")
    owner = lax.axis_index("diag")
    first_core = slab_index % 2 == 0
    chip = slab_index // 2
    x, y = chip // 4, chip % 4
    group, member = owner // GROUP, owner % GROUP

    def of_chip(for_first, for_second):
        got = swap_cores(jnp.where(first_core, for_second, for_first))
        return jnp.where(
            first_core,
            jnp.concatenate([for_first, got]),
            jnp.concatenate([got, for_second]),
        )

    def placed(blocks):
        full = jnp.zeros((CHIPS, ROWS, W), jnp.float32)
        for i, block in enumerate(blocks):
            place = (x ^ (i // 4)) * 4 + (y + i % 4) % 4
            full = lax.dynamic_update_slice(full, block[None], (place, 0, 0))
        return full.reshape(W, W)

    places = [(x ^ (i // 4)) * 4 + (y + i % 4) % 4 for i in range(CHIPS)]
    length = row_a.shape[1]
    begin = slab_index * length
    at = [slab_index % 2, row_live[0] - begin, column_live[0] - begin, group, member, chip]
    at = jnp.stack(at + places).astype(jnp.int32)

    together = lax.optimization_barrier
    own_factor = of_chip(left[0], right[0])
    own_window = of_chip(window_a[0], window_b[0])
    corner = corner_to_all(left, right)
    cross, below, above = (across(own_factor, route) for route in (CROSS, UP, DOWN))
    own_window, cross, below, above = together((own_window, cross, below, above))
    far, cross_above = across(above, DOWN), across(above, CROSS)
    cross_below = across(cross, UP)
    up_1, down_1 = from_member(corner, 1), from_member(corner, -1)
    own_window, far, cross_above, cross_below, up_1, down_1 = together(
        (own_window, far, cross_above, cross_below, up_1, down_1)
    )
    cross_far = across(far, CROSS)
    up_2, down_2 = from_member(up_1, 1), from_member(down_1, -1)
    w_below, w_above = across(own_window, UP), across(own_window, DOWN)
    cross_far, up_2, down_2, w_below, w_above = together(
        (cross_far, up_2, down_2, w_below, w_above)
    )
    up_3, down_3 = from_member(up_2, 1), from_member(down_2, -1)
    w_far, w_cross = across(w_above, DOWN), across(own_window, CROSS)
    factor = placed([own_factor, above, far, below, cross, cross_above, cross_far, cross_below])
    factor_other = swap_cores(factor)
    up_3, down_3, w_far, w_cross, factor, factor_other = together(
        (up_3, down_3, w_far, w_cross, factor, factor_other)
    )
    up_4 = from_member(up_3, 1)
    w_cross_above, w_cross_below = across(w_cross, DOWN), across(w_cross, UP)
    w_cross_far = across(w_far, CROSS)
    square = (OVL, OVL)
    early, tail, early_slices, tail_slices = local_kernel(
        early_chain_body,
        [(2, *square), (2, *square), (3, SLICE, OVL), (3, SLICE, OVL)],
        4 * OVL**3,
        [square],
    )(at, up_1, up_2, up_3, down_3, down_2, down_1)
    blocks = [own_window, w_above, w_far, w_below, w_cross]
    part = corner_part((0, 1, 2, 3, 4), at, factor, factor_other, blocks)
    up_4, w_cross_above, w_cross_far, w_cross_below, early, tail, early_slices, tail_slices, part = together(
        (up_4, w_cross_above, w_cross_far, w_cross_below, early, tail, early_slices, tail_slices, part)
    )
    blocks += [w_cross_above, w_cross_far, w_cross_below]
    fourth, slices = local_kernel(
        late_chain_body, [square, (7, SLICE, OVL)], 2 * OVL**3, [square]
    )(at, early, early_slices, tail_slices, up_4)
    part, slices = together((part, slices))
    slices = swap_cores(slices)
    base_corner = corner_part((5, 6, 7), at, factor, factor_other, blocks, part)
    (outgoing,) = local_kernel(
        terms_body, [(16, SLICE, OVL)], 14 * SLICE * OVL * OVL, [(2 * GROUP, SLICE, OVL)]
    )(at, base_corner, slices, up_1, early, fourth, down_3, tail)
    outgoing, factor, factor_other, tail = together((outgoing, factor, factor_other, tail))
    incoming = lax.all_to_all(outgoing, "diag", split_axis=0, concat_axis=0, tiled=True)

    (prefix,) = local_kernel(prefix_body, [square], 4 * OVL**3)(
        at, up_1, up_2, up_3, up_4, down_1, tail, down_2
    )
    prefix_other = swap_cores(prefix)
    own_columns = jnp.where(
        first_core,
        lax.dynamic_slice_in_dim(factor, chip * ROWS, ROWS, 1),
        lax.dynamic_slice_in_dim(factor_other, chip * ROWS, ROWS, 1),
    )
    (base,) = local_kernel(base_body, [(ROWS, W)], 2 * ROWS * W * W, [(W, W)])(
        at, factor, factor_other, own_columns, *blocks
    )
    slabs = local_kernel(slab_body, [row_a.shape[1:]] * 4, 4 * length * W * W)(
        at, factor, factor_other, row_a[0], row_b[0], column_a[0], column_b[0]
    )
    top_columns = own_columns[:OVL]
    incoming, base, prefix_other, top_columns, slabs = together(
        (incoming, base, prefix_other, top_columns, slabs)
    )
    (shares,) = local_kernel(sum_body, [(CHIPS, 2, SLICE, OVL)], 0)(at, incoming)
    ends = lax.all_to_all(
        shares, "slab", split_axis=0, concat_axis=0, tiled=True, axis_index_groups=SAME_CORE
    )
    kept, sent = local_kernel(
        final_body,
        [(ROWS // 2, W)] * 2,
        2 * OVL**3 + ROWS * OVL * (OVL + W),
    )(at, factor, factor_other, ends, prefix, prefix_other, top_columns, base)
    received = swap_cores(sent)
    updated_a = jnp.where(first_core, kept, received)
    updated_b = jnp.where(first_core, received, kept)
    return (updated_a[None], updated_b[None], *(slab[None] for slab in slabs))


def solution(mesh):
    rows = P("diag", "slab", None)
    return jax.shard_map(
        shards,
        mesh=mesh,
        in_specs=(rows,) * 8 + (P("diag"),) * 2,
        out_specs=(rows,) * 6,
        check_vma=False,
    )
```

```python
import functools

import jax
import jax.numpy as jnp
from jax import lax
from jax.experimental import pallas as pl
from jax.experimental.pallas import tpu as pltpu
from jax.sharding import PartitionSpec as P

OVL = 256
W = 768
EDGE = W - OVL
ROWS = 96
CHIPS = 8
SLICE = OVL // CHIPS
GROUP = 8

NN = (((1,), (0,)), ((), ()))
TN = (((0,), (0,)), ((), ()))


def slab_route(move):
    return [
        ((x * 4 + y) * 2 + c, (move(x, y)[0] * 4 + move(x, y)[1]) * 2 + c)
        for x in range(2)
        for y in range(4)
        for c in range(2)
    ]


CROSS = slab_route(lambda x, y: (1 - x, y))
UP = slab_route(lambda x, y: (x, (y + 1) % 4))
DOWN = slab_route(lambda x, y: (x, (y + 3) % 4))
OTHER_CORE = [(i, i ^ 1) for i in range(16)]
SAME_CORE = [[i for i in range(16) if i % 2 == c] for c in range(2)]


def swap_cores(block):
    return lax.ppermute(block, "slab", OTHER_CORE)


def from_member(block, d):
    route = [(g * GROUP + (m + d) % GROUP, g * GROUP + m) for g in range(2) for m in range(GROUP)]
    return lax.ppermute(block, "diag", route)


def across(block, route):
    return lax.ppermute(block, "slab", route)


def pieces_body(left_ref, right_ref, out_ref):
    for chip in range(CHIPS):
        out_ref[2 * chip] = left_ref[0]
        out_ref[2 * chip + 1] = right_ref[0]


def corner_to_all(left, right):
    rows = left.shape[1]
    edge = pl.BlockSpec((1, rows, OVL), lambda i: (0, 0, EDGE // OVL))
    pieces = pl.pallas_call(
        pieces_body,
        grid=(1,),
        out_shape=jax.ShapeDtypeStruct((2 * CHIPS, rows, OVL), jnp.float32),
        in_specs=[edge, edge],
        out_specs=pl.BlockSpec((2 * CHIPS, rows, OVL), lambda i: (0, 0, 0)),
        compiler_params=pltpu.CompilerParams(vmem_limit_bytes=8 * 2**20),
    )(left, right)
    pieces = lax.all_to_all(pieces, "slab", split_axis=0, concat_axis=0, tiled=True)
    count = -(-OVL // rows)
    return pieces[:count].reshape(count * rows, OVL)[:OVL]


def split(a):
    high = a.astype(jnp.bfloat16)
    return high, (a - high.astype(jnp.float32)).astype(jnp.bfloat16)


def three(a, b, dims=NN):
    def dot(p, q):
        return lax.dot_general(p, q, dims, preferred_element_type=jnp.float32)

    return dot(a[0], b[0]) + (dot(a[0], b[1]) + dot(a[1], b[0]))


CORE, ROW_LIVE, COLUMN_LIVE, MY_GROUP, MEMBER, CHIP, PLACE = range(7)
SCALARS = pl.BlockSpec(memory_space=pltpu.SMEM)
WHOLE = pl.BlockSpec(memory_space=pltpu.VMEM)


def block_of(shape):
    return pl.BlockSpec(shape, lambda i: (0,) * len(shape))


def local_kernel(body, shapes, flops, scratch=()):
    def call(at, *arrays):
        moved = sum(a.size for a in arrays) * 4
        return pl.pallas_call(
            body,
            grid=(1,),
            out_shape=[jax.ShapeDtypeStruct(shape, jnp.float32) for shape in shapes],
            in_specs=[SCALARS] + [WHOLE] * len(arrays),
            out_specs=[block_of(shape) for shape in shapes],
            scratch_shapes=[pltpu.VMEM(shape, jnp.float32) for shape in scratch],
            compiler_params=pltpu.CompilerParams(vmem_limit_bytes=16 * 2**20),
            cost_estimate=pl.CostEstimate(flops=6 * flops, bytes_accessed=moved, transcendentals=0),
        )(at, *arrays)

    return call


def product_of(a, b, dims=NN):
    return three(split(a), split(b), dims)


def chip_rows(at_ref):
    return pl.ds(pl.multiple_of(at_ref[CHIP] * SLICE, SLICE), SLICE)


def by_core(at_ref, own_ref, other_ref, run):
    for core in range(2):

        @pl.when(at_ref[CORE] == core)
        def _(core=core):
            run(*((own_ref, other_ref) if core == 0 else (other_ref, own_ref)), core)


def slab_body(at_ref, own_ref, other_ref, ra_ref, rb_ref, ca_ref, cb_ref, *outs):
    length = ra_ref.shape[0]

    def update(factor_ref, sources, targets, live):
        stacked = split(jnp.concatenate([source[...] for source in sources]))
        keep = lax.broadcasted_iota(jnp.int32, (length, OVL), 0) < live
        for t in range(W // OVL):
            columns = pl.ds(t * OVL, OVL)
            new = three(stacked, split(factor_ref[:, columns]))
            for i in range(2):
                targets[i][:, columns] = jnp.where(
                    keep, new[i * length : (i + 1) * length], sources[i][:, columns]
                )

    def run(left_ref, right_ref, core):
        update(left_ref, (ra_ref, rb_ref), outs[:2], at_ref[ROW_LIVE])
        update(right_ref, (ca_ref, cb_ref), outs[2:], at_ref[COLUMN_LIVE])

    by_core(at_ref, own_ref, other_ref, run)


def corner_body(positions, at_ref, own_ref, other_ref, *refs):
    blocks, (*before, out_ref, window, factor) = refs[: len(positions)], refs[len(positions) :]

    def run(left_ref, right_ref, core):
        for j, i in enumerate(positions):
            rows = pl.ds(j * ROWS, ROWS)
            start = pl.multiple_of(at_ref[PLACE + i] * ROWS, ROWS)
            window[rows, :] = blocks[j][...]
            factor[rows, :] = left_ref[pl.ds(start, ROWS), EDGE:]
        half = split(product_of(window[...], right_ref[:, EDGE:]))
        left = split(factor[...])
        part = three(half, left, TN) if core == 0 else three(left, half, TN)
        out_ref[...] = part + before[0][...] if before else part

    by_core(at_ref, own_ref, other_ref, run)


def corner_part(positions, at, factor, factor_other, blocks, *before):
    rows = len(positions) * ROWS
    return local_kernel(
        functools.partial(corner_body, positions),
        [(OVL, OVL)],
        rows * OVL * (W + OVL),
        [(rows, W), (rows, OVL)],
    )(at, factor, factor_other, *(blocks[i] for i in positions), *before)[0]


def slice_into(at_ref, product, out_ref, turned):
    turned[...] = product.T
    out_ref[...] = turned[chip_rows(at_ref), :]


def early_chain_body(
    at_ref, one, two, three_on, five, six, seven, chain_ref, tail_ref, slices_ref, tail_slices_ref, turned
):
    chain_ref[0] = product_of(one[...], two[...])
    chain_ref[1] = product_of(chain_ref[0], three_on[...])
    tail_ref[0] = product_of(five[...], six[...])
    tail_ref[1] = product_of(tail_ref[0], seven[...])
    for t in range(3):
        slice_into(at_ref, one[...] if t == 0 else chain_ref[t - 1], slices_ref.at[t], turned)
        slice_into(at_ref, five[...] if t == 0 else tail_ref[t - 1], tail_slices_ref.at[t], turned)


def late_chain_body(at_ref, early_ref, early_slices_ref, tail_slices_ref, four, chain_ref, slices_ref, turned):
    chain_ref[...] = product_of(early_ref[1], four[...])
    slices_ref[:3] = early_slices_ref[...]
    slice_into(at_ref, chain_ref[...], slices_ref.at[3], turned)
    tails = product_of(tail_slices_ref[...].reshape(3 * SLICE, OVL), turned[...])
    slices_ref[4:] = tails.reshape(3, SLICE, OVL)


def terms_body(at_ref, corner_ref, slices_ref, one_ref, early_ref, four_ref, five_ref, tail_ref, out_ref, reach):
    reach[:GROUP] = jnp.zeros((GROUP, SLICE, OVL), jnp.float32)
    reach[GROUP] = corner_ref[chip_rows(at_ref), :]
    near = product_of(slices_ref[...].reshape((GROUP - 1) * SLICE, OVL), corner_ref[...])
    for t in range(3):
        chain = one_ref[...] if t == 0 else early_ref[t - 1]
        reach[GROUP + 1 + t] = product_of(near[t * SLICE : (t + 1) * SLICE], chain)
    far = product_of(near[3 * SLICE :], four_ref[...])
    reach[GROUP + 4] = far[:SLICE]
    for t in range(3):
        tail = five_ref[...] if t == 0 else tail_ref[t - 1]
        reach[GROUP + 5 + t] = product_of(far[(t + 1) * SLICE : (t + 2) * SLICE], tail)
    group, member = at_ref[MY_GROUP], at_ref[MEMBER]
    for target in range(16):
        g, m = target // GROUP, target % GROUP
        place = jnp.where(
            group == g, GROUP + m - 1 - member, jnp.where(group < g, 2 * GROUP - 1 - member, 0)
        )
        out_ref[target] = reach[place]


def prefix_body(at_ref, one, two, three_on, four, seven, tail_ref, six, out_ref):
    member = at_ref[MEMBER]
    row = lax.broadcasted_iota(jnp.int32, (OVL, OVL), 0)
    column = lax.broadcasted_iota(jnp.int32, (OVL, OVL), 1)
    out_ref[...] = jnp.where(row == column, 1.0, 0.0)

    @pl.when(member == 1)
    def _():
        out_ref[...] = seven[...]

    @pl.when(member == 2)
    def _():
        out_ref[...] = product_of(six[...], seven[...])

    @pl.when(member >= 3)
    def _():
        out_ref[...] = tail_ref[1]

    for least, ref in ((4, four), (5, three_on), (6, two), (7, one)):

        @pl.when(member >= least)
        def _(ref=ref):
            out_ref[...] = product_of(ref[...], out_ref[...])


def sum_body(at_ref, in_ref, out_ref):
    group = at_ref[MY_GROUP]
    low = in_ref[0]
    high = in_ref[GROUP]
    for m in range(1, GROUP):
        low = low + in_ref[m]
        high = high + in_ref[GROUP + m]
    entering = jnp.where(group == 0, 0.0, low)
    within = jnp.where(group == 0, low, high)
    for chip in range(CHIPS):
        out_ref[chip, 0] = entering
        out_ref[chip, 1] = within


def base_body(at_ref, own_ref, other_ref, columns_ref, *refs):
    blocks, (base_ref, window) = refs[:CHIPS], refs[CHIPS:]
    for i in range(CHIPS):
        start = pl.multiple_of(at_ref[PLACE + i] * ROWS, ROWS)
        window[pl.ds(start, ROWS), :] = blocks[i][...]
    half = product_of(columns_ref[...], window[...], TN)

    def run(left_ref, right_ref, core):
        base_ref[...] = product_of(half, right_ref[...])

    by_core(at_ref, own_ref, other_ref, run)


def final_body(
    at_ref, own_ref, other_ref, ends_ref, prefix_ref, prefix_other_ref, columns_ref, base_ref,
    kept_ref, sent_ref,
):
    entering = ends_ref[:, 0].reshape(OVL, OVL)
    within = ends_ref[:, 1].reshape(OVL, OVL)
    step = product_of(entering, prefix_ref[...] * 2.0**-48)
    carry = within + product_of(prefix_other_ref[...], step, TN) * 2.0**48

    def run(left_ref, right_ref, core):
        turned = (((0,), (1,)), ((), ())) if core == 0 else TN
        part = product_of(columns_ref[...], carry, turned)
        updated = base_ref[...] + product_of(part, right_ref[:OVL, :])
        rows = ROWS // 2
        kept_ref[...] = updated[core * rows : (core + 1) * rows]
        sent_ref[...] = updated[(1 - core) * rows : (2 - core) * rows]

    by_core(at_ref, own_ref, other_ref, run)


def shards(left, right, window_a, window_b, row_a, row_b, column_a, column_b, row_live, column_live):
    slab_index = lax.axis_index("slab")
    owner = lax.axis_index("diag")
    first_core = slab_index % 2 == 0
    chip = slab_index // 2
    x, y = chip // 4, chip % 4
    group, member = owner // GROUP, owner % GROUP

    def of_chip(for_first, for_second):
        got = swap_cores(jnp.where(first_core, for_second, for_first))
        return jnp.where(
            first_core,
            jnp.concatenate([for_first, got]),
            jnp.concatenate([got, for_second]),
        )

    def placed(blocks):
        full = jnp.zeros((CHIPS, ROWS, W), jnp.float32)
        for place, block in zip(places, blocks):
            full = lax.dynamic_update_slice(full, block[None], (place, zero, zero))
        return full.reshape(W, W)

    places = [(x ^ (i // 4)) * 4 + (y + i % 4) % 4 for i in range(CHIPS)]
    length = row_a.shape[1]
    begin = slab_index * length
    at = [slab_index % 2, row_live[0] - begin, column_live[0] - begin, group, member, chip]
    at = jnp.stack(at + places).astype(jnp.int32)
    places = [p.astype(jnp.uint32) for p in places]
    columns_at = (chip * ROWS).astype(jnp.uint32)
    zero = jnp.uint32(0)
    at, places, columns_at, left, right, window_a, window_b = lax.optimization_barrier(
        (at, places, columns_at, left, right, window_a, window_b)
    )

    together = lax.optimization_barrier
    own_factor = of_chip(left[0], right[0])
    own_window = of_chip(window_a[0], window_b[0])
    corner = corner_to_all(left, right)
    cross, below, above = (across(own_factor, route) for route in (CROSS, UP, DOWN))
    own_window, cross, below, above = together((own_window, cross, below, above))
    far, cross_above = across(above, DOWN), across(above, CROSS)
    cross_below = across(cross, UP)
    up_1, down_1 = from_member(corner, 1), from_member(corner, -1)
    own_window, far, cross_above, cross_below, up_1, down_1 = together(
        (own_window, far, cross_above, cross_below, up_1, down_1)
    )
    cross_far = across(far, CROSS)
    up_2, down_2 = from_member(up_1, 1), from_member(down_1, -1)
    w_below, w_above = across(own_window, UP), across(own_window, DOWN)
    cross_far, up_2, down_2, w_below, w_above = together(
        (cross_far, up_2, down_2, w_below, w_above)
    )
    up_3, down_3 = from_member(up_2, 1), from_member(down_2, -1)
    w_far, w_cross = across(w_above, DOWN), across(own_window, CROSS)
    factor = placed([own_factor, above, far, below, cross, cross_above, cross_far, cross_below])
    factor_other = swap_cores(factor)
    up_3, down_3, w_far, w_cross, factor, factor_other = together(
        (up_3, down_3, w_far, w_cross, factor, factor_other)
    )
    up_4 = from_member(up_3, 1)
    w_cross_above, w_cross_below = across(w_cross, DOWN), across(w_cross, UP)
    w_cross_far = across(w_far, CROSS)
    square = (OVL, OVL)
    early, tail, early_slices, tail_slices = local_kernel(
        early_chain_body,
        [(2, *square), (2, *square), (3, SLICE, OVL), (3, SLICE, OVL)],
        4 * OVL**3,
        [square],
    )(at, up_1, up_2, up_3, down_3, down_2, down_1)
    blocks = [own_window, w_above, w_far, w_below, w_cross]
    part = corner_part((0, 1, 2, 3, 4), at, factor, factor_other, blocks)
    up_4, w_cross_above, w_cross_far, w_cross_below, early, tail, early_slices, tail_slices, part = together(
        (up_4, w_cross_above, w_cross_far, w_cross_below, early, tail, early_slices, tail_slices, part)
    )
    blocks += [w_cross_above, w_cross_far, w_cross_below]
    fourth, slices = local_kernel(
        late_chain_body, [square, (7, SLICE, OVL)], 2 * OVL**3, [square]
    )(at, early, early_slices, tail_slices, up_4)
    part, slices = together((part, slices))
    slices = swap_cores(slices)
    base_corner = corner_part((5, 6, 7), at, factor, factor_other, blocks, part)
    (outgoing,) = local_kernel(
        terms_body, [(16, SLICE, OVL)], 14 * SLICE * OVL * OVL, [(2 * GROUP, SLICE, OVL)]
    )(at, base_corner, slices, up_1, early, fourth, down_3, tail)
    outgoing, factor, factor_other, tail = together((outgoing, factor, factor_other, tail))
    incoming = lax.all_to_all(outgoing, "diag", split_axis=0, concat_axis=0, tiled=True)

    (prefix,) = local_kernel(prefix_body, [square], 4 * OVL**3)(
        at, up_1, up_2, up_3, up_4, down_1, tail, down_2
    )
    prefix_other = swap_cores(prefix)
    own_columns = jnp.where(
        first_core,
        lax.dynamic_slice(factor, (zero, columns_at), (W, ROWS)),
        lax.dynamic_slice(factor_other, (zero, columns_at), (W, ROWS)),
    )
    (base,) = local_kernel(base_body, [(ROWS, W)], 2 * ROWS * W * W, [(W, W)])(
        at, factor, factor_other, own_columns, *blocks
    )
    slabs = local_kernel(slab_body, [row_a.shape[1:]] * 4, 4 * length * W * W)(
        at, factor, factor_other, row_a[0], row_b[0], column_a[0], column_b[0]
    )
    top_columns = own_columns[:OVL]
    incoming, base, prefix_other, top_columns, slabs = together(
        (incoming, base, prefix_other, top_columns, slabs)
    )
    (shares,) = local_kernel(sum_body, [(CHIPS, 2, SLICE, OVL)], 0)(at, incoming)
    ends = lax.all_to_all(
        shares, "slab", split_axis=0, concat_axis=0, tiled=True, axis_index_groups=SAME_CORE
    )
    kept, sent = local_kernel(
        final_body,
        [(ROWS // 2, W)] * 2,
        2 * OVL**3 + ROWS * OVL * (OVL + W),
    )(at, factor, factor_other, ends, prefix, prefix_other, top_columns, base)
    received = swap_cores(sent)
    updated_a = jnp.where(first_core, kept, received)
    updated_b = jnp.where(first_core, received, kept)
    return (updated_a[None], updated_b[None], *(slab[None] for slab in slabs))


def solution(mesh):
    rows = P("diag", "slab", None)
    return jax.shard_map(
        shards,
        mesh=mesh,
        in_specs=(rows,) * 8 + (P("diag"),) * 2,
        out_specs=(rows,) * 6,
        check_vma=False,
    )
```

```python
import functools

import jax
import jax.numpy as jnp
from jax import lax
from jax.experimental import pallas as pl
from jax.experimental.pallas import tpu as pltpu
from jax.sharding import PartitionSpec as P

OVL = 256
W = 768
EDGE = W - OVL
ROWS = 96
CHIPS = 8
SLICE = OVL // CHIPS
GROUP = 8

NN = (((1,), (0,)), ((), ()))
TN = (((0,), (0,)), ((), ()))


def slab_route(move):
    return [
        ((x * 4 + y) * 2 + c, (move(x, y)[0] * 4 + move(x, y)[1]) * 2 + c)
        for x in range(2)
        for y in range(4)
        for c in range(2)
    ]


CROSS = slab_route(lambda x, y: (1 - x, y))
UP = slab_route(lambda x, y: (x, (y + 1) % 4))
DOWN = slab_route(lambda x, y: (x, (y + 3) % 4))
OTHER_CORE = [(i, i ^ 1) for i in range(16)]
SAME_CORE = [[i for i in range(16) if i % 2 == c] for c in range(2)]


def swap_cores(block):
    return lax.ppermute(block, "slab", OTHER_CORE)


def from_member(block, d):
    route = [(g * GROUP + (m + d) % GROUP, g * GROUP + m) for g in range(2) for m in range(GROUP)]
    return lax.ppermute(block, "diag", route)


def across(block, route):
    return lax.ppermute(block, "slab", route)


def pieces_body(left_ref, right_ref, out_ref):
    for chip in range(CHIPS):
        out_ref[2 * chip] = left_ref[0]
        out_ref[2 * chip + 1] = right_ref[0]


def corner_to_all(left, right):
    rows = left.shape[1]
    edge = pl.BlockSpec((1, rows, OVL), lambda i: (0, 0, EDGE // OVL))
    pieces = pl.pallas_call(
        pieces_body,
        grid=(1,),
        out_shape=jax.ShapeDtypeStruct((2 * CHIPS, rows, OVL), jnp.float32),
        in_specs=[edge, edge],
        out_specs=pl.BlockSpec((2 * CHIPS, rows, OVL), lambda i: (0, 0, 0)),
        compiler_params=pltpu.CompilerParams(vmem_limit_bytes=8 * 2**20),
    )(left, right)
    pieces = lax.all_to_all(pieces, "slab", split_axis=0, concat_axis=0, tiled=True)
    count = -(-OVL // rows)
    return pieces[:count].reshape(count * rows, OVL)[:OVL]


def split(a):
    high = a.astype(jnp.bfloat16)
    return high, (a - high.astype(jnp.float32)).astype(jnp.bfloat16)


def three(a, b, dims=NN):
    def dot(p, q):
        return lax.dot_general(p, q, dims, preferred_element_type=jnp.float32)

    return dot(a[0], b[0]) + (dot(a[0], b[1]) + dot(a[1], b[0]))


CORE, ROW_LIVE, COLUMN_LIVE, MY_GROUP, MEMBER, CHIP, PLACE = range(7)
SCALARS = pl.BlockSpec(memory_space=pltpu.SMEM)
WHOLE = pl.BlockSpec(memory_space=pltpu.VMEM)


def block_of(shape):
    return pl.BlockSpec(shape, lambda i: (0,) * len(shape))


def local_kernel(body, shapes, flops, scratch=()):
    def call(at, *arrays):
        moved = sum(a.size for a in arrays) * 4
        return pl.pallas_call(
            body,
            grid=(1,),
            out_shape=[jax.ShapeDtypeStruct(shape, jnp.float32) for shape in shapes],
            in_specs=[SCALARS] + [WHOLE] * len(arrays),
            out_specs=[block_of(shape) for shape in shapes],
            scratch_shapes=[pltpu.VMEM(shape, jnp.float32) for shape in scratch],
            compiler_params=pltpu.CompilerParams(vmem_limit_bytes=16 * 2**20),
            cost_estimate=pl.CostEstimate(flops=6 * flops, bytes_accessed=moved, transcendentals=0),
        )(at, *arrays)

    return call


def product_of(a, b, dims=NN):
    return three(split(a), split(b), dims)


def chip_rows(at_ref):
    return pl.ds(pl.multiple_of(at_ref[CHIP] * SLICE, SLICE), SLICE)


def by_core(at_ref, own_ref, other_ref, run):
    for core in range(2):

        @pl.when(at_ref[CORE] == core)
        def _(core=core):
            run(*((own_ref, other_ref) if core == 0 else (other_ref, own_ref)), core)


def slab_body(at_ref, own_ref, other_ref, ra_ref, rb_ref, ca_ref, cb_ref, *outs):
    length = ra_ref.shape[0]

    def update(factor_ref, sources, targets, live):
        stacked = split(jnp.concatenate([source[...] for source in sources]))
        keep = lax.broadcasted_iota(jnp.int32, (length, OVL), 0) < live
        for t in range(W // OVL):
            columns = pl.ds(t * OVL, OVL)
            new = three(stacked, split(factor_ref[:, columns]))
            for i in range(2):
                targets[i][:, columns] = jnp.where(
                    keep, new[i * length : (i + 1) * length], sources[i][:, columns]
                )

    def run(left_ref, right_ref, core):
        update(left_ref, (ra_ref, rb_ref), outs[:2], at_ref[ROW_LIVE])
        update(right_ref, (ca_ref, cb_ref), outs[2:], at_ref[COLUMN_LIVE])

    by_core(at_ref, own_ref, other_ref, run)


def corner_body(positions, at_ref, own_ref, other_ref, *refs):
    blocks, (*before, out_ref, window, factor) = refs[: len(positions)], refs[len(positions) :]

    def run(left_ref, right_ref, core):
        for j, i in enumerate(positions):
            rows = pl.ds(j * ROWS, ROWS)
            start = pl.multiple_of(at_ref[PLACE + i] * ROWS, ROWS)
            window[rows, :] = blocks[j][...]
            factor[rows, :] = left_ref[pl.ds(start, ROWS), EDGE:]
        half = split(product_of(window[...], right_ref[:, EDGE:]))
        left = split(factor[...])
        part = three(half, left, TN) if core == 0 else three(left, half, TN)
        out_ref[...] = part + before[0][...] if before else part

    by_core(at_ref, own_ref, other_ref, run)


def corner_part(positions, at, factor, factor_other, blocks, *before):
    rows = len(positions) * ROWS
    return local_kernel(
        functools.partial(corner_body, positions),
        [(OVL, OVL)],
        rows * OVL * (W + OVL),
        [(rows, W), (rows, OVL)],
    )(at, factor, factor_other, *(blocks[i] for i in positions), *before)[0]


def slice_into(at_ref, product, out_ref, turned):
    turned[...] = product.T
    out_ref[...] = turned[chip_rows(at_ref), :]


def early_chain_body(
    at_ref, one, two, three_on, five, six, seven, chain_ref, tail_ref, slices_ref, tail_slices_ref, turned
):
    chain_ref[0] = product_of(one[...], two[...])
    chain_ref[1] = product_of(chain_ref[0], three_on[...])
    tail_ref[0] = product_of(five[...], six[...])
    tail_ref[1] = product_of(tail_ref[0], seven[...])
    for t in range(3):
        slice_into(at_ref, one[...] if t == 0 else chain_ref[t - 1], slices_ref.at[t], turned)
        slice_into(at_ref, five[...] if t == 0 else tail_ref[t - 1], tail_slices_ref.at[t], turned)


def late_chain_body(at_ref, early_ref, early_slices_ref, tail_slices_ref, four, chain_ref, slices_ref, turned):
    chain_ref[...] = product_of(early_ref[1], four[...])
    slices_ref[:3] = early_slices_ref[...]
    slice_into(at_ref, chain_ref[...], slices_ref.at[3], turned)
    tails = product_of(tail_slices_ref[...].reshape(3 * SLICE, OVL), turned[...])
    slices_ref[4:] = tails.reshape(3, SLICE, OVL)


def terms_body(at_ref, corner_ref, slices_ref, one_ref, early_ref, four_ref, five_ref, tail_ref, out_ref, reach):
    reach[:GROUP] = jnp.zeros((GROUP, SLICE, OVL), jnp.float32)
    reach[GROUP] = corner_ref[chip_rows(at_ref), :]
    near = product_of(slices_ref[...].reshape((GROUP - 1) * SLICE, OVL), corner_ref[...])
    for t in range(3):
        chain = one_ref[...] if t == 0 else early_ref[t - 1]
        reach[GROUP + 1 + t] = product_of(near[t * SLICE : (t + 1) * SLICE], chain)
    far = product_of(near[3 * SLICE :], four_ref[...])
    reach[GROUP + 4] = far[:SLICE]
    for t in range(3):
        tail = five_ref[...] if t == 0 else tail_ref[t - 1]
        reach[GROUP + 5 + t] = product_of(far[(t + 1) * SLICE : (t + 2) * SLICE], tail)
    group, member = at_ref[MY_GROUP], at_ref[MEMBER]
    for target in range(16):
        g, m = target // GROUP, target % GROUP
        place = jnp.where(
            group == g, GROUP + m - 1 - member, jnp.where(group < g, 2 * GROUP - 1 - member, 0)
        )
        out_ref[target] = reach[place]


def prefix_body(at_ref, one, two, three_on, four, seven, tail_ref, six, out_ref):
    member = at_ref[MEMBER]
    row = lax.broadcasted_iota(jnp.int32, (OVL, OVL), 0)
    column = lax.broadcasted_iota(jnp.int32, (OVL, OVL), 1)
    out_ref[...] = jnp.where(row == column, 1.0, 0.0)

    @pl.when(member == 1)
    def _():
        out_ref[...] = seven[...]

    @pl.when(member == 2)
    def _():
        out_ref[...] = product_of(six[...], seven[...])

    @pl.when(member >= 3)
    def _():
        out_ref[...] = tail_ref[1]

    for least, ref in ((4, four), (5, three_on), (6, two), (7, one)):

        @pl.when(member >= least)
        def _(ref=ref):
            out_ref[...] = product_of(ref[...], out_ref[...])


def sum_body(at_ref, in_ref, out_ref):
    group = at_ref[MY_GROUP]
    low = in_ref[0]
    high = in_ref[GROUP]
    for m in range(1, GROUP):
        low = low + in_ref[m]
        high = high + in_ref[GROUP + m]
    entering = jnp.where(group == 0, 0.0, low)
    within = jnp.where(group == 0, low, high)
    for chip in range(CHIPS):
        out_ref[chip, 0] = entering
        out_ref[chip, 1] = within


def base_body(at_ref, own_ref, other_ref, columns_ref, *refs):
    blocks, (base_ref, window) = refs[:CHIPS], refs[CHIPS:]
    for i in range(CHIPS):
        start = pl.multiple_of(at_ref[PLACE + i] * ROWS, ROWS)
        window[pl.ds(start, ROWS), :] = blocks[i][...]
    half = product_of(columns_ref[...], window[...], TN)

    def run(left_ref, right_ref, core):
        base_ref[...] = product_of(half, right_ref[...])

    by_core(at_ref, own_ref, other_ref, run)


def final_body(
    at_ref, own_ref, other_ref, ends_ref, prefix_ref, prefix_other_ref, columns_ref, base_ref,
    kept_ref, sent_ref,
):
    entering = ends_ref[:, 0].reshape(OVL, OVL)
    within = ends_ref[:, 1].reshape(OVL, OVL)
    step = product_of(entering, prefix_ref[...] * 2.0**-48)
    carry = within + product_of(prefix_other_ref[...], step, TN) * 2.0**48

    def run(left_ref, right_ref, core):
        turned = (((0,), (1,)), ((), ())) if core == 0 else TN
        part = product_of(columns_ref[...], carry, turned)
        updated = base_ref[...] + product_of(part, right_ref[:OVL, :])
        rows = ROWS // 2
        kept_ref[...] = updated[core * rows : (core + 1) * rows]
        sent_ref[...] = updated[(1 - core) * rows : (2 - core) * rows]

    by_core(at_ref, own_ref, other_ref, run)


def shards(left, right, window_a, window_b, row_a, row_b, column_a, column_b, row_live, column_live):
    slab_index = lax.axis_index("slab")
    owner = lax.axis_index("diag")
    first_core = (slab_index & 1) == 0
    chip = slab_index >> 1
    x, y = chip >> 2, chip & 3
    group, member = owner >> 3, owner & (GROUP - 1)

    def of_chip(for_first, for_second):
        got = swap_cores(jnp.where(first_core, for_second, for_first))
        return jnp.where(
            first_core,
            jnp.concatenate([for_first, got]),
            jnp.concatenate([got, for_second]),
        )

    def placed(blocks):
        full = jnp.zeros((CHIPS, ROWS, W), jnp.float32)
        for place, block in zip(places, blocks):
            full = lax.dynamic_update_slice(full, block[None], (place, zero, zero))
        return full.reshape(W, W)

    places = [((x ^ (i // 4)) << 2) + ((y + i % 4) & 3) for i in range(CHIPS)]
    length = row_a.shape[1]
    begin = slab_index * length
    at = [slab_index & 1, row_live[0] - begin, column_live[0] - begin, group, member, chip]
    at = jnp.stack(at + places).astype(jnp.int32)
    places = [p.astype(jnp.uint32) for p in places]
    columns_at = (chip * ROWS).astype(jnp.uint32)
    zero = jnp.uint32(0)
    at, places, columns_at, left, right, window_a, window_b = lax.optimization_barrier(
        (at, places, columns_at, left, right, window_a, window_b)
    )

    together = lax.optimization_barrier
    own_factor = of_chip(left[0], right[0])
    own_window = of_chip(window_a[0], window_b[0])
    corner = corner_to_all(left, right)
    cross, below, above = (across(own_factor, route) for route in (CROSS, UP, DOWN))
    own_window, cross, below, above = together((own_window, cross, below, above))
    far, cross_above = across(above, DOWN), across(above, CROSS)
    cross_below = across(cross, UP)
    up_1, down_1 = from_member(corner, 1), from_member(corner, -1)
    own_window, far, cross_above, cross_below, up_1, down_1 = together(
        (own_window, far, cross_above, cross_below, up_1, down_1)
    )
    cross_far = across(far, CROSS)
    up_2, down_2 = from_member(up_1, 1), from_member(down_1, -1)
    w_below, w_above = across(own_window, UP), across(own_window, DOWN)
    cross_far, up_2, down_2, w_below, w_above = together(
        (cross_far, up_2, down_2, w_below, w_above)
    )
    up_3, down_3 = from_member(up_2, 1), from_member(down_2, -1)
    w_far, w_cross = across(w_above, DOWN), across(own_window, CROSS)
    factor = placed([own_factor, above, far, below, cross, cross_above, cross_far, cross_below])
    factor_other = swap_cores(factor)
    up_3, down_3, w_far, w_cross, factor, factor_other = together(
        (up_3, down_3, w_far, w_cross, factor, factor_other)
    )
    up_4 = from_member(up_3, 1)
    w_cross_above, w_cross_below = across(w_cross, DOWN), across(w_cross, UP)
    w_cross_far = across(w_far, CROSS)
    square = (OVL, OVL)
    early, tail, early_slices, tail_slices = local_kernel(
        early_chain_body,
        [(2, *square), (2, *square), (3, SLICE, OVL), (3, SLICE, OVL)],
        4 * OVL**3,
        [square],
    )(at, up_1, up_2, up_3, down_3, down_2, down_1)
    blocks = [own_window, w_above, w_far, w_below, w_cross]
    part = corner_part((0, 1, 2, 3, 4), at, factor, factor_other, blocks)
    up_4, w_cross_above, w_cross_far, w_cross_below, early, tail, early_slices, tail_slices, part = together(
        (up_4, w_cross_above, w_cross_far, w_cross_below, early, tail, early_slices, tail_slices, part)
    )
    blocks += [w_cross_above, w_cross_far, w_cross_below]
    fourth, slices = local_kernel(
        late_chain_body, [square, (7, SLICE, OVL)], 2 * OVL**3, [square]
    )(at, early, early_slices, tail_slices, up_4)
    part, slices = together((part, slices))
    slices = swap_cores(slices)
    base_corner = corner_part((5, 6, 7), at, factor, factor_other, blocks, part)
    (outgoing,) = local_kernel(
        terms_body, [(16, SLICE, OVL)], 14 * SLICE * OVL * OVL, [(2 * GROUP, SLICE, OVL)]
    )(at, base_corner, slices, up_1, early, fourth, down_3, tail)
    outgoing, factor, factor_other, tail = together((outgoing, factor, factor_other, tail))
    incoming = lax.all_to_all(outgoing, "diag", split_axis=0, concat_axis=0, tiled=True)

    (prefix,) = local_kernel(prefix_body, [square], 4 * OVL**3)(
        at, up_1, up_2, up_3, up_4, down_1, tail, down_2
    )
    prefix_other = swap_cores(prefix)
    own_columns = jnp.where(
        first_core,
        lax.dynamic_slice(factor, (zero, columns_at), (W, ROWS)),
        lax.dynamic_slice(factor_other, (zero, columns_at), (W, ROWS)),
    )
    (base,) = local_kernel(base_body, [(ROWS, W)], 2 * ROWS * W * W, [(W, W)])(
        at, factor, factor_other, own_columns, *blocks
    )
    slabs = local_kernel(slab_body, [row_a.shape[1:]] * 4, 4 * length * W * W)(
        at, factor, factor_other, row_a[0], row_b[0], column_a[0], column_b[0]
    )
    top_columns = own_columns[:OVL]
    incoming, base, prefix_other, top_columns, slabs = together(
        (incoming, base, prefix_other, top_columns, slabs)
    )
    (shares,) = local_kernel(sum_body, [(CHIPS, 2, SLICE, OVL)], 0)(at, incoming)
    ends = lax.all_to_all(
        shares, "slab", split_axis=0, concat_axis=0, tiled=True, axis_index_groups=SAME_CORE
    )
    kept, sent = local_kernel(
        final_body,
        [(ROWS // 2, W)] * 2,
        2 * OVL**3 + ROWS * OVL * (OVL + W),
    )(at, factor, factor_other, ends, prefix, prefix_other, top_columns, base)
    received = swap_cores(sent)
    updated_a = jnp.where(first_core, kept, received)
    updated_b = jnp.where(first_core, received, kept)
    return (updated_a[None], updated_b[None], *(slab[None] for slab in slabs))


def solution(mesh):
    rows = P("diag", "slab", None)
    return jax.shard_map(
        shards,
        mesh=mesh,
        in_specs=(rows,) * 8 + (P("diag"),) * 2,
        out_specs=(rows,) * 6,
        check_vma=False,
    )
```

```python
import functools

import jax
import jax.numpy as jnp
from jax import lax
from jax.experimental import pallas as pl
from jax.experimental.pallas import tpu as pltpu
from jax.sharding import PartitionSpec as P

OVL = 256
W = 768
EDGE = W - OVL
ROWS = 96
CHIPS = 8
SLICE = OVL // CHIPS
GROUP = 8

NN = (((1,), (0,)), ((), ()))
TN = (((0,), (0,)), ((), ()))


def slab_route(move):
    return [
        ((x * 4 + y) * 2 + c, (move(x, y)[0] * 4 + move(x, y)[1]) * 2 + c)
        for x in range(2)
        for y in range(4)
        for c in range(2)
    ]


CROSS = slab_route(lambda x, y: (1 - x, y))
UP = slab_route(lambda x, y: (x, (y + 1) % 4))
DOWN = slab_route(lambda x, y: (x, (y + 3) % 4))
OTHER_CORE = [(i, i ^ 1) for i in range(16)]
SAME_CORE = [[i for i in range(16) if i % 2 == c] for c in range(2)]


def swap_cores(block):
    return lax.ppermute(block, "slab", OTHER_CORE)


def from_member(block, d):
    route = [(g * GROUP + (m + d) % GROUP, g * GROUP + m) for g in range(2) for m in range(GROUP)]
    return lax.ppermute(block, "diag", route)


def across(block, route):
    return lax.ppermute(block, "slab", route)


def pieces_body(left_ref, right_ref, out_ref):
    for chip in range(CHIPS):
        out_ref[2 * chip] = left_ref[0]
        out_ref[2 * chip + 1] = right_ref[0]


def corner_to_all(left, right):
    rows = left.shape[1]
    edge = pl.BlockSpec((1, rows, OVL), lambda i: (0, 0, EDGE // OVL))
    pieces = pl.pallas_call(
        pieces_body,
        grid=(1,),
        out_shape=jax.ShapeDtypeStruct((2 * CHIPS, rows, OVL), jnp.float32),
        in_specs=[edge, edge],
        out_specs=pl.BlockSpec((2 * CHIPS, rows, OVL), lambda i: (0, 0, 0)),
        compiler_params=pltpu.CompilerParams(vmem_limit_bytes=8 * 2**20),
    )(left, right)
    pieces = lax.all_to_all(pieces, "slab", split_axis=0, concat_axis=0, tiled=True)
    count = -(-OVL // rows)
    return pieces[:count].reshape(count * rows, OVL)[:OVL]


def split(a):
    high = a.astype(jnp.bfloat16)
    return high, (a - high.astype(jnp.float32)).astype(jnp.bfloat16)


def three(a, b, dims=NN):
    def dot(p, q):
        return lax.dot_general(p, q, dims, preferred_element_type=jnp.float32)

    return dot(a[0], b[0]) + (dot(a[0], b[1]) + dot(a[1], b[0]))


CORE, ROW_LIVE, COLUMN_LIVE, MY_GROUP, MEMBER, CHIP, PLACE = range(7)
SCALARS = pl.BlockSpec(memory_space=pltpu.SMEM)
WHOLE = pl.BlockSpec(memory_space=pltpu.VMEM)


def block_of(shape):
    return pl.BlockSpec(shape, lambda i: (0,) * len(shape))


def local_kernel(body, shapes, flops, scratch=()):
    def call(at, *arrays):
        moved = sum(a.size for a in arrays) * 4
        return pl.pallas_call(
            body,
            grid=(1,),
            out_shape=[jax.ShapeDtypeStruct(shape, jnp.float32) for shape in shapes],
            in_specs=[SCALARS] + [WHOLE] * len(arrays),
            out_specs=[block_of(shape) for shape in shapes],
            scratch_shapes=[pltpu.VMEM(shape, jnp.float32) for shape in scratch],
            compiler_params=pltpu.CompilerParams(vmem_limit_bytes=16 * 2**20),
            cost_estimate=pl.CostEstimate(flops=6 * flops, bytes_accessed=moved, transcendentals=0),
        )(at, *arrays)

    return call


def product_of(a, b, dims=NN):
    return three(split(a), split(b), dims)


def chip_rows(at_ref):
    return pl.ds(pl.multiple_of(at_ref[CHIP] * SLICE, SLICE), SLICE)


def by_core(at_ref, own_ref, other_ref, run):
    for core in range(2):

        @pl.when(at_ref[CORE] == core)
        def _(core=core):
            run(*((own_ref, other_ref) if core == 0 else (other_ref, own_ref)), core)


def slab_body(at_ref, own_ref, other_ref, ra_ref, rb_ref, ca_ref, cb_ref, *outs):
    length = ra_ref.shape[0]

    def update(factor_ref, sources, targets, live):
        stacked = split(jnp.concatenate([source[...] for source in sources]))
        keep = lax.broadcasted_iota(jnp.int32, (length, OVL), 0) < live
        for t in range(W // OVL):
            columns = pl.ds(t * OVL, OVL)
            new = three(stacked, split(factor_ref[:, columns]))
            for i in range(2):
                targets[i][:, columns] = jnp.where(
                    keep, new[i * length : (i + 1) * length], sources[i][:, columns]
                )

    def run(left_ref, right_ref, core):
        update(left_ref, (ra_ref, rb_ref), outs[:2], at_ref[ROW_LIVE])
        update(right_ref, (ca_ref, cb_ref), outs[2:], at_ref[COLUMN_LIVE])

    by_core(at_ref, own_ref, other_ref, run)


def corner_body(positions, at_ref, own_ref, other_ref, *refs):
    blocks, (*before, out_ref, window, factor) = refs[: len(positions)], refs[len(positions) :]

    def run(left_ref, right_ref, core):
        for j, i in enumerate(positions):
            rows = pl.ds(j * ROWS, ROWS)
            start = pl.multiple_of(at_ref[PLACE + i] * ROWS, ROWS)
            window[rows, :] = blocks[j][...]
            factor[rows, :] = left_ref[pl.ds(start, ROWS), EDGE:]
        half = split(product_of(window[...], right_ref[:, EDGE:]))
        left = split(factor[...])
        part = three(half, left, TN) if core == 0 else three(left, half, TN)
        out_ref[...] = part + before[0][...] if before else part

    by_core(at_ref, own_ref, other_ref, run)


def corner_part(positions, at, factor, factor_other, blocks, *before):
    rows = len(positions) * ROWS
    return local_kernel(
        functools.partial(corner_body, positions),
        [(OVL, OVL)],
        rows * OVL * (W + OVL),
        [(rows, W), (rows, OVL)],
    )(at, factor, factor_other, *(blocks[i] for i in positions), *before)[0]


def slice_into(at_ref, product, out_ref, turned):
    turned[...] = product.T
    out_ref[...] = turned[chip_rows(at_ref), :]


def early_chain_body(
    at_ref, one, two, three_on, five, six, seven, chain_ref, tail_ref, slices_ref, tail_slices_ref, turned
):
    chain_ref[0] = product_of(one[...], two[...])
    chain_ref[1] = product_of(chain_ref[0], three_on[...])
    tail_ref[0] = product_of(five[...], six[...])
    tail_ref[1] = product_of(tail_ref[0], seven[...])
    for t in range(3):
        slice_into(at_ref, one[...] if t == 0 else chain_ref[t - 1], slices_ref.at[t], turned)
        slice_into(at_ref, five[...] if t == 0 else tail_ref[t - 1], tail_slices_ref.at[t], turned)


def late_chain_body(at_ref, early_ref, early_slices_ref, tail_slices_ref, four, chain_ref, slices_ref, turned):
    chain_ref[...] = product_of(early_ref[1], four[...])
    slices_ref[:3] = early_slices_ref[...]
    slice_into(at_ref, chain_ref[...], slices_ref.at[3], turned)
    tails = product_of(tail_slices_ref[...].reshape(3 * SLICE, OVL), turned[...])
    slices_ref[4:] = tails.reshape(3, SLICE, OVL)


def terms_body(at_ref, corner_ref, slices_ref, one_ref, early_ref, four_ref, five_ref, tail_ref, out_ref, reach):
    reach[:GROUP] = jnp.zeros((GROUP, SLICE, OVL), jnp.float32)
    reach[GROUP] = corner_ref[chip_rows(at_ref), :]
    near = product_of(slices_ref[...].reshape((GROUP - 1) * SLICE, OVL), corner_ref[...])
    for t in range(3):
        chain = one_ref[...] if t == 0 else early_ref[t - 1]
        reach[GROUP + 1 + t] = product_of(near[t * SLICE : (t + 1) * SLICE], chain)
    far = product_of(near[3 * SLICE :], four_ref[...])
    reach[GROUP + 4] = far[:SLICE]
    for t in range(3):
        tail = five_ref[...] if t == 0 else tail_ref[t - 1]
        reach[GROUP + 5 + t] = product_of(far[(t + 1) * SLICE : (t + 2) * SLICE], tail)
    group, member = at_ref[MY_GROUP], at_ref[MEMBER]
    for target in range(16):
        g, m = target // GROUP, target % GROUP
        place = jnp.where(
            group == g, GROUP + m - 1 - member, jnp.where(group < g, 2 * GROUP - 1 - member, 0)
        )
        out_ref[target] = reach[place]


def prefix_body(at_ref, one, two, three_on, four, seven, tail_ref, six, out_ref):
    member = at_ref[MEMBER]
    row = lax.broadcasted_iota(jnp.int32, (OVL, OVL), 0)
    column = lax.broadcasted_iota(jnp.int32, (OVL, OVL), 1)
    out_ref[...] = jnp.where(row == column, 1.0, 0.0)

    @pl.when(member == 1)
    def _():
        out_ref[...] = seven[...]

    @pl.when(member == 2)
    def _():
        out_ref[...] = product_of(six[...], seven[...])

    @pl.when(member >= 3)
    def _():
        out_ref[...] = tail_ref[1]

    for least, ref in ((4, four), (5, three_on), (6, two), (7, one)):

        @pl.when(member >= least)
        def _(ref=ref):
            out_ref[...] = product_of(ref[...], out_ref[...])


def sum_body(at_ref, in_ref, out_ref):
    group = at_ref[MY_GROUP]
    low = in_ref[0]
    high = in_ref[GROUP]
    for m in range(1, GROUP):
        low = low + in_ref[m]
        high = high + in_ref[GROUP + m]
    entering = jnp.where(group == 0, 0.0, low)
    within = jnp.where(group == 0, low, high)
    for chip in range(CHIPS):
        out_ref[chip, 0] = entering
        out_ref[chip, 1] = within


def base_body(at_ref, own_ref, other_ref, columns_ref, *refs):
    blocks, (base_ref, window) = refs[:CHIPS], refs[CHIPS:]
    for i in range(CHIPS):
        start = pl.multiple_of(at_ref[PLACE + i] * ROWS, ROWS)
        window[pl.ds(start, ROWS), :] = blocks[i][...]
    half = product_of(columns_ref[...], window[...], TN)

    def run(left_ref, right_ref, core):
        base_ref[...] = product_of(half, right_ref[...])

    by_core(at_ref, own_ref, other_ref, run)


def final_body(
    at_ref, top_ref, ends_ref, prefix_ref, prefix_other_ref, columns_ref, base_ref,
    kept_ref, sent_ref,
):
    entering = ends_ref[:, 0].reshape(OVL, OVL)
    within = ends_ref[:, 1].reshape(OVL, OVL)
    step = product_of(entering, prefix_ref[...] * 2.0**-48)
    carry = within + product_of(prefix_other_ref[...], step, TN) * 2.0**48

    for core in range(2):

        @pl.when(at_ref[CORE] == core)
        def _(core=core):
            turned = (((0,), (1,)), ((), ())) if core == 0 else TN
            part = product_of(columns_ref[...], carry, turned)
            updated = base_ref[...] + product_of(part, top_ref[...])
            rows = ROWS // 2
            kept_ref[...] = updated[core * rows : (core + 1) * rows]
            sent_ref[...] = updated[(1 - core) * rows : (2 - core) * rows]


def shards(left, right, window_a, window_b, row_a, row_b, column_a, column_b, row_live, column_live):
    slab_index = lax.axis_index("slab")
    owner = lax.axis_index("diag")
    first_core = (slab_index & 1) == 0
    chip = slab_index >> 1
    x, y = chip >> 2, chip & 3
    group, member = owner >> 3, owner & (GROUP - 1)

    def of_chip(for_first, for_second):
        got = swap_cores(jnp.where(first_core, for_second, for_first))
        return jnp.where(
            first_core,
            jnp.concatenate([for_first, got]),
            jnp.concatenate([got, for_second]),
        )

    def placed(blocks):
        full = jnp.zeros((CHIPS, ROWS, W), jnp.float32)
        for place, block in zip(places, blocks):
            full = lax.dynamic_update_slice(full, block[None], (place, zero, zero))
        return full.reshape(W, W)

    places = [((x ^ (i // 4)) << 2) + ((y + i % 4) & 3) for i in range(CHIPS)]
    length = row_a.shape[1]
    begin = slab_index * length
    at = [slab_index & 1, row_live[0] - begin, column_live[0] - begin, group, member, chip]
    at = jnp.stack(at + places).astype(jnp.int32)
    places = [p.astype(jnp.uint32) for p in places]
    columns_at = (chip * ROWS).astype(jnp.uint32)
    zero = jnp.uint32(0)
    at, places, columns_at, left, right, window_a, window_b = lax.optimization_barrier(
        (at, places, columns_at, left, right, window_a, window_b)
    )

    together = lax.optimization_barrier
    own_factor = of_chip(left[0], right[0])
    own_window = of_chip(window_a[0], window_b[0])
    corner = corner_to_all(left, right)
    cross, below, above = (across(own_factor, route) for route in (CROSS, UP, DOWN))
    own_window, cross, below, above = together((own_window, cross, below, above))
    far, cross_above = across(above, DOWN), across(above, CROSS)
    cross_below = across(cross, UP)
    up_1, down_1 = from_member(corner, 1), from_member(corner, -1)
    own_window, far, cross_above, cross_below, up_1, down_1 = together(
        (own_window, far, cross_above, cross_below, up_1, down_1)
    )
    cross_far = across(far, CROSS)
    up_2, down_2 = from_member(up_1, 1), from_member(down_1, -1)
    w_below, w_above = across(own_window, UP), across(own_window, DOWN)
    cross_far, up_2, down_2, w_below, w_above = together(
        (cross_far, up_2, down_2, w_below, w_above)
    )
    up_3, down_3 = from_member(up_2, 1), from_member(down_2, -1)
    w_far, w_cross = across(w_above, DOWN), across(own_window, CROSS)
    factor = placed([own_factor, above, far, below, cross, cross_above, cross_far, cross_below])
    factor_other = swap_cores(factor)
    up_3, down_3, w_far, w_cross, factor, factor_other = together(
        (up_3, down_3, w_far, w_cross, factor, factor_other)
    )
    up_4 = from_member(up_3, 1)
    w_cross_above, w_cross_below = across(w_cross, DOWN), across(w_cross, UP)
    w_cross_far = across(w_far, CROSS)
    square = (OVL, OVL)
    early, tail, early_slices, tail_slices = local_kernel(
        early_chain_body,
        [(2, *square), (2, *square), (3, SLICE, OVL), (3, SLICE, OVL)],
        4 * OVL**3,
        [square],
    )(at, up_1, up_2, up_3, down_3, down_2, down_1)
    blocks = [own_window, w_above, w_far, w_below, w_cross]
    part = corner_part((0, 1, 2, 3, 4), at, factor, factor_other, blocks)
    up_4, w_cross_above, w_cross_far, w_cross_below, early, tail, early_slices, tail_slices, part = together(
        (up_4, w_cross_above, w_cross_far, w_cross_below, early, tail, early_slices, tail_slices, part)
    )
    blocks += [w_cross_above, w_cross_far, w_cross_below]
    fourth, slices = local_kernel(
        late_chain_body, [square, (7, SLICE, OVL)], 2 * OVL**3, [square]
    )(at, early, early_slices, tail_slices, up_4)
    part, slices = together((part, slices))
    slices = swap_cores(slices)
    base_corner = corner_part((5, 6, 7), at, factor, factor_other, blocks, part)
    (outgoing,) = local_kernel(
        terms_body, [(16, SLICE, OVL)], 14 * SLICE * OVL * OVL, [(2 * GROUP, SLICE, OVL)]
    )(at, base_corner, slices, up_1, early, fourth, down_3, tail)
    outgoing, factor, factor_other, tail = together((outgoing, factor, factor_other, tail))
    incoming = lax.all_to_all(outgoing, "diag", split_axis=0, concat_axis=0, tiled=True)

    (prefix,) = local_kernel(prefix_body, [square], 4 * OVL**3)(
        at, up_1, up_2, up_3, up_4, down_1, tail, down_2
    )
    prefix_other = swap_cores(prefix)
    own_columns = jnp.where(
        first_core,
        lax.dynamic_slice(factor, (zero, columns_at), (W, ROWS)),
        lax.dynamic_slice(factor_other, (zero, columns_at), (W, ROWS)),
    )
    (base,) = local_kernel(base_body, [(ROWS, W)], 2 * ROWS * W * W, [(W, W)])(
        at, factor, factor_other, own_columns, *blocks
    )
    slabs = local_kernel(slab_body, [row_a.shape[1:]] * 4, 4 * length * W * W)(
        at, factor, factor_other, row_a[0], row_b[0], column_a[0], column_b[0]
    )
    top_columns = own_columns[:OVL]
    right_top = jnp.where(first_core, factor_other[:OVL], factor[:OVL])
    incoming, base, prefix_other, top_columns, right_top, slabs = together(
        (incoming, base, prefix_other, top_columns, right_top, slabs)
    )
    (shares,) = local_kernel(sum_body, [(CHIPS, 2, SLICE, OVL)], 0)(at, incoming)
    ends = lax.all_to_all(
        shares, "slab", split_axis=0, concat_axis=0, tiled=True, axis_index_groups=SAME_CORE
    )
    kept, sent = local_kernel(
        final_body,
        [(ROWS // 2, W)] * 2,
        2 * OVL**3 + ROWS * OVL * (OVL + W),
    )(at, right_top, ends, prefix, prefix_other, top_columns, base)
    received = swap_cores(sent)
    updated_a = jnp.where(first_core, kept, received)
    updated_b = jnp.where(first_core, received, kept)
    return (updated_a[None], updated_b[None], *(slab[None] for slab in slabs))


def solution(mesh):
    rows = P("diag", "slab", None)
    return jax.shard_map(
        shards,
        mesh=mesh,
        in_specs=(rows,) * 8 + (P("diag"),) * 2,
        out_specs=(rows,) * 6,
        check_vma=False,
    )
```
